32 devices in a mesh: dp: 2 (over x), ctx: 16 (over z, y, core).
Axes of the slice: x: 2, y: 2, z: 4, core: 2. Of those that a mesh axis runs over, the one named last changes fastest.
Arguments:
- tokens: bfloat16 [2, 2048, 1024], P('dp', 'ctx'), may hold values from -6 to 6
- segments: int32 [2, 2048], P('dp', 'ctx'), may hold values from 0 to 2, as said below
- cotangent: bfloat16 [2, 2048, 1024], P('dp', 'ctx'), may hold values from -6 to 6
- conv_weights: bfloat16 [1024, 17920], P('ctx'), may hold values from -0.1875 to 0.1875
- attn_weights: bfloat16 [1024, 16896], P('ctx')
- vectors: float32 [7, 1024], replicated, may hold values from 0.5 to 1.5
- head_gains: float32 [2, 64], replicated, may hold values from 0.5 to 1.5
- master_conv: float32 [1024, 17920], P('ctx', 'dp'), may hold values from -0.1875 to 0.1875
- first_conv: float32 [1024, 17920], P('ctx', 'dp'), may hold values from -6 to 6
- second_conv: float32 [1024, 17920], P('ctx', 'dp'), may hold values from 0.1 to 100
- master_attn: float32 [1024, 16896], P('ctx', 'dp'), may hold values from -0.1875 to 0.1875
- first_attn: float32 [1024, 16896], P('ctx', 'dp'), may hold values from -6 to 6
- second_attn: float32 [1024, 16896], P('ctx', 'dp'), may hold values from 0.1 to 100
Outputs:
- out_tokens: bfloat16 [2, 2048, 1024], P('dp', 'ctx')
- grad_tokens: float32 [2, 2048, 1024], P('dp', 'ctx')
- grad_conv: float32 [1024, 17920], P('ctx', 'dp')
- grad_attn: float32 [1024, 16896], P('ctx', 'dp')
- grad_vectors: float32 [7, 1024], replicated
- grad_gains: float32 [2, 64], replicated
- new_master_conv: float32 [1024, 17920], P('ctx', 'dp')
- new_first_conv: float32 [1024, 17920], P('ctx', 'dp')
- new_second_conv: float32 [1024, 17920], P('ctx', 'dp')
- new_master_attn: float32 [1024, 16896], P('ctx', 'dp')
- new_first_attn: float32 [1024, 16896], P('ctx', 'dp')
- new_second_attn: float32 [1024, 16896], P('ctx', 'dp')
- new_conv_weights: bfloat16 [1024, 17920], P('ctx')
- new_attn_weights: bfloat16 [1024, 16896], P('ctx')
The draws below stay inside these ranges and needn't reach their ends.
Inputs may be any that keep to these rules, and one draw needn't show every extreme that they name: `segments`: within each sequence the segment ids start at 0 and never fall, each of the 3 ids is used; document 1 begins within the first 128 positions and ends within the last 128 positions.
All inputs are finite; a program needn't handle non-finite values.
Results may differ from the reference program's by a relative error of at most 0.025.
Values may be sent and summed in bfloat16 or wider, within the bound.
A program may use at most 640 MiB of HBM per device.

```python
import math
import jax
import jax.numpy as jnp
from jax import lax

D = 1024
FF = 4608
HEADS = 16
KV_HEADS = 8
HEAD_DIM = 64
STEP = 5
TOK_DEV = 128
SEQ = 2048
SEQS = 2
KVW = 512
C1 = 17920
C2 = 16896


def draw_attn_weights(key, part):
    values = jax.random.normal(key, (D, C2), jnp.float32) * D ** (-0.5)
    columns = jnp.arange(C2)
    boost = jnp.where((columns >= D + 2 * KVW) & (columns < 2 * D + 2 * KVW), 4.0, 1.0)
    return (values * boost).astype(jnp.bfloat16)


def draw_segments(key, part):
    first_key = jax.random.fold_in(key, 11)
    last_key = jax.random.fold_in(key, 23)
    begin = jax.random.randint(first_key, (SEQS, 1), 1, TOK_DEV)
    finish = jax.random.randint(last_key, (SEQS, 1), SEQ - TOK_DEV + 1, SEQ)
    places = jnp.arange(SEQ, dtype=jnp.int32)[None, :]
    return ((places >= begin).astype(jnp.int32) + (places >= finish).astype(jnp.int32)).astype(jnp.int32)


def block_scale(key, dims, split, low, high):
    factor_of, own = 1.0, jax.random.fold_in(key, 6)
    for position, shards_of in split:
        steps = jnp.exp(jax.random.uniform(jax.random.fold_in(own, position), (shards_of,), jnp.float32, low / len(split), high / len(split)))
        factor_of = factor_of * jnp.repeat(steps, dims[position] // shards_of).reshape([-1 if axis == position else 1 for axis in range(len(dims))])
    return factor_of


def gaussian(stream_key, shape, deviation, most, shards=(), kind=jnp.bfloat16):
    drawn = deviation * jax.random.normal(stream_key, shape, jnp.float32)
    if shards:
        drawn = drawn * block_scale(stream_key, shape, shards, -0.22, 0.18)
    return jnp.clip(drawn, -most, most).astype(kind)


def setup_inputs(seed: int = 0) -> dict:
    splits = jax.random.split(jax.random.key(seed), 14)
    return {
        "tokens": gaussian(splits[0], (SEQS, SEQ, D), 1.0, 6.0, ((0, 2), (1, 16))),
        "segments": draw_segments(jax.random.fold_in(splits[13], 71), 0),
        "cotangent": gaussian(splits[2], (SEQS, SEQ, D), 1.0, 6.0, ((0, 2), (1, 16))),
        "conv_weights": gaussian(splits[3], (D, C1), D ** -0.5, 0.1875, ((0, 16),)),
        "attn_weights": draw_attn_weights(jax.random.fold_in(splits[13], 71), 0),
        "vectors": jnp.clip(1.0 + 0.1 * jax.random.normal(splits[5], (7, D), jnp.float32), 0.5, 1.5),
        "head_gains": jnp.clip(1.0 + 0.1 * jax.random.normal(splits[6], (2, HEAD_DIM), jnp.float32), 0.5, 1.5),
        "master_conv": gaussian(splits[7], (D, C1), D ** -0.5, 0.1875, ((0, 16), (1, 2)), jnp.float32),
        "first_conv": gaussian(splits[8], (D, C1), 1.0, 6.0, ((0, 16), (1, 2)), jnp.float32),
        "second_conv": jnp.clip(jnp.exp(math.log(100.0) - 6.9077553 * jax.random.uniform(splits[9], (D, C1), jnp.float32) ** block_scale(splits[9], (D, C1), ((0, 16), (1, 2)), -0.2, 0.2)), 0.1, 100.0),
        "master_attn": gaussian(splits[10], (D, C2), D ** -0.5, 0.1875, ((0, 16), (1, 2)), jnp.float32),
        "first_attn": gaussian(splits[11], (D, C2), 1.0, 6.0, ((0, 16), (1, 2)), jnp.float32),
        "second_attn": jnp.clip(jnp.exp(math.log(100.0) - 6.9077553 * jax.random.uniform(splits[12], (D, C2), jnp.float32) ** block_scale(splits[12], (D, C2), ((0, 16), (1, 2)), -0.2, 0.2)), 0.1, 100.0),
    }


norm_eps = 1e-05
rope_base = 1000000.0
learn_rate = 0.01
decay_rate = 0.1
beta_one = 0.9
beta_two = 0.95
adam_eps = 1e-08
masked_score = -1e+30
highest = lax.Precision.HIGHEST

@jax.custom_vjp
def low(v):
    return lax.optimization_barrier(v.astype(jnp.bfloat16)).astype(jnp.float32)

@jax.custom_vjp
def low_back(v):
    return v

def low_keep(v):
    return (low(v), None)

def low_pass(kept, grad):
    return (grad,)

def back_keep(v):
    return (v, None)

def back_low(kept, grad):
    return (low(grad),)
low.defvjp(low_keep, low_pass)
low_back.defvjp(back_keep, back_low)

def rms_apply(value, gain):
    return value * lax.rsqrt(lax.optimization_barrier(jnp.mean(value * value, axis=-1, keepdims=True)) + norm_eps) * gain

def rotate(value, cosines, sines):
    half_width = value.shape[-1] // 2
    turned = jnp.concatenate([-value[..., half_width:], value[..., :half_width]], axis=-1)
    return value * cosines + turned * sines

def doc_positions(segment):
    places = jnp.arange(segment.shape[0], dtype=jnp.int32)
    starts = jnp.concatenate([jnp.ones((1,), dtype=jnp.bool_), segment[1:] != segment[:-1]])
    return places - lax.cummax(jnp.where(starts, places, 0), axis=0)

def rope_tables(positions):
    inverse_freq = rope_base ** (-(jnp.arange(HEAD_DIM // 2, dtype=jnp.float32) * 2.0) / HEAD_DIM)
    angles = positions.astype(jnp.float32)[:, None] * inverse_freq[None, :]
    cosines = jnp.concatenate([jnp.cos(angles), jnp.cos(angles)], axis=-1)
    sines = jnp.concatenate([jnp.sin(angles), jnp.sin(angles)], axis=-1)
    return (cosines[:, None, :], sines[:, None, :])

def matmul(left, right):
    return jnp.dot(left, right, precision=highest, preferred_element_type=jnp.float32)

def matmul_t(left, right):
    return lax.dot_general(left, right, (((1,), (1,)), ((), ())), precision=highest, preferred_element_type=jnp.float32)

def feed_forward(value, gain, matrices, base):
    hidden = low(rms_apply(value, gain))
    gate_out = low_back(matmul(hidden, matrices[:, base:base + FF]))
    up_out = low_back(matmul(hidden, matrices[:, base + FF:base + 2 * FF]))
    mixed = low(jax.nn.silu(gate_out) * up_out)
    return value + low_back(matmul_t(mixed, matrices[:, base + 2 * FF:base + 3 * FF]))

def conv_layer(value, segment, conv_mats, vectors):
    hidden = low(rms_apply(value, vectors[0]))
    proj = low_back(matmul(hidden, conv_mats[:, :3 * D]))
    gate_b = proj[:, :D]
    gate_c = proj[:, D:2 * D]
    inner = proj[:, 2 * D:]
    mixed = gate_b * inner
    prev_one = jnp.concatenate([jnp.full((1,), -1, jnp.int32), segment[:-1]])
    prev_two = jnp.concatenate([jnp.full((2,), -1, jnp.int32), segment[:-2]])
    mask_one = (prev_one == segment).astype(jnp.float32)[:, None]
    mask_two = (prev_two == segment).astype(jnp.float32)[:, None]
    shifted_one = jnp.concatenate([jnp.zeros((1, D), jnp.float32), mixed[:-1]], axis=0)
    shifted_two = jnp.concatenate([jnp.zeros((2, D), jnp.float32), mixed[:-2]], axis=0)
    conv = vectors[4] * mixed + vectors[5] * shifted_one * mask_one + vectors[6] * shifted_two * mask_two
    outer = low(gate_c * conv)
    value = value + low_back(matmul_t(outer, conv_mats[:, 3 * D:4 * D]))
    return feed_forward(value, vectors[1], conv_mats, 4 * D)

def attend_block(q_block, q_pos, q_seg, keys_all, values_all, k_seg, k_pos):
    scores = jnp.einsum('tgrd,ngd->grtn', q_block, keys_all, precision=highest) * HEAD_DIM ** (-0.5)
    scores = low_back(scores)
    allowed = (k_pos[None, :] <= q_pos[:, None]) & (k_seg[None, :] == q_seg[:, None])
    masked = jnp.where(allowed, scores, masked_score)
    row_top = lax.optimization_barrier(jnp.max(masked, axis=-1, keepdims=True))
    exp_total = lax.optimization_barrier(jnp.sum(jnp.where(allowed, jnp.exp(masked - row_top), 0.0), axis=-1, keepdims=True))
    weights = jnp.where(allowed, jnp.exp(masked - row_top - jnp.log(exp_total)), 0.0)
    return jnp.einsum('grtn,ngd->tgrd', low(weights), values_all, precision=highest)

def attention_layer(value, segment, attn_mats, vectors, head_gains):
    length = value.shape[0]
    group = HEADS // KV_HEADS
    qkv_width = D + 2 * KVW
    hidden = low(rms_apply(value, vectors[2]))
    qkv = low_back(matmul(hidden, attn_mats[:, :qkv_width]))
    q_raw = qkv[:, :D].reshape(length, HEADS, HEAD_DIM)
    k_raw = qkv[:, D:D + KVW].reshape(length, KV_HEADS, HEAD_DIM)
    values_all = low(qkv[:, D + KVW:].reshape(length, KV_HEADS, HEAD_DIM))
    cosines, sines = rope_tables(doc_positions(segment))
    query = low(rotate(rms_apply(q_raw, head_gains[0]), cosines, sines))
    keys_all = low(rotate(rms_apply(k_raw, head_gains[1]), cosines, sines))
    block_rows = min(256, length)
    block_count = length // block_rows
    places = jnp.arange(length, dtype=jnp.int32)
    q_blocks = query.reshape(block_count, block_rows, KV_HEADS, group, HEAD_DIM)
    blockwise = jax.checkpoint(attend_block)
    attended = lax.map(lambda block_item: blockwise(block_item[0], block_item[1], block_item[2], keys_all, values_all, segment, places), (q_blocks, places.reshape(block_count, block_rows), segment.reshape(block_count, block_rows)))
    attended = low(low_back(attended.reshape(length, D)))
    value = value + low_back(matmul_t(attended, attn_mats[:, qkv_width:qkv_width + D]))
    return feed_forward(value, vectors[3], attn_mats, qkv_width + D)

def forward(tokens, conv_mats, attn_mats, vectors, head_gains, segments):
    results = []
    for seq_index in range(SEQS):
        hidden = conv_layer(tokens[seq_index], segments[seq_index], conv_mats, vectors)
        results.append(attention_layer(hidden, segments[seq_index], attn_mats, vectors, head_gains))
    return jnp.stack(results)

def adam_update(master, first_moment, second, gradient, step_value):
    first_new = beta_one * first_moment + (1.0 - beta_one) * gradient
    second_new = beta_two * second + (1.0 - beta_two) * gradient * gradient
    first_hat = first_new / (1.0 - beta_one ** step_value)
    second_hat = second_new / (1.0 - beta_two ** step_value)
    master_new = master - learn_rate * (first_hat / (jnp.sqrt(second_hat) + adam_eps) + decay_rate * master)
    return (master_new, first_new, second_new)

def reference(tokens, segments, cotangent, conv_weights, attn_weights, vectors, head_gains, master_conv, first_conv, second_conv, master_attn, first_attn, second_attn):

    def wrapped(tok_in, conv_in, attn_in, vec_in, gain_in):
        return forward(tok_in, conv_in, attn_in, vec_in, gain_in, segments)
    outputs, pullback = jax.vjp(wrapped, tokens.astype(jnp.float32), conv_weights.astype(jnp.float32), attn_weights.astype(jnp.float32), vectors, head_gains)
    grad_tokens, grad_conv, grad_attn, grad_vectors, grad_gains = pullback(cotangent.astype(jnp.float32))
    step_value = jnp.float32(STEP)
    new_master_conv, new_first_conv, new_second_conv = adam_update(master_conv, first_conv, second_conv, grad_conv, step_value)
    new_master_attn, new_first_attn, new_second_attn = adam_update(master_attn, first_attn, second_attn, grad_attn, step_value)
    return (outputs.astype(jnp.bfloat16), grad_tokens, grad_conv, grad_attn, grad_vectors, grad_gains, new_master_conv, new_first_conv, new_second_conv, new_master_attn, new_first_attn, new_second_attn, new_master_conv.astype(jnp.bfloat16), new_master_attn.astype(jnp.bfloat16))
```

```python
import functools
import jax
import jax.numpy as jnp
from jax import lax
from jax.sharding import Mesh, PartitionSpec as P
import jax.experimental.pallas as pl
import jax.experimental.pallas.tpu as pltpu

D = 1024
FF = 4608
HEADS = 16
KV_HEADS = 8
HEAD_DIM = 64
STEP = 5
KVW = 512
T = 128
QF = FF // 4
QD = D // 4
CW = 4 * QD + 3 * QF
AW = 3 * QD + 3 * QF

norm_eps = 1e-05
rope_base = 1000000.0
learn_rate = 0.01
decay_rate = 0.1
beta_one = 0.9
beta_two = 0.95
adam_eps = 1e-08

MESH = pl.DeviceIdType.MESH
BF = jnp.bfloat16
F32 = jnp.float32
PLANE = ((1, 1), (1, 0), (0, 1))

CONV_PARTS = (
    (0, QD, 0, 0),
    (D, QD, QD, 0),
    (2 * D, QD, 2 * QD, 0),
    (3 * D, QD, 3 * QD, 1),
    (4 * D, QF, 4 * QD, 2),
    (4 * D + FF, QF, 4 * QD + QF, 3),
    (4 * D + 2 * FF, QF, 4 * QD + 2 * QF, 4),
)
ATTN_PARTS = (
    (0, QD, 0, 0),
    (D, KVW // 4, QD, 0),
    (D + KVW, KVW // 4, QD + KVW // 4, 0),
    (2 * D, QD, 2 * QD, 1),
    (3 * D, QF, 3 * QD, 2),
    (3 * D + FF, QF, 3 * QD + QF, 3),
    (3 * D + 2 * FF, QF, 3 * QD + 2 * QF, 4),
)
CONV_SPANS = ((0, 768), (768, 256), (1024, QF), (1024 + QF, QF), (1024 + 2 * QF, QF))
ATTN_SPANS = ((0, 512), (512, 256), (768, QF), (768 + QF, QF), (768 + 2 * QF, QF))


def nn(a, b):
    return jnp.dot(a, b, preferred_element_type=F32)


def nt(a, b):
    return lax.dot_general(a, b, (((1,), (1,)), ((), ())), preferred_element_type=F32)


def tn(a, b):
    return lax.dot_general(a, b, (((0,), (0,)), ((), ())), preferred_element_type=F32)


def rms_scale(v):
    return lax.rsqrt(jnp.mean(v * v, axis=-1, keepdims=True) + norm_eps)


class Place:
    def __init__(self, O):
        self.O = O
        self.x, self.z = lax.axis_index("dp"), lax.axis_index("z")
        self.y, self.c = lax.axis_index("y"), lax.axis_index("c")
        self.r = self.x * 2 + self.y

    def at(self, dx=0, dz=0, dy=0, dc=0):
        out = {}
        if not (isinstance(dx, int) and dx == 0):
            out["dp"] = lax.rem(self.x + dx, 2)
        if not (isinstance(dz, int) and dz == 0):
            out["z"] = lax.rem(self.z + dz, self.O)
        if not (isinstance(dy, int) and dy == 0):
            out["y"] = lax.rem(self.y + dy, 2)
        if not (isinstance(dc, int) and dc == 0):
            out["c"] = lax.rem(self.c + dc, 2)
        return out

    def block(self, dx, dy):
        return lax.rem(self.x + dx, 2) * 2 + lax.rem(self.y + dy, 2)


def greet(here):
    O = here.O
    barrier = pltpu.get_barrier_semaphore()

    def hello(**k):
        pl.semaphore_signal(barrier, inc=1, device_id=here.at(**k), device_id_type=MESH)

    hello(dx=1, dy=1)
    hello(dx=1)
    hello(dy=1)
    hello(dc=1)
    hello(dz=1, dc=1)
    hello(dz=O - 1, dc=1)

    def along(dz, carry):
        for dy in (0, 1):
            hello(dz=dz, dy=dy)
        return carry

    lax.fori_loop(1, O, along, 0)
    pl.semaphore_wait(barrier, 6 + 2 * (O - 1))


def remote(src, dst, ss, rs, dev):
    return pltpu.make_async_remote_copy(
        src_ref=src, dst_ref=dst, send_sem=ss, recv_sem=rs, device_id=dev, device_id_type=MESH
    )


def gather_block(here, H, ss, rs):
    out = []
    for k, (dx, dy) in enumerate(PLANE):
        cp = remote(H.at[here.r], H.at[here.r], ss.at[k], rs.at[k], here.at(dx=dx, dy=dy))
        cp.start()
        out.append(cp)
    return out


def wait_all(copies):
    for cp in copies:
        cp.wait()


def scatter_sums(here, tile_fn, part, own, S, R, ss, rs):
    out = []
    for n in (0, 1):
        part[...] = tile_fn(n).reshape(4, T, D // 2)
        for k, (dx, dy) in enumerate(PLANE):
            S[n, k] = part[here.block(dx, dy)].astype(BF)
            cp = remote(S.at[n, k], R.at[n, k], ss.at[n, k], rs.at[n, k], here.at(dx=dx, dy=dy))
            cp.start()
            out.append(cp)
        own[:, n * (D // 2) : (n + 1) * (D // 2)] = part[here.r]
    return out


def sum_blocks(own, R):
    halves = []
    for n in (0, 1):
        t = own[:, n * (D // 2) : (n + 1) * (D // 2)]
        for k in range(3):
            t = t + R[n, k].astype(F32)
        halves.append(t)
    return jnp.concatenate(halves, axis=1)


class Weights:
    def __init__(self, here, hbm, W, parts, spans, ls, ss, rs, cs, cr):
        self.here, self.hbm, self.W = here, hbm, W
        self.parts, self.spans = parts, spans
        self.ls, self.ss, self.rs, self.cs, self.cr = ls, ss, rs, cs, cr

    def source(self, part, dy):
        base, width, _, _ = part
        chip = self.here.x * 2 + lax.rem(self.here.y + dy, 2)
        return self.hbm.at[:, pl.ds(pl.multiple_of(base + chip * width, 128), width)]

    def target(self, part):
        _, width, place, _ = part
        h = self.here
        return self.W.at[h.z * 2 + h.y, h.c, :, pl.ds(place, width)]

    def start(self):
        h = self.here
        for part in self.parts:
            g = part[3]
            pltpu.make_async_copy(self.source(part, 0), self.target(part), self.ls.at[g]).start()
        for part in self.parts:
            g = part[3]
            remote(self.source(part, 1), self.target(part), self.ss.at[g], self.rs.at[g], h.at(dy=1)).start()

            def along(dz, carry):
                for dy in (0, 1):
                    remote(
                        self.source(part, dy), self.target(part), self.ss.at[g], self.rs.at[g], h.at(dz=dz, dy=dy)
                    ).start()
                return carry

            lax.fori_loop(1, h.O, along, 0)

    def bytes_of(self, g, shards):
        place, width = self.spans[g]
        return self.W.at[pl.ds(0, shards), 0, :, pl.ds(place, width)]

    def arrive(self, g):
        h = self.here
        place, width = self.spans[g]
        one = self.bytes_of(g, 1)
        pltpu.make_async_copy(one, one, self.ls.at[g]).wait()
        rest = self.bytes_of(g, 2 * h.O - 1)
        pltpu.make_async_copy(rest, rest, self.rs.at[g]).wait()
        mine = self.W.at[:, h.c, :, pl.ds(place, width)]
        cp = remote(mine, mine, self.cs.at[g], self.cr.at[g], h.at(dc=1))
        cp.start()
        cp.wait()

    def finish(self):
        for g in range(5):
            rest = self.bytes_of(g, 2 * self.here.O - 1)
            pltpu.make_async_copy(rest, rest, self.ss.at[g]).wait()


def cols(W, place, width):
    v = W[:, :, :, pl.ds(place, width)]
    return v.reshape(D, width)


def rows_of(W, n, place, width):
    h = W.shape[0] // 2
    v = W[n * h : (n + 1) * h, :, :, pl.ds(place, width)]
    return v.reshape(D // 2, width)


def lane_low(shape):
    return lax.broadcasted_iota(jnp.int32, shape, len(shape) - 1) < 64


def lane_first(shape):
    return lax.rem(lax.broadcasted_iota(jnp.int32, shape, len(shape) - 1), 64) < 32


def head_mean(v):
    low = lane_low(v.shape)
    a = jnp.sum(jnp.where(low, v, 0.0), axis=-1, keepdims=True)
    b = jnp.sum(jnp.where(low, 0.0, v), axis=-1, keepdims=True)
    return jnp.where(low, a, b) * (1.0 / HEAD_DIM)


def turn(v):
    return jnp.where(lane_first(v.shape), pltpu.roll(v, 96, 1), pltpu.roll(v, 32, 1))


def to_pairs(left, right):
    low = lane_low(left.shape)
    a = jnp.where(low, left, pltpu.roll(right, 64, 1))
    b = jnp.where(low, pltpu.roll(left, 64, 1), right)
    return a, b


def stacked(a, b):
    low = lane_low(a.shape)
    zero = jnp.zeros_like(a)
    return (jnp.where(low, a, zero), jnp.where(low, b, zero), jnp.where(low, zero, a), jnp.where(low, zero, b))


def ffn_forward_tile(H, W, gate_at, up_at, gu, u, n):
    w = QF // 3
    h = H[...].reshape(4 * T, D)
    at = pl.multiple_of(n * w, 128)
    gate = nn(h, cols(W, gate_at + at, w))
    up = nn(h, cols(W, up_at + at, w))
    gu[0, :, pl.ds(at, w)] = gate
    gu[1, :, pl.ds(at, w)] = up
    u[:, pl.ds(at, w)] = (gate / (1.0 + jnp.exp(-gate)) * up).astype(BF)


def taps(here, vec):
    at = pl.ds(pl.multiple_of(here.r * QD, 128), QD)
    return tuple(vec[4 + i : 5 + i, at] for i in range(3))


def behind(here, b, mine, from_c, from_z, start):
    z, c, yb = here.z, here.c, b % 2
    if yb:
        before = jnp.where(c == 1, from_c[2 * b : 2 * b + 2], from_c[2 * b - 2 : 2 * b])
    else:
        before = jnp.where(c == 1, from_c[2 * b : 2 * b + 2], from_z[2 * b + 2 : 2 * b + 4])
    row = lax.broadcasted_iota(jnp.int32, (T, QD), 0)
    one = jnp.where(row == 0, before[1:2], pltpu.roll(mine, 1, 0))
    two = jnp.where(row == 0, before[0:1], jnp.where(row == 1, before[1:2], pltpu.roll(mine, 2, 0)))
    t = z * 512 + yb * 256 + c * T + lax.broadcasted_iota(jnp.int32, (T, 1), 0)
    pos = t - start[b * T : (b + 1) * T, 0:1]
    return one, two, jnp.where(pos >= 1, 1.0, 0.0), jnp.where(pos >= 2, 1.0, 0.0)


def forward_kernel(
    O, tok, vec, hg, cosb, sinb, start, wc_hbm, wa_hbm,
    out_tok, x1, x2, x3, h1, h2, h3, h4, bcx, cz, gu1, gu2, qkr, kv, oab, lse, wc, wa, Q, tail_c, tail_z,
    u, part, own, S, R, tails, acc,
    ags, agr, rss, rsr, hs, hr, kvs, kvr, wls, wss, wrs, wcs, wcr,
):
    here = Place(O)
    x, y, z, c, r = here.x, here.y, here.z, here.c, here.r
    greet(here)
    conv = Weights(here, wc_hbm, wc, CONV_PARTS, CONV_SPANS, wls.at[0], wss.at[0], wrs.at[0], wcs.at[0], wcr.at[0])
    attn = Weights(here, wa_hbm, wa, ATTN_PARTS, ATTN_SPANS, wls.at[1], wss.at[1], wrs.at[1], wcs.at[1], wcr.at[1])
    conv.start()

    x0 = tok[...].astype(F32)
    h1[r] = (x0 * rms_scale(x0) * vec[0:1, :]).astype(BF)
    copies = gather_block(here, h1, ags.at[0], agr.at[0])
    attn.start()
    conv.arrive(0)
    wait_all(copies)

    h = h1[...].reshape(4 * T, D)
    for i in range(3):
        bcx[i] = nn(h, cols(wc, i * QD, QD))
    bx = bcx[0] * bcx[2]
    for b in range(4):
        tails[2 * b : 2 * b + 2, :] = bx[b * T + T - 2 : b * T + T, :]
    over = remote(tails, tail_c, hs.at[0], hr.at[0], here.at(dc=1))
    over.start()
    ahead = remote(tails, tail_z, hs.at[1], hr.at[1], here.at(dz=1, dc=1))

    @pl.when((c == 1) & (z < O - 1))
    def _():
        ahead.start()

    over.wait()

    @pl.when((c == 0) & (z > 0))
    def _():
        ahead.wait_recv()

    @pl.when((c == 1) & (z < O - 1))
    def _():
        ahead.wait_send()

    tap0, tap1, tap2 = taps(here, vec)
    from_c, from_z = tail_c[...], jnp.where(z > 0, tail_z[...], 0.0)
    for b in range(4):
        mine = bx[b * T : (b + 1) * T, :]
        one, two, m1, m2 = behind(here, b, mine, from_c, from_z, start)
        cz[b * T : (b + 1) * T, :] = tap0 * mine + tap1 * one * m1 + tap2 * two * m2
    yc = (bcx[1] * cz[...]).astype(BF)
    conv.arrive(1)
    copies = scatter_sums(
        here, lambda n: nt(yc, rows_of(wc, n, 3 * QD, QD)), part, own, S.at[0], R.at[0], rss.at[0], rsr.at[0]
    )
    wait_all(copies)
    xn = tok[...].astype(F32) + sum_blocks(own, R.at[0])
    x1[...] = xn
    h2[r] = (xn * rms_scale(xn) * vec[1:2, :]).astype(BF)
    copies = gather_block(here, h2, ags.at[1], agr.at[1])
    conv.arrive(2)
    conv.arrive(3)
    wait_all(copies)

    def ffn1(n, carry):
        ffn_forward_tile(h2, wc, 4 * QD, 4 * QD + QF, gu1, u, n)
        return carry

    lax.fori_loop(0, 3, ffn1, 0)
    conv.arrive(4)
    copies = scatter_sums(
        here, lambda n: nt(u[...], rows_of(wc, n, 4 * QD + 2 * QF, QF)), part, own, S.at[1], R.at[1], rss.at[1], rsr.at[1]
    )
    wait_all(copies)
    xn = x1[...] + sum_blocks(own, R.at[1])
    x2[...] = xn
    h3[r] = (xn * rms_scale(xn) * vec[2:3, :]).astype(BF)
    copies = gather_block(here, h3, ags.at[2], agr.at[2])
    attn.arrive(0)
    wait_all(copies)

    qkv = nn(h3[...].reshape(4 * T, D), cols(wa, 0, 512))
    qa, qb = to_pairs(qkv[:, 0:128], qkv[:, 128:256])
    raw = (qa, qb, qkv[:, 256:384])
    turned = []
    for i in range(3):
        qkr[i] = raw[i]
        gain = hg[0:1, :] if i < 2 else hg[1:2, :]
        w = raw[i] * lax.rsqrt(head_mean(raw[i] * raw[i]) + norm_eps) * gain
        turned.append(w * cosb[...] + turn(w) * sinb[...])
    keys = turned[2].astype(BF)
    values = qkv[:, 384:512].astype(BF)
    for b in range(4):
        kv[z, b, c, :, 0:128] = keys[b * T : (b + 1) * T]
        kv[z, b, c, :, 128:256] = values[b * T : (b + 1) * T]
    mine = kv.at[z, :, c]

    def send_up(dz, carry):
        @pl.when(z + dz < O)
        def _():
            remote(mine, mine, kvs.at[dz], kvr.at[dz], here.at(dz=dz)).start()

        return carry

    lax.fori_loop(1, O, send_up, 0)
    pair0 = remote(mine, mine, kvs.at[0], kvr.at[0], here.at(dc=1))
    pair0.start()
    for s in (0, 1):
        low4 = stacked(*(
            (turned[i][s * 256 : (s + 1) * 256] * (HEAD_DIM ** -0.5)).astype(BF) for i in (0, 1)
        ))
        for g in range(4):
            Q[s, g] = low4[g]

    def pass_on(dz, carry):
        @pl.when(z - dz >= 0)
        def _():
            got = kv.at[z - dz, :, c]
            remote(mine, mine, kvs.at[dz], kvr.at[dz], here.at(dz=dz)).wait_recv()
            remote(got, got, kvs.at[O + dz], kvr.at[O + dz], here.at(dc=1)).start()

        return carry

    lax.fori_loop(1, O, pass_on, 0)
    pair0.wait()

    def pass_wait(dz, carry):
        @pl.when(z - dz >= 0)
        def _():
            got = kv.at[z - dz, :, c]
            remote(got, got, kvs.at[O + dz], kvr.at[O + dz], here.at(dc=1)).wait()

        @pl.when(z + dz < O)
        def _():
            remote(mine, mine, kvs.at[dz], kvr.at[dz], here.at(dz=dz)).wait_send()

        return carry

    lax.fori_loop(1, O, pass_wait, 0)

    low = lane_low((256, 128))
    for s in (0, 1):
        acc[...] = jnp.zeros_like(acc)
        first_of = start[s * 256 : (s + 1) * 256, 0:1]
        row = lax.broadcasted_iota(jnp.int32, (256, 1), 0)
        t = z * 512 + lax.div(row, T) * 256 + c * T + lax.rem(row, T)

        def chunk(j, carry):
            block = kv[lax.div(j, 2), 2 * s + lax.rem(j, 2)].reshape(256, 256)
            k, v = block[:, 0:128], block[:, 128:256]
            one = jnp.ones_like(v)
            v_low = jnp.where(low, v, one)
            v_high = jnp.where(low, one, v)
            at = j * 256 + lax.broadcasted_iota(jnp.int32, (256, 256), 1)
            allowed = (at >= first_of) & (at <= t)
            for g in range(4):
                sc = nt(Q[s, g], k)
                p = jnp.where(allowed, jnp.exp(sc), 0.0).astype(BF)
                acc[g] += nn(p, v_low if g < 2 else v_high)
            return carry

        lax.fori_loop(0, 2 * z + 2, chunk, 0)
        heads = []
        for g in range(4):
            a = acc[g]
            other = pltpu.roll(a, 64, 1)
            heads.append(a / other)
            total = jnp.where(low, other, a) if g < 2 else jnp.where(low, a, other)
            lse[s, :, g * 256 : (g + 1) * 256] = jnp.transpose(jnp.log(total))[0:8, :]
        oab[0, s * 256 : (s + 1) * 256, :] = jnp.where(low, heads[0], heads[2])
        oab[1, s * 256 : (s + 1) * 256, :] = jnp.where(low, heads[1], heads[3])
    left, right = to_pairs(oab[0], oab[1])
    ao = jnp.concatenate([left, right], axis=1).astype(BF)
    attn.arrive(1)
    copies = scatter_sums(
        here, lambda n: nt(ao, rows_of(wa, n, 2 * QD, QD)), part, own, S.at[0], R.at[0], rss.at[2], rsr.at[2]
    )
    wait_all(copies)
    xn = x2[...] + sum_blocks(own, R.at[0])
    x3[...] = xn
    h4[r] = (xn * rms_scale(xn) * vec[3:4, :]).astype(BF)
    copies = gather_block(here, h4, ags.at[3], agr.at[3])
    attn.arrive(2)
    attn.arrive(3)
    wait_all(copies)

    def ffn2(n, carry):
        ffn_forward_tile(h4, wa, 3 * QD, 3 * QD + QF, gu2, u, n)
        return carry

    lax.fori_loop(0, 3, ffn2, 0)
    attn.arrive(4)
    copies = scatter_sums(
        here, lambda n: nt(u[...], rows_of(wa, n, 3 * QD + 2 * QF, QF)), part, own, S.at[1], R.at[1], rss.at[3], rsr.at[3]
    )
    wait_all(copies)
    out_tok[...] = (x3[...] + sum_blocks(own, R.at[1])).astype(BF)
    conv.finish()
    attn.finish()


def any_spec():
    return pl.BlockSpec(memory_space=pl.ANY)


def vmem():
    return pl.BlockSpec(memory_space=pltpu.VMEM)


def forward(O, tok, vec, hg, cosb, sinb, start, wc_hbm, wa_hbm):
    sds = jax.ShapeDtypeStruct
    G = 4 * T
    outs = (
        sds((T, D), BF),
        *(sds((T, D), F32) for _ in range(3)),
        *(sds((4, T, D), BF) for _ in range(4)),
        sds((3, G, QD), F32), sds((G, QD), F32),
        sds((2, G, QF), F32), sds((2, G, QF), F32),
        sds((3, G, 128), F32), sds((O, 4, 2, T, 256), BF), sds((2, G, 128), F32), sds((2, 8, 2 * G), F32),
        sds((2 * O, 2, D // (4 * O), CW), BF), sds((2 * O, 2, D // (4 * O), AW), BF),
        sds((2, 4, 256, 128), BF), sds((8, QD), F32), sds((8, QD), F32),
    )
    dma = pltpu.SemaphoreType.DMA
    return pl.pallas_call(
        functools.partial(forward_kernel, O),
        out_shape=outs,
        in_specs=[vmem()] * 6 + [any_spec()] * 2,
        out_specs=tuple(vmem() for _ in outs),
        scratch_shapes=[
            pltpu.VMEM((G, QF), BF), pltpu.VMEM((4, T, D // 2), F32), pltpu.VMEM((T, D), F32),
            pltpu.VMEM((2, 2, 3, T, D // 2), BF), pltpu.VMEM((2, 2, 3, T, D // 2), BF),
            pltpu.VMEM((8, QD), F32), pltpu.VMEM((4, 256, 128), F32),
            dma((4, 3)), dma((4, 3)), dma((4, 2, 3)), dma((4, 2, 3)), dma((2,)), dma((2,)),
            dma((2 * O,)), dma((2 * O,)),
            dma((2, 5)), dma((2, 5)), dma((2, 5)), dma((2, 5)), dma((2, 5)),
        ],
        compiler_params=pltpu.CompilerParams(
            collective_id=1, has_side_effects=True, vmem_limit_bytes=61 * 2**20
        ),
        cost_estimate=pl.CostEstimate(flops=10**10, bytes_accessed=6 * 10**7, transcendentals=10**7),
        name="forward",
    )(tok, vec, hg, cosb, sinb, start, wc_hbm, wa_hbm)


def tables(O, segments):
    seg = lax.all_gather(segments, ("dp", "z", "y", "c"), axis=0, tiled=True).reshape(2, O * 512)
    n0 = jnp.sum((seg < 1).astype(jnp.int32), axis=1)
    n1 = jnp.sum((seg < 2).astype(jnp.int32), axis=1)
    z, c = lax.axis_index("z"), lax.axis_index("c")
    own = lax.dynamic_slice(
        seg.reshape(2, O, 2, 2, T), (0, z, 0, c, 0), (2, 1, 2, 1, T)
    ).reshape(2, 2, T)
    first = jnp.where(own == 0, 0, jnp.where(own == 1, n0[:, None, None], n1[:, None, None]))
    t = z * 512 + c * T + jnp.arange(2, dtype=jnp.int32)[None, :, None] * 256 + jnp.arange(T, dtype=jnp.int32)[None, None]
    pos = (t - first).reshape(4 * T)
    inverse_freq = rope_base ** (-(jnp.arange(HEAD_DIM // 2, dtype=F32) * 2.0) / HEAD_DIM)
    angles = pos.astype(F32)[:, None] * inverse_freq[None, :]
    cosines, sines = jnp.cos(angles), jnp.sin(angles)
    cosb = jnp.concatenate([cosines] * 4, axis=1)
    sinb = jnp.concatenate([-sines, sines] * 2, axis=1)
    return cosb, sinb, jnp.broadcast_to(first.reshape(4 * T, 1), (4 * T, 128))


def rms_back(x, gain, dh):
    r = rms_scale(x)
    inner = jnp.mean(x * gain * dh, axis=-1, keepdims=True)
    return r * gain * dh - x * (r * r * r) * inner, jnp.sum(dh * x * r, axis=0, keepdims=True)


class Keep:
    def __init__(self, stage, sem):
        self.stage, self.sem, self.flying = stage, sem, [None, None]
        self.turn = 0

    def put(self, left, right, out, place, width, step=384):
        i = self.turn
        self.turn = 1 - i
        if self.flying[i] is not None:
            self.flying[i].wait()
        step = min(step, width)
        stage = self.stage.at[i]
        shape = (*self.stage.shape[1:4], step)

        def body(n, carry):
            at = pl.multiple_of(n * step, 128)
            stage[:, :, :, pl.ds(at, step)] = nn(left[...], right(at, step)).astype(BF).reshape(shape)
            return carry

        lax.fori_loop(0, width // step, body, 0)
        cp = pltpu.make_async_copy(
            stage.at[:, :, :, pl.ds(0, width)], out.at[:, :, :, pl.ds(place, width)], self.sem.at[i]
        )
        cp.start()
        self.flying[i] = cp

    def finish(self):
        for cp in self.flying:
            if cp is not None:
                cp.wait()


def ffn_back_tile(DF, W, down_at, gu, dg, du, mx, n):
    w = QF // 3
    at = pl.multiple_of(n * w, 128)
    d = nn(DF[...].reshape(4 * T, D), cols(W, down_at + at, w))
    gate, up = gu[0, :, pl.ds(at, w)], gu[1, :, pl.ds(at, w)]
    sig = 1.0 / (1.0 + jnp.exp(-gate))
    silu = gate * sig
    dg[:, pl.ds(at, w)] = (d * up * (sig * (1.0 + gate * (1.0 - sig)))).astype(BF)
    du[:, pl.ds(at, w)] = (d * silu).astype(BF)
    mx[:, pl.ds(at, w)] = (silu * up).astype(BF)


def backward_kernel(
    O, cot, tok, vec, hg, cosb, sinb, start, start_row, x1, x2, x3, h1, h2, h3, h4, bcx, cz, gu1, gu2, qkr, kv, oab,
    lse, wc, wa, Q, tail_c, tail_z,
    dtok, vg, dwc, dwa,
    W, gu, DG, HH, dg, du, mx, LT, stage, part, own, S, R, dO, delta, dq, dqab, dkv, dkc, dkz, dkk, heads, head_c, head_z, dprev,
    ags, agr, rss, rsr, hs, hr, kvs, kvr, wls, gls, sts, hls,
):
    here = Place(O)
    x, y, z, c, r = here.x, here.y, here.z, here.c, here.r
    loads = [pltpu.make_async_copy(h, HH, hls.at[i]) for i, h in enumerate((h4, h3, h2, h1))]
    loads[0].start()

    def transposed(i):
        loads[i].wait()
        LT[...] = jnp.transpose(flat(HH))
        if i < 3:
            loads[i + 1].start()

    load_w = pltpu.make_async_copy(wa, W.at[:, :, :, pl.ds(0, AW)], wls.at[0])
    load_w.start()
    load_g = pltpu.make_async_copy(gu2, gu, gls.at[0])
    load_g.start()
    load_kv = pltpu.make_async_copy(kv, dkv, gls.at[2])
    load_kv.start()
    greet(here)
    keep = Keep(stage, sts)
    vg[...] = jnp.zeros_like(vg)

    DF = DG.at[0]
    DF[r] = cot[...]
    copies = gather_block(here, DF, ags.at[0], agr.at[0])
    load_w.wait()
    load_g.wait()
    wait_all(copies)

    def flat(H):
        return H[...].reshape(4 * T, D)

    def ffn_back(i, DF, at, x_in, gain_row, out, dy):
        def tile(n, carry):
            ffn_back_tile(DF, W, at + 2 * QF, gu, dg, du, mx, n)
            return carry

        lax.fori_loop(0, 3, tile, 0)
        copies = scatter_sums(
            here,
            lambda n: nt(dg[...], rows_of(W, n, at, QF)) + nt(du[...], rows_of(W, n, at + QF, QF)),
            part, own, S.at[i % 2], R.at[i % 2], rss.at[i], rsr.at[i],
        )
        LT[...] = jnp.transpose(flat(DF))
        keep.put(LT, lambda a, w: mx[:, pl.ds(a, w)], out, at + 2 * QF, QF)
        wait_all(copies)
        dx, dgain = rms_back(x_in[...], vec[gain_row : gain_row + 1, :], sum_blocks(own, R.at[i % 2]))
        vg[gain_row : gain_row + 1, :] = dgain
        dprev[...] = dy + dx
        H2 = DG.at[i + 1]
        H2[r] = dprev[...].astype(BF)
        copies = gather_block(here, H2, ags.at[i + 1], agr.at[i + 1])
        transposed(i)
        keep.put(LT, lambda a, w: dg[:, pl.ds(a, w)], out, at, QF)
        keep.put(LT, lambda a, w: du[:, pl.ds(a, w)], out, at + QF, QF)
        wait_all(copies)

    ffn_back(0, DF, 3 * QD, x3, 3, dwa, cot[...].astype(F32))
    load_g = pltpu.make_async_copy(gu1, gu, gls.at[1])
    load_g.start()

    DA = DG.at[1]
    d_out = nn(flat(DA), cols(W, 2 * QD, QD)).astype(BF).astype(F32)
    left, right = to_pairs(oab[0], oab[1])
    ao = jnp.concatenate([left, right], axis=1).astype(BF)
    mx[:, 0:QD] = ao
    LT[...] = jnp.transpose(flat(DA))
    keep.put(LT, lambda a, w: mx[:, pl.ds(a, w)], dwa, 2 * QD, QD, QD)
    da, db = to_pairs(d_out[:, 0:128], d_out[:, 128:256])
    for s in (0, 1):
        rows = slice(s * 256, (s + 1) * 256)
        four = stacked(da[rows], db[rows])
        o_of = (oab[0, rows, :], oab[1, rows, :])
        for g in range(4):
            dO[s, g] = four[g].astype(BF)
            dl = jnp.sum(four[g] * o_of[g % 2], axis=-1, keepdims=True)
            delta[s, :, g * 256 : (g + 1) * 256] = jnp.transpose(jnp.broadcast_to(dl, (256, 128)))[0:8, :]
    load_kv.wait()
    low = lane_low((256, 128))
    for s in (0, 1):
        dq[...] = jnp.zeros_like(dq)
        first_of = start_row[0:1, s * 256 : (s + 1) * 256]
        col = lax.broadcasted_iota(jnp.int32, (1, 256), 1)
        t = z * 512 + lax.div(col, T) * 256 + c * T + lax.rem(col, T)

        def chunk(j, carry):
            block = dkv[lax.div(j, 2), 2 * s + lax.rem(j, 2)].reshape(256, 256)
            k, v = block[:, 0:128], block[:, 128:256]
            at = j * 256 + lax.broadcasted_iota(jnp.int32, (256, 256), 0)
            allowed = (at >= first_of) & (at <= t)
            dk = jnp.zeros((256, 128), F32)
            dv = jnp.zeros((256, 128), F32)
            for g in range(4):
                span = slice(g * 256, (g + 1) * 256)
                p = jnp.where(allowed, jnp.exp(nt(k, Q[s, g]) - lse[s, 0:1, span]), 0.0)
                ds = (p * (nt(v, dO[s, g]) - delta[s, 0:1, span])).astype(BF)
                dv = dv + nn(p.astype(BF), dO[s, g])
                dk = dk + nn(ds, Q[s, g])
                dq[g] += tn(ds, k)
            dkv[lax.div(j, 2), 2 * s + lax.rem(j, 2)] = (
                jnp.concatenate([dk, dv], axis=1).astype(BF).reshape(2, T, 256)
            )
            return carry

        lax.fori_loop(0, 2 * z + 2, chunk, 0)
        rows = slice(s * 256, (s + 1) * 256)
        dqab[0, rows, :] = jnp.where(low, dq[0], dq[2]) * (HEAD_DIM ** -0.5)
        dqab[1, rows, :] = jnp.where(low, dq[1], dq[3]) * (HEAD_DIM ** -0.5)

    over = remote(dkv.at[:, :, 1 - c], dkc, kvs.at[0], kvr.at[0], here.at(dc=1))
    over.start()
    over.wait()

    def send_down(zz, carry):
        dkv[zz, :, c] = (dkv[zz, :, c].astype(F32) + dkc[zz].astype(F32)).astype(BF)
        d = z - zz
        remote(dkv.at[zz, :, c], dkz.at[z], kvs.at[d], kvr.at[d], here.at(dz=O - d)).start()
        return carry

    lax.fori_loop(0, z, send_down, 0)
    dkk[...] = (dkv[z, :, c].astype(F32) + dkc[z].astype(F32)).reshape(4 * T, 256)

    def take(d, carry):
        @pl.when(z + d < O)
        def _():
            remote(dkv.at[z, :, c], dkz.at[z + d], kvs.at[d], kvr.at[d], here.at(dz=O - d)).wait_recv()
            dkk[...] += dkz[z + d].astype(F32).reshape(4 * T, 256)

        return carry

    lax.fori_loop(1, O, take, 0)

    def sent(zz, carry):
        d = z - zz
        remote(dkv.at[zz, :, c], dkz.at[z], kvs.at[d], kvr.at[d], here.at(dz=O - d)).wait_send()
        return carry

    lax.fori_loop(0, z, sent, 0)

    for i in range(3):
        up = dqab[i] if i < 2 else dkk[:, 0:128]
        raw = qkr[i]
        gain = hg[0:1, :] if i < 2 else hg[1:2, :]
        dw = up * cosb[...] + turn(up * sinb[...])
        rr = lax.rsqrt(head_mean(raw * raw) + norm_eps)
        dgain = jnp.sum(dw * raw * rr, axis=0, keepdims=True)
        row = 8 if i < 2 else 9
        vg[row : row + 1, 0:128] += dgain
        draw = rr * gain * dw - raw * (rr * rr * rr) * head_mean(raw * gain * dw)
        if i < 2:
            dqab[i] = draw
        else:
            dg[:, 256:384] = draw.astype(BF)
    left, right = to_pairs(dqab[0], dqab[1])
    dg[:, 0:128] = left.astype(BF)
    dg[:, 128:256] = right.astype(BF)
    dg[:, 384:512] = dkk[:, 128:256].astype(BF)
    copies = scatter_sums(
        here, lambda n: nt(dg[:, 0:512], rows_of(W, n, 0, 512)), part, own, S.at[1], R.at[1], rss.at[1], rsr.at[1]
    )
    load_w = pltpu.make_async_copy(wc, W, wls.at[1])
    load_w.start()
    transposed(1)
    keep.put(LT, lambda a, w: dg[:, pl.ds(a, w)], dwa, 0, 512, 256)
    wait_all(copies)
    dx, dgain = rms_back(x2[...], vec[2:3, :], sum_blocks(own, R.at[1]))
    vg[2:3, :] = dgain
    dprev[...] += dx
    D2 = DG.at[2]
    D2[r] = dprev[...].astype(BF)
    copies = gather_block(here, D2, ags.at[2], agr.at[2])
    load_w.wait()
    load_g.wait()
    wait_all(copies)

    ffn_back(2, D2, 4 * QD, x1, 1, dwc, dprev[...])

    DD = DG.at[3]
    tap0, tap1, tap2 = taps(here, vec)
    from_c, from_z = tail_c[...], jnp.where(z > 0, tail_z[...], 0.0)
    dyc = nn(flat(DD), cols(W, 3 * QD, QD))
    mx[:, 0:QD] = (bcx[1] * cz[...]).astype(BF)
    dg[:, QD : 2 * QD] = (dyc * cz[...]).astype(BF)
    dzs = dyc * bcx[1]
    bx = bcx[0] * bcx[2]
    row = lax.broadcasted_iota(jnp.int32, (T, QD), 0)
    g0, g1, g2 = (jnp.zeros((1, QD), F32) for _ in range(3))
    for b in range(4):
        mine = bx[b * T : (b + 1) * T, :]
        dzb = dzs[b * T : (b + 1) * T, :]
        one, two, m1, m2 = behind(here, b, mine, from_c, from_z, start)
        g0 = g0 + jnp.sum(dzb * mine, axis=0, keepdims=True)
        g1 = g1 + jnp.sum(dzb * one * m1, axis=0, keepdims=True)
        g2 = g2 + jnp.sum(dzb * two * m2, axis=0, keepdims=True)
        b1 = tap1 * dzb * m1
        b2 = tap2 * dzb * m2
        heads[2 * b : 2 * b + 1, :] = b2[0:1]
        heads[2 * b + 1 : 2 * b + 2, :] = b1[0:1] + b2[1:2]
        dkk[b * T : (b + 1) * T, :] = (
            tap0 * dzb
            + jnp.where(row < T - 1, pltpu.roll(b1, T - 1, 0), 0.0)
            + jnp.where(row < T - 2, pltpu.roll(b2, T - 2, 0), 0.0)
        )
    over = remote(heads, head_c, hs.at[0], hr.at[0], here.at(dc=1))
    over.start()
    back = remote(heads, head_z, hs.at[1], hr.at[1], here.at(dz=O - 1, dc=1))

    @pl.when((c == 0) & (z > 0))
    def _():
        back.start()

    tap_at = pl.ds(pl.multiple_of(r * QD, 128), QD)
    vg[4:5, tap_at] = g0
    vg[5:6, tap_at] = g1
    vg[6:7, tap_at] = g2
    over.wait()

    @pl.when((c == 1) & (z < O - 1))
    def _():
        back.wait_recv()

    @pl.when((c == 0) & (z > 0))
    def _():
        back.wait_send()

    to_c, to_z = head_c[...], jnp.where(z < O - 1, head_z[...], 0.0)
    for b in range(4):
        rows = slice(b * T, (b + 1) * T)
        if b % 2:
            e = jnp.where(c == 0, to_c[2 * b : 2 * b + 2], to_z[2 * b - 2 : 2 * b])
        else:
            e = jnp.where(c == 0, to_c[2 * b : 2 * b + 2], to_c[2 * b + 2 : 2 * b + 4])
        dbx = dkk[rows, :] + jnp.where(row == T - 2, e[0:1], jnp.where(row == T - 1, e[1:2], 0.0))
        dg[rows, 0:QD] = (dbx * bcx[2, rows, :]).astype(BF)
        dg[rows, 2 * QD : 3 * QD] = (dbx * bcx[0, rows, :]).astype(BF)
    copies = scatter_sums(
        here, lambda n: nt(dg[:, 0:768], rows_of(W, n, 0, 768)), part, own, S.at[1], R.at[1], rss.at[3], rsr.at[3]
    )
    LT[...] = jnp.transpose(flat(DD))
    keep.put(LT, lambda a, w: mx[:, pl.ds(a, w)], dwc, 3 * QD, QD, QD)
    transposed(3)
    keep.put(LT, lambda a, w: dg[:, pl.ds(a, w)], dwc, 0, 768, 384)
    wait_all(copies)
    dx, dgain = rms_back(tok[...].astype(F32), vec[0:1, :], sum_blocks(own, R.at[1]))
    vg[0:1, :] = dgain
    dtok[...] = dprev[...] + dx
    keep.finish()


def backward(O, cot, tok, vec, hg, cosb, sinb, start, start_row, saved):
    (x1, x2, x3, h1, h2, h3, h4, bcx, cz, gu1, gu2, qkr, kv, oab, lse, wc, wa, Q, tail_c, tail_z) = saved
    sds = jax.ShapeDtypeStruct
    G = 4 * T
    rows = D // (4 * O)
    outs = (
        sds((T, D), F32), sds((16, D), F32),
        sds((2 * O, 2, rows, CW), BF), sds((2 * O, 2, rows, AW), BF),
    )
    dma = pltpu.SemaphoreType.DMA
    V = pltpu.VMEM
    args = (cot, tok, vec, hg, cosb, sinb, start, start_row, *saved)
    hbm = {id(a) for a in (gu1, gu2, wc, wa, kv, h1, h2, h3, h4)}
    return pl.pallas_call(
        functools.partial(backward_kernel, O),
        out_shape=outs,
        in_specs=[any_spec() if id(a) in hbm else vmem() for a in args],
        out_specs=(vmem(), vmem(), any_spec(), any_spec()),
        scratch_shapes=[
            V((2 * O, 2, rows, CW), BF), V((2, G, QF), F32), V((4, 4, T, D), BF), V((4, T, D), BF),
            V((G, QF), BF), V((G, QF), BF), V((G, QF), BF), V((D, G), BF), V((2, 2 * O, 2, rows, QF), BF),
            V((4, T, D // 2), F32), V((T, D), F32), V((2, 2, 3, T, D // 2), BF), V((2, 2, 3, T, D // 2), BF),
            V((2, 4, 256, 128), BF), V((2, 8, 2 * G), F32), V((4, 256, 128), F32), V((2, G, 128), F32),
            V((O, 4, 2, T, 256), BF), V((O, 4, T, 256), BF), V((O, 4, T, 256), BF), V((G, 256), F32),
            V((8, QD), F32), V((8, QD), F32), V((8, QD), F32), V((T, D), F32),
            dma((4, 3)), dma((4, 3)), dma((4, 2, 3)), dma((4, 2, 3)), dma((2,)), dma((2,)),
            dma((O,)), dma((O,)), dma((2,)), dma((3,)), dma((2,)), dma((4,)),
        ],
        compiler_params=pltpu.CompilerParams(
            collective_id=2, has_side_effects=True, vmem_limit_bytes=62 * 2**20
        ),
        cost_estimate=pl.CostEstimate(flops=2 * 10**10, bytes_accessed=10**8, transcendentals=10**7),
        name="backward",
    )(*args)


class Owners:
    def __init__(self, here, G, own, got, out, parts, spans, half, ls, cs, cr, ss, rs):
        self.here, self.G, self.own, self.got, self.out = here, G, own, got, out
        self.parts, self.spans, self.half = parts, spans, half
        self.ls, self.cs, self.cr, self.ss, self.rs = ls, cs, cr, ss, rs

    def span(self, g):
        place, width = self.spans[g]
        return pl.ds(place, width)

    def pair(self, g):
        h, at = self.here, self.span(g)
        return (
            pltpu.make_async_copy(self.G.at[:, h.c, :, at], self.own.at[:, :, at], self.ls.at[g]),
            remote(self.G.at[:, 1 - h.c, :, at], self.got.at[:, :, at], self.cs.at[g], self.cr.at[g], h.at(dc=1)),
        )

    def pieces(self, g):
        r, half = self.here.r, self.half
        out = []
        for base, width, place, group in self.parts:
            if group != g:
                continue
            first = half - base
            if 0 < first < 4 * width:
                assert first < width
                out.append((place, first, jnp.where(r == 0, 0, 1), jnp.where(r == 0, base, base + r * width - half)))
                out.append((place + first, width - first, 1, base + r * width + first - half))
            elif first >= 4 * width:
                out.append((place, width, 0, base + r * width))
            else:
                out.append((place, width, 1, base + r * width - half))
        return out

    def each(self, g, act, local):
        h = self.here
        for place, width, owner, at in self.pieces(g):
            dx = lax.rem(owner + h.x, 2)
            at = pl.multiple_of(at, 128)

            def one(dz, dy):
                shard = lax.rem(h.z + dz, h.O) * 2 + lax.rem(h.y + dy, 2)
                return (
                    self.own.at[shard, :, pl.ds(place, width)],
                    self.out.at[h.z, :, pl.ds(at, width)],
                )

            def along(dz, carry):
                for dy in (0, 1):
                    src, dst = one(dz, dy)
                    act(remote(src, dst, self.ss.at[g], self.rs, h.at(dx=dx, dz=dz, dy=dy)))
                return carry

            src, dst = one(0, 0)

            @pl.when(dx != 0)
            def _():
                act(remote(src, dst, self.ss.at[g], self.rs, h.at(dx=dx)))

            if local:

                @pl.when(dx == 0)
                def _():
                    pltpu.make_async_copy(src, dst, self.rs).start()

            src, dst = one(0, 1)
            act(remote(src, dst, self.ss.at[g], self.rs, h.at(dx=dx, dy=1)))
            lax.fori_loop(1, h.O, along, 0)

    def begin(self):
        for g in self.order:
            a, b = self.pair(g)
            a.start()
            b.start()

    order = (4, 2, 3, 1, 0)

    def send(self):
        for g in self.order:
            a, b = self.pair(g)
            a.wait()
            b.wait()
            at = self.span(g)
            self.own[:, :, at] = (self.own[:, :, at].astype(F32) + self.got[:, :, at].astype(F32)).astype(BF)
            self.each(g, lambda cp: cp.start(), True)

    def finish(self):
        for g in self.order:
            self.each(g, lambda cp: cp.wait_send(), False)
        pltpu.make_async_copy(self.out, self.out, self.rs).wait()


def owners_kernel(O, dwa, dwc, vg, ga, gc, total, own_a, got_a, own_c, got_c, v0, v1, v2, ls, cs, cr, ss, rs, vs, vr):
    here = Place(O)
    x, y, z, c, r = here.x, here.y, here.z, here.c, here.r
    barrier = pltpu.get_barrier_semaphore()

    def hello(**k):
        pl.semaphore_signal(barrier, inc=1, device_id=here.at(**k), device_id_type=MESH)

    def greet_all(dz, carry):
        for dx in (0, 1):
            for dy in (0, 1):
                hello(dx=dx, dz=dz, dy=dy)
        return carry

    for dx, dy in PLANE:
        hello(dx=dx, dy=dy)
    hello(dc=1)
    lax.fori_loop(1, O, greet_all, 0)
    pl.semaphore_wait(barrier, 4 + 4 * (O - 1))
    A = Owners(here, dwa, own_a, got_a, ga, ATTN_PARTS, ATTN_SPANS, (2 * D + D + 3 * FF) // 2, ls.at[0], cs.at[0], cr.at[0], ss.at[0], rs.at[0])
    Cv = Owners(here, dwc, own_c, got_c, gc, CONV_PARTS, CONV_SPANS, (4 * D + 3 * FF) // 2, ls.at[1], cs.at[1], cr.at[1], ss.at[1], rs.at[1])
    A.begin()
    Cv.begin()
    v0[c] = vg[...]
    cp = remote(v0.at[c], v0.at[c], vs.at[0], vr.at[0], here.at(dc=1))
    cp.start()
    A.send()
    cp.wait()
    v1[r] = v0[0] + v0[1]
    copies = []
    for k, (dx, dy) in enumerate(PLANE):
        cp = remote(v1.at[r], v1.at[r], vs.at[1 + k], vr.at[1 + k], here.at(dx=dx, dy=dy))
        cp.start()
        copies.append(cp)
    Cv.send()
    wait_all(copies)
    v2[z] = v1[0] + v1[1] + v1[2] + v1[3]

    def start(dz, carry):
        remote(v2.at[z], v2.at[z], vs.at[3 + dz], vr.at[3 + dz], here.at(dz=dz)).start()
        return carry

    lax.fori_loop(1, O, start, 0)

    def wait(dz, carry):
        remote(v2.at[z], v2.at[z], vs.at[3 + dz], vr.at[3 + dz], here.at(dz=dz)).wait()
        return carry

    lax.fori_loop(1, O, wait, 0)
    t = v2[0]
    for i in range(1, O):
        t = t + v2[i]
    total[...] = t
    A.finish()
    Cv.finish()


def owners(O, dwa, dwc, vg):
    sds = jax.ShapeDtypeStruct
    rows = D // (4 * O)
    dma = pltpu.SemaphoreType.DMA
    V = pltpu.VMEM
    return pl.pallas_call(
        functools.partial(owners_kernel, O),
        out_shape=(sds((O, rows, 2 * AW), BF), sds((O, rows, 2 * CW), BF), sds((16, D), F32)),
        in_specs=[any_spec(), any_spec(), vmem()],
        out_specs=(any_spec(), any_spec(), vmem()),
        scratch_shapes=[
            V((2 * O, rows, AW), BF), V((2 * O, rows, AW), BF), V((2 * O, rows, CW), BF), V((2 * O, rows, CW), BF),
            V((2, 16, D), F32), V((4, 16, D), F32), V((O, 16, D), F32),
            dma((2, 5)), dma((2, 5)), dma((2, 5)), dma((2, 5)), dma((2,)), dma((O + 3,)), dma((O + 3,)),
        ],
        compiler_params=pltpu.CompilerParams(
            collective_id=3, has_side_effects=True, vmem_limit_bytes=60 * 2**20
        ),
        cost_estimate=pl.CostEstimate(flops=10**8, bytes_accessed=6 * 10**7, transcendentals=0),
        name="owners",
    )(dwa, dwc, vg)


def adam_update(master, first_moment, second, gradient, step_value):
    first_new = beta_one * first_moment + (1.0 - beta_one) * gradient
    second_new = beta_two * second + (1.0 - beta_two) * gradient * gradient
    first_hat = first_new / (1.0 - beta_one**step_value)
    second_hat = second_new / (1.0 - beta_two**step_value)
    master_new = master - learn_rate * (
        first_hat / (jnp.sqrt(second_hat) + adam_eps) + decay_rate * master
    )
    return (master_new, first_new, second_new)


def shards(
    tokens, segments, cotangent, conv_weights, attn_weights, vectors, head_gains,
    master_conv, first_conv, second_conv, master_attn, first_attn, second_attn,
):
    O = lax.axis_size("z")
    cosb, sinb, start = tables(O, segments)
    start_row = jnp.broadcast_to(start[:, 0][None, :], (8, 4 * T))
    hg = jnp.concatenate([head_gains, head_gains], axis=1)
    tok = tokens[0]
    out_tok, *saved = forward(O, tok, vectors, hg, cosb, sinb, start, conv_weights, attn_weights)
    dtok, vg, dwc, dwa = backward(O, cotangent[0], tok, vectors, hg, cosb, sinb, start, start_row, saved)
    ga, gc, total = owners(O, dwa, dwc, vg)
    grad_attn = jnp.sum(ga.astype(F32), axis=0)
    grad_conv = jnp.sum(gc.astype(F32), axis=0)
    grad_vectors = total[0:7]
    grad_gains = total[8:10, 0:64] + total[8:10, 64:128]
    step_value = jnp.float32(STEP)
    new_conv = adam_update(master_conv, first_conv, second_conv, grad_conv, step_value)
    new_attn = adam_update(master_attn, first_attn, second_attn, grad_attn, step_value)
    return (
        out_tok[None], dtok[None], grad_conv, grad_attn, grad_vectors, grad_gains, *new_conv, *new_attn,
        lax.all_gather(new_conv[0].astype(BF), "dp", axis=1, tiled=True),
        lax.all_gather(new_attn[0].astype(BF), "dp", axis=1, tiled=True),
    )


def solution(mesh):
    outer = mesh.shape["ctx"] // 4
    split = Mesh(mesh.devices.reshape(mesh.shape["dp"], outer, 2, 2), ("dp", "z", "y", "c"))
    ctx = ("z", "y", "c")
    seq, rows, state = P("dp", ctx, None), P(ctx, None), P(ctx, "dp")
    return jax.shard_map(
        shards,
        mesh=split,
        in_specs=(seq, P("dp", ctx), seq, rows, rows, P(), P(), *([state] * 6)),
        out_specs=(seq, seq, state, state, P(), P(), *([state] * 6), rows, rows),
        check_vma=False,
    )
```

```python
import functools
import jax
import jax.numpy as jnp
from jax import lax
from jax.sharding import Mesh, PartitionSpec as P
import jax.experimental.pallas as pl
import jax.experimental.pallas.tpu as pltpu

D = 1024
FF = 4608
HEADS = 16
KV_HEADS = 8
HEAD_DIM = 64
STEP = 5
KVW = 512
T = 128
QF = FF // 4
QD = D // 4
CW = 4 * QD + 3 * QF
AW = 3 * QD + 3 * QF

norm_eps = 1e-05
rope_base = 1000000.0
learn_rate = 0.01
decay_rate = 0.1
beta_one = 0.9
beta_two = 0.95
adam_eps = 1e-08

MESH = pl.DeviceIdType.MESH

SCHEDULE = {
    "in": ("f0", "f1",),
    "start": ("p0", "p1", "f2",),
    "h1 sent": ("f3", "p2",),
    "h1 relayed": ("f4", "b0", "p3",),
    "h1": ("f5", "l0", "p4", "l1", "r0",),
    "conv": ("r1", "p5",),
    "x1 sent": (),
    "x1 relayed": ("b2", "f6", "f7",),
    "h2 sent": (),
    "h2 relayed": ("b3", "f8",),
    "gate1 0": ("l2", "r2",),
    "gate1 1": ("l3", "r3",),
    "gate1 2": ("l4", "r4",),
    "down1": ("p6", "l5", "p7", "r5", "p8",),
    "x2 sent": (),
    "x2 relayed": ("f9", "b6",),
    "h3 sent": ("p9", "f10", "b7",),
    "h3 relayed": ("f11", "l6", "l7",),
    "qkv": ("r6",),
    "kv sent": ("b8",),
    "kv": ("p10",),
    "half": ("p11", "b9",),
    "attended": ("l8", "r7",),
    "x3 sent": ("b10",),
    "x3 relayed": ("l9",),
    "h4 sent": ("b11",),
    "h4 relayed": (),
    "gate2 0": ("l10", "r8",),
    "gate2 1": ("l11", "r9",),
    "gate2 2": ("r10",),
    "down2": ("r11",),
    "x4 sent": (),
    "x4 relayed": (),
}
BF = jnp.bfloat16
F32 = jnp.float32
PLANE = ((1, 1), (1, 0), (0, 1))

TILE = 384
WIDE = 2 * QF


def packed(lead, base, place):
    parts, spans = list(lead), []
    for n in range(3):
        for k in (0, 1):
            parts.append((base + k * FF + n * TILE, QF, TILE, place + (2 * n + k) * TILE, 2 + n))
    parts.append((base + 2 * FF, QF, QF, place + WIDE, 5))
    for g in range(6):
        mine = [p for p in parts if p[4] == g]
        spans.append((mine[0][3], sum(p[2] for p in mine)))
    return tuple(parts), tuple(spans)


CONV_PARTS, CONV_SPANS = packed(
    ((0, QD, QD, 0, 0), (D, QD, QD, QD, 0), (2 * D, QD, QD, 2 * QD, 0), (3 * D, QD, QD, 3 * QD, 1)), 4 * D, 4 * QD
)
KQ = KVW // 4
ATTN_PARTS, ATTN_SPANS = packed(
    ((0, QD, QD, 0, 0), (D, KQ, KQ, QD, 0), (D + KVW, KQ, KQ, QD + KQ, 0), (2 * D, QD, QD, 2 * QD, 1)), 3 * D, 3 * QD
)


def nn(a, b):
    return jnp.dot(a, b, preferred_element_type=F32)


def nt(a, b):
    return lax.dot_general(a, b, (((1,), (1,)), ((), ())), preferred_element_type=F32)


def tn(a, b):
    return lax.dot_general(a, b, (((0,), (0,)), ((), ())), preferred_element_type=F32)


def rms_scale(v):
    return lax.rsqrt(jnp.mean(v * v, axis=-1, keepdims=True) + norm_eps)


class Place:
    def __init__(self, O):
        self.O = O
        self.x, self.z = lax.axis_index("dp"), lax.axis_index("z")
        self.y, self.c = lax.axis_index("y"), lax.axis_index("c")
        self.r = self.x * 2 + self.y

    def at(self, dx=0, dz=0, dy=0, dc=0):
        out = {}
        if not (isinstance(dx, int) and dx == 0):
            out["dp"] = lax.rem(self.x + dx, 2)
        if not (isinstance(dz, int) and dz == 0):
            out["z"] = lax.rem(self.z + dz, self.O)
        if not (isinstance(dy, int) and dy == 0):
            out["y"] = lax.rem(self.y + dy, 2)
        if not (isinstance(dc, int) and dc == 0):
            out["c"] = lax.rem(self.c + dc, 2)
        return out

    def block(self, dx, dy):
        return lax.rem(self.x + dx, 2) * 2 + lax.rem(self.y + dy, 2)


def greet(here):
    O = here.O
    barrier = pltpu.get_barrier_semaphore()

    def hello(**k):
        pl.semaphore_signal(barrier, inc=1, device_id=here.at(**k), device_id_type=MESH)

    hello(dx=1, dy=1)
    hello(dx=1)
    hello(dy=1)
    hello(dc=1)
    hello(dz=1, dc=1)
    hello(dz=O - 1, dc=1)

    def along(dz, carry):
        for dy in (0, 1):
            hello(dz=dz, dy=dy)
        return carry

    lax.fori_loop(1, O, along, 0)
    pl.semaphore_wait(barrier, 6 + 2 * (O - 1))


def remote(src, dst, ss, rs, dev):
    return pltpu.make_async_remote_copy(
        src_ref=src, dst_ref=dst, send_sem=ss, recv_sem=rs, device_id=dev, device_id_type=MESH
    )


HALF = (slice(0, T // 2), slice(T // 2, T))


class Gather:
    def __init__(self, here, H, ss, rs):
        self.here = here
        r, rx, ry = here.r, here.block(1, 0), here.block(0, 1)
        to_x, to_y = here.at(dx=1), here.at(dy=1)

        def cp(i, block, half, dev):
            rows = pl.ds(half * (T // 2), T // 2)
            return remote(H.at[block, rows], H.at[block, rows], ss.at[i], rs.at[i], dev)

        self.first = (cp(0, r, 0, to_x), cp(1, r, 1, to_y), cp(2, r, 1, to_x), cp(3, r, 0, to_y))
        self.then = (cp(4, rx, 0, to_y), cp(5, ry, 1, to_x))
        for c in self.first:
            c.start()

    def relay(self):
        for i in (0, 1):
            self.first[i].wait_recv()
            self.then[i].start()

    def wait(self):
        for c in self.first[2:]:
            c.wait_recv()
        for c in self.then:
            c.wait_recv()
        for c in self.first + self.then:
            c.wait_send()


class Sums:
    def __init__(self, here, part, S, R, ss, rs):
        self.here, self.part, self.S, self.R, self.ss, self.rs = here, part, S, R, ss, rs

    def cp(self, n, i):
        h = self.here
        dev = h.at(dx=1) if i % 2 == 0 else h.at(dy=1)
        return remote(self.S.at[n, i], self.R.at[n, i], self.ss.at[n, i], self.rs.at[n, i], dev)

    def put(self, n, i, block, half):
        self.S[n, i] = self.part[n, block, HALF[half], :].astype(BF)
        self.cp(n, i).start()

    def begin(self, tile_fn):
        h = self.here
        rx, ry, rd = h.block(1, 0), h.block(0, 1), h.block(1, 1)
        for n in (0, 1):
            self.part[n] = tile_fn(n).reshape(4, T, D // 2)
            self.put(n, 0, rd, 0)
            self.put(n, 1, rd, 1)
            self.put(n, 2, rx, 0)
            self.put(n, 3, ry, 1)

    def relay(self):
        h = self.here
        rx, ry = h.block(1, 0), h.block(0, 1)
        for n in (0, 1):
            for i, block, half in ((0, ry, 0), (1, rx, 1)):
                self.cp(n, i).wait_recv()
                at = 5 - i
                both = self.part[n, block, HALF[half], :] + self.R[n, i].astype(F32)
                self.S[n, at] = both.astype(BF)
                self.cp(n, at).start()

    def wait(self):
        out = []
        for n in (0, 1):
            for i in (2, 3, 4, 5):
                self.cp(n, i).wait_recv()
            for i in range(6):
                self.cp(n, i).wait_send()
            mine = self.part[n, self.here.r]
            R = self.R
            low = mine[HALF[0]] + R[n, 2].astype(F32) + R[n, 5].astype(F32)
            high = mine[HALF[1]] + R[n, 4].astype(F32) + R[n, 3].astype(F32)
            out.append(jnp.concatenate([low, high], axis=0))
        return jnp.concatenate(out, axis=1)


def wait_all(copies):
    for cp in copies:
        cp.wait()


class Weights:
    def __init__(self, here, hbm, W, parts, spans, ls, ys, yr, zs, zr, cs, cr):
        self.here, self.hbm, self.W = here, hbm, W
        self.parts, self.spans = parts, spans
        self.ls, self.ys, self.yr, self.zs, self.zr, self.cs, self.cr = ls, ys, yr, zs, zr, cs, cr
        self.relayed = here.O == 4
        self.passed = set()

    def source(self, part, dy):
        base, stride, width, _, _ = part
        chip = self.here.x * 2 + lax.rem(self.here.y + dy, 2)
        return self.hbm.at[:, pl.ds(pl.multiple_of(base + chip * stride, 128), width)]

    def target(self, part):
        _, _, width, place, _ = part
        h = self.here
        return self.W.at[h.z * 2 + h.y, h.c, :, pl.ds(place, width)]

    def fetch(self, g):
        h = self.here
        for part in self.parts:
            if part[4] != g:
                continue
            pltpu.make_async_copy(self.source(part, 0), self.target(part), self.ls.at[g]).start()
            remote(self.source(part, 1), self.target(part), self.ys.at[g], self.yr.at[g], h.at(dy=1)).start()

    def shards(self, g, first, count):
        place, width = self.spans[g]
        return self.W.at[pl.ds(first, count), self.here.c, :, pl.ds(place, width)]

    def hop(self, g, dz, owner):
        src = self.shards(g, 2 * owner, 2)
        return remote(src, src, self.zs.at[g, dz], self.zr.at[g, dz], self.here.at(dz=dz))

    def near(self, dz):
        z = self.here.z
        return z < 3 if dz == 1 else z > 0 if dz == 3 else z >= 0

    def came(self, dz):
        z = self.here.z
        return z > 0 if dz == 1 else z < 3 if dz == 3 else z >= 0

    def bridge(self, g, owner, dz):
        src = self.shards(g, 2 * owner, 2)
        return remote(src, src, self.zs.at[g, 0], self.zr.at[g, 0], self.here.at(dz=dz))

    def push(self, g):
        h = self.here
        one = self.shards(g, 0, 1)
        pltpu.make_async_copy(one, one, self.ls.at[g]).wait()
        pltpu.make_async_copy(one, one, self.yr.at[g]).wait()
        self.core_copy(g, h.z).start()
        if self.relayed:
            for dz in (2, 1, 3):

                @pl.when(self.near(dz))
                def _():
                    self.hop(g, dz, h.z).start()
        else:

            def along(dz, carry):
                self.hop(g, dz, h.z).start()
                return carry

            lax.fori_loop(1, h.O, along, 0)

    def core_copy(self, g, owner):
        mine = self.shards(g, 2 * owner, 2)
        return remote(mine, mine, self.cs.at[g], self.cr.at[g], self.here.at(dc=1))

    def behind(self, dz):
        return lax.rem(self.here.z + self.here.O - dz, self.here.O)

    def pass_far(self, g):
        h = self.here
        if not self.relayed:
            return
        self.passed.add(g)
        self.hop(g, 2, h.z).wait_recv()

        @pl.when(h.z == 2)
        def _():
            self.bridge(g, 0, 1).start()

        @pl.when(h.z == 1)
        def _():
            self.bridge(g, 3, 3).start()

        self.core_copy(g, self.behind(2)).start()

    def land(self, g):
        h = self.here
        if self.relayed:
            if g not in self.passed:
                self.pass_far(g)
            for dz in (1, 3):

                @pl.when(self.came(dz))
                def _():
                    self.hop(g, dz, h.z).wait_recv()
                    self.core_copy(g, self.behind(dz)).start()

            @pl.when((h.z == 0) | (h.z == 3))
            def _():
                self.bridge(g, 0, 1).wait_recv()
                self.core_copy(g, 3 - h.z).start()

        else:

            def along(dz, carry):
                self.hop(g, dz, h.z).wait_recv()
                self.core_copy(g, self.behind(dz)).start()
                return carry

            lax.fori_loop(1, h.O, along, 0)

    def ready(self, g):
        place, width = self.spans[g]
        half = self.W.at[:, 0, :, pl.ds(place, width)]
        pltpu.make_async_copy(half, half, self.cs.at[g]).wait()
        pltpu.make_async_copy(half, half, self.cr.at[g]).wait()

    def finish(self):
        h = self.here
        for g in range(6):
            one = self.shards(g, 0, 1)
            pltpu.make_async_copy(one, one, self.ys.at[g]).wait()
            if self.relayed:
                for dz in (1, 2, 3):

                    @pl.when(self.near(dz))
                    def _():
                        self.hop(g, dz, h.z).wait_send()

                @pl.when((h.z == 1) | (h.z == 2))
                def _():
                    self.bridge(g, 0, 1).wait_send()

            else:

                def along(dz, carry):
                    self.hop(g, dz, h.z).wait_send()
                    return carry

                lax.fori_loop(1, h.O, along, 0)


def cols(W, place, width):
    v = W[:, :, :, pl.ds(place, width)]
    return v.reshape(D, width)


def rows_of(W, n, place, width):
    h = W.shape[0] // 2
    v = W[n * h : (n + 1) * h, :, :, pl.ds(place, width)]
    return v.reshape(D // 2, width)


def lane_low(shape):
    return lax.broadcasted_iota(jnp.int32, shape, len(shape) - 1) < 64


def lane_first(shape):
    return lax.rem(lax.broadcasted_iota(jnp.int32, shape, len(shape) - 1), 64) < 32


def head_mean(v):
    low = lane_low(v.shape)
    a = jnp.sum(jnp.where(low, v, 0.0), axis=-1, keepdims=True)
    b = jnp.sum(jnp.where(low, 0.0, v), axis=-1, keepdims=True)
    return jnp.where(low, a, b) * (1.0 / HEAD_DIM)


def turn(v):
    return jnp.where(lane_first(v.shape), pltpu.roll(v, 96, 1), pltpu.roll(v, 32, 1))


def to_pairs(left, right):
    low = lane_low(left.shape)
    a = jnp.where(low, left, pltpu.roll(right, 64, 1))
    b = jnp.where(low, pltpu.roll(left, 64, 1), right)
    return a, b


def stacked(a, b):
    low = lane_low(a.shape)
    zero = jnp.zeros_like(a)
    return (jnp.where(low, a, zero), jnp.where(low, b, zero), jnp.where(low, zero, a), jnp.where(low, zero, b))


def ffn_forward_tile(H, W, at, gu, u, n):
    both = nn(H[...].reshape(4 * T, D), cols(W, at + 2 * n * TILE, 2 * TILE))
    gu[:, 2 * n * TILE : 2 * (n + 1) * TILE] = both
    gate, up = both[:, 0:TILE], both[:, TILE:]
    u[:, n * TILE : (n + 1) * TILE] = (gate / (1.0 + jnp.exp(-gate)) * up).astype(BF)


def taps(here, vec):
    at = pl.ds(pl.multiple_of(here.r * QD, 128), QD)
    return tuple(vec[4 + i : 5 + i, at] for i in range(3))


def behind(here, b, mine, from_c, from_z, start):
    z, c, yb = here.z, here.c, b % 2
    if yb:
        before = jnp.where(c == 1, from_c[2 * b : 2 * b + 2], from_c[2 * b - 2 : 2 * b])
    else:
        before = jnp.where(c == 1, from_c[2 * b : 2 * b + 2], from_z[2 * b + 2 : 2 * b + 4])
    row = lax.broadcasted_iota(jnp.int32, (T, QD), 0)
    one = jnp.where(row == 0, before[1:2], pltpu.roll(mine, 1, 0))
    two = jnp.where(row == 0, before[0:1], jnp.where(row == 1, before[1:2], pltpu.roll(mine, 2, 0)))
    t = z * 512 + yb * 256 + c * T + lax.broadcasted_iota(jnp.int32, (T, 1), 0)
    pos = t - start[b * T : (b + 1) * T, 0:1]
    return one, two, jnp.where(pos >= 1, 1.0, 0.0), jnp.where(pos >= 2, 1.0, 0.0)


def meta_copies(here, M1, M2, M3, ms, mr):
    def along(act):
        def body(dz, carry):
            act(remote(M1.at[here.z], M1.at[here.z], ms.at[dz], mr.at[dz], here.at(dz=dz)))
            return carry

        lax.fori_loop(1, here.O, body, 0)

    core = remote(M2.at[here.c], M2.at[here.c], ms.at[0], mr.at[0], here.at(dc=1))
    plane = [
        remote(M3.at[here.r], M3.at[here.r], ms.at[here.O + k], mr.at[here.O + k], here.at(dx=dx, dy=dy))
        for k, (dx, dy) in enumerate(PLANE)
    ]
    return along, core, plane


def write_starts(here, M3, start, start_row):
    counts = jnp.sum(M3[...].reshape(4, 2 * here.O, 8, T), axis=1)
    for b in range(4):
        xb = b // 2
        pair = counts[2 * xb] + counts[2 * xb + 1]
        begin, end = pair[1:2, :], here.O * 4 * T - pair[2:3, :]
        seg = M3[b, here.c, here.z, 0:1, :]
        start_row[:, b * T : (b + 1) * T] = jnp.broadcast_to(
            jnp.where(seg == 0, 0, jnp.where(seg == 1, begin, end)), (8, T)
        )
        ids = jnp.transpose(jnp.broadcast_to(seg.astype(F32), (T, T)))
        first = jnp.where(ids < 0.5, 0, jnp.where(ids < 1.5, begin, end))
        start[b * T : (b + 1) * T, :] = first


def write_rotary(here, start, freq, cosb, sinb):
    for b in range(4):
        rows = slice(b * T, (b + 1) * T)
        t = here.z * 512 + (b % 2) * 256 + here.c * T + lax.broadcasted_iota(jnp.int32, (T, T), 0)
        angle = (t - start[rows, :]).astype(F32) * freq[0:1, :]
        cosb[rows, :] = jnp.cos(angle)
        sinb[rows, :] = jnp.sin(angle) * freq[1:2, :]


def forward_kernel(
    O, tok, cot, vec, hg, meta, freq, wc_hbm, wa_hbm,
    out_tok, x1, x2, x3, h1_out, h2_out, h3_out, h4_out, bcx, cz, gu1_out, gu2_out, qkr, kv_out, oab, lse, wc_out, wa_out, Q,
    tail_c, tail_z, cosb, sinb, start, start_row, cots_out,
    cots, h1, h2, h3, h4, gu1, gu2, kv, wc, wa,
    u, part, S, R, tails, acc, M1, M2, M3,
    ags, agr, rss, rsr, hs, hr, kvs, kvr, wls, wys, wyr, wzs, wzr, wcs, wcr, ms, mr, outs,
):
    here = Place(O)
    x, y, z, c, r = here.x, here.y, here.z, here.c, here.r
    greet(here)
    sets = []
    for i, (hbm, W, parts, spans) in enumerate(
        ((wc_hbm, wc, CONV_PARTS, CONV_SPANS), (wa_hbm, wa, ATTN_PARTS, ATTN_SPANS))
    ):
        sets.append(
            Weights(here, hbm, W, parts, spans, *(a.at[i] for a in (wls, wys, wyr, wzs, wzr, wcs, wcr)))
        )
    queue = [(w, g) for w in sets for g in range(6)]

    def at(point):
        for step in SCHEDULE[point]:
            w, g = queue[int(step[1:])]
            {"f": w.fetch, "p": w.push, "b": w.pass_far, "l": w.land, "r": w.ready}[step[0]](g)

    z_meta, core_meta, plane_meta = meta_copies(here, M1, M2, M3, ms, mr)
    M1[z] = meta[...]
    z_meta(lambda cp: cp.start())
    saving = []

    def save(i, src, dst):
        cp = pltpu.make_async_copy(src, dst, outs.at[i])
        cp.start()
        saving.append(cp)

    at("in")
    x0 = tok[...].astype(F32)
    h1[r] = (x0 * rms_scale(x0) * vec[0:1, :]).astype(BF)
    blocks = Gather(here, h1, ags.at[0], agr.at[0])
    at("start")
    z_meta(lambda cp: cp.wait())
    M2[c] = M1[...]
    core_meta.start()
    at("h1 sent")
    blocks.relay()
    core_meta.wait()
    M3[r] = M2[...]
    for cp in plane_meta:
        cp.start()
    at("h1 relayed")
    blocks.wait()
    wait_all(plane_meta)
    write_starts(here, M3, start, start_row)
    at("h1")

    save(0, h1, h1_out)
    h = h1[...].reshape(4 * T, D)
    for i in range(3):
        bcx[i] = nn(h, cols(wc, i * QD, QD))
    bx = bcx[0] * bcx[2]
    for b in range(4):
        tails[2 * b : 2 * b + 2, :] = bx[b * T + T - 2 : b * T + T, :]
    over = remote(tails, tail_c, hs.at[0], hr.at[0], here.at(dc=1))
    over.start()
    ahead = remote(tails, tail_z, hs.at[1], hr.at[1], here.at(dz=1, dc=1))

    @pl.when((c == 1) & (z < O - 1))
    def _():
        ahead.start()

    over.wait()

    @pl.when((c == 0) & (z > 0))
    def _():
        ahead.wait_recv()

    @pl.when((c == 1) & (z < O - 1))
    def _():
        ahead.wait_send()

    tap0, tap1, tap2 = taps(here, vec)
    from_c, from_z = tail_c[...], jnp.where(z > 0, tail_z[...], 0.0)
    for b in range(4):
        mine = bx[b * T : (b + 1) * T, :]
        one, two, m1, m2 = behind(here, b, mine, from_c, from_z, start)
        cz[b * T : (b + 1) * T, :] = tap0 * mine + tap1 * one * m1 + tap2 * two * m2
    yc = (bcx[1] * cz[...]).astype(BF)
    at("conv")
    sums = Sums(here, part, S, R, rss.at[0], rsr.at[0])
    sums.begin(lambda n: nt(yc, rows_of(wc, n, 3 * QD, QD)))
    at("x1 sent")
    sums.relay()
    at("x1 relayed")
    xn = tok[...].astype(F32) + sums.wait()
    x1[...] = xn
    h2[r] = (xn * rms_scale(xn) * vec[1:2, :]).astype(BF)
    blocks = Gather(here, h2, ags.at[1], agr.at[1])
    at("h2 sent")
    blocks.relay()
    at("h2 relayed")
    write_rotary(here, start, freq, cosb, sinb)
    blocks.wait()
    cots[r] = cot[...]
    cot_blocks = Gather(here, cots, ags.at[4], agr.at[4])
    for n in range(3):
        at("gate1 %d" % n)
        if n == 1:
            cot_blocks.relay()
        ffn_forward_tile(h2, wc, 4 * QD, gu1, u, n)
    cot_blocks.wait()
    save(9, cots, cots_out)
    save(1, h2, h2_out)
    save(2, gu1, gu1_out)
    at("down1")
    sums = Sums(here, part, S, R, rss.at[1], rsr.at[1])
    sums.begin(lambda n: nt(u[...], rows_of(wc, n, 4 * QD + WIDE, QF)))
    save(3, wc, wc_out)
    at("x2 sent")
    sums.relay()
    at("x2 relayed")
    xn = x1[...] + sums.wait()
    x2[...] = xn
    h3[r] = (xn * rms_scale(xn) * vec[2:3, :]).astype(BF)
    blocks = Gather(here, h3, ags.at[2], agr.at[2])
    at("h3 sent")
    blocks.relay()
    at("h3 relayed")
    blocks.wait()
    at("qkv")

    qkv = nn(h3[...].reshape(4 * T, D), cols(wa, 0, 512))
    qa, qb = to_pairs(qkv[:, 0:128], qkv[:, 128:256])
    raw = (qa, qb, qkv[:, 256:384])
    turned = []
    for i in range(3):
        qkr[i] = raw[i]
        gain = hg[0:1, :] if i < 2 else hg[1:2, :]
        w = raw[i] * lax.rsqrt(head_mean(raw[i] * raw[i]) + norm_eps) * gain
        turned.append(w * cosb[...] + turn(w) * sinb[...])
    keys = turned[2].astype(BF)
    values = qkv[:, 384:512].astype(BF)
    for b in range(4):
        kv[z, b, c, :, 0:128] = keys[b * T : (b + 1) * T]
        kv[z, b, c, :, 128:256] = values[b * T : (b + 1) * T]
    mine = kv.at[z, :, c]

    bridged = O == 4

    def far(dz):
        return bridged and dz == 3

    def up(dz):
        return remote(mine, mine, kvs.at[dz], kvr.at[dz], here.at(dz=dz))

    def over_far():
        got = kv.at[0, :, c]
        return remote(got, got, kvs.at[2 * O], kvr.at[2 * O], here.at(dz=1))

    def along_z(act):
        if bridged:
            for dz in range(1, O):
                act(dz)
        else:

            def body(dz, carry):
                act(dz)
                return carry

            lax.fori_loop(1, O, body, 0)

    def send_up(dz):
        if not far(dz):

            @pl.when(z + dz < O)
            def _():
                up(dz).start()

    along_z(send_up)
    at("kv sent")
    pair0 = remote(mine, mine, kvs.at[0], kvr.at[0], here.at(dc=1))
    pair0.start()
    for s in (0, 1):
        low4 = stacked(*(
            (turned[i][s * 256 : (s + 1) * 256] * (HEAD_DIM ** -0.5)).astype(BF) for i in (0, 1)
        ))
        for g in range(4):
            Q[s, g] = low4[g]

    def passed(dz):
        got = kv.at[z - dz, :, c]
        return remote(got, got, kvs.at[O + dz], kvr.at[O + dz], here.at(dc=1))

    if bridged:

        @pl.when(z == 2)
        def _():
            up(2).wait_recv()
            over_far().start()

    def pass_on(dz):
        @pl.when(z - dz >= 0)
        def _():
            if far(dz):
                over_far().wait_recv()
            elif bridged and dz == 2:

                @pl.when(z != 2)
                def _():
                    up(dz).wait_recv()

            else:
                up(dz).wait_recv()
            passed(dz).start()

    along_z(pass_on)
    pair0.wait()

    def pass_wait(dz):
        @pl.when(z - dz >= 0)
        def _():
            passed(dz).wait()

    along_z(pass_wait)
    at("kv")
    save(4, h3, h3_out)
    save(5, kv, kv_out)

    low = lane_low((256, 128))
    for s in (0, 1):
        if s:
            at("half")
        acc[...] = jnp.zeros_like(acc)
        first_of = start[s * 256 : (s + 1) * 256, 0:1]
        row = lax.broadcasted_iota(jnp.int32, (256, 1), 0)
        t = z * 512 + lax.div(row, T) * 256 + c * T + lax.rem(row, T)

        def chunk(j, carry):
            block = kv[lax.div(j, 2), 2 * s + lax.rem(j, 2)].reshape(256, 256)
            k, v = block[:, 0:128], block[:, 128:256]
            one = jnp.ones_like(v)
            v_low = jnp.where(low, v, one)
            v_high = jnp.where(low, one, v)
            at = j * 256 + lax.broadcasted_iota(jnp.int32, (256, 256), 1)
            allowed = (at >= first_of) & (at <= t)
            for g in range(4):
                sc = nt(Q[s, g], k)
                p = jnp.where(allowed, jnp.exp(sc), 0.0).astype(BF)
                acc[g] += nn(p, v_low if g < 2 else v_high)
            return carry

        lax.fori_loop(0, 2 * z + 2, chunk, 0)
        heads = []
        for g in range(4):
            a = acc[g]
            other = pltpu.roll(a, 64, 1)
            heads.append(a / other)
            total = jnp.where(low, other, a) if g < 2 else jnp.where(low, a, other)
            lse[s, :, g * 256 : (g + 1) * 256] = jnp.transpose(jnp.log(total))[0:8, :]
        oab[0, s * 256 : (s + 1) * 256, :] = jnp.where(low, heads[0], heads[2])
        oab[1, s * 256 : (s + 1) * 256, :] = jnp.where(low, heads[1], heads[3])
    at("attended")
    left, right = to_pairs(oab[0], oab[1])
    ao = jnp.concatenate([left, right], axis=1).astype(BF)
    sums = Sums(here, part, S, R, rss.at[2], rsr.at[2])
    sums.begin(lambda n: nt(ao, rows_of(wa, n, 2 * QD, QD)))
    at("x3 sent")
    sums.relay()
    at("x3 relayed")
    xn = x2[...] + sums.wait()
    x3[...] = xn
    h4[r] = (xn * rms_scale(xn) * vec[3:4, :]).astype(BF)
    blocks = Gather(here, h4, ags.at[3], agr.at[3])
    at("h4 sent")
    blocks.relay()
    at("h4 relayed")
    blocks.wait()
    for n in range(3):
        at("gate2 %d" % n)
        ffn_forward_tile(h4, wa, 3 * QD, gu2, u, n)
    save(6, h4, h4_out)
    save(7, gu2, gu2_out)
    at("down2")
    sums = Sums(here, part, S, R, rss.at[3], rsr.at[3])
    sums.begin(lambda n: nt(u[...], rows_of(wa, n, 3 * QD + WIDE, QF)))
    save(8, wa, wa_out)
    at("x4 sent")
    sums.relay()
    at("x4 relayed")
    out_tok[...] = (x3[...] + sums.wait()).astype(BF)

    def up_sent(dz):
        if not far(dz):

            @pl.when(z + dz < O)
            def _():
                up(dz).wait_send()

    along_z(up_sent)
    if bridged:

        @pl.when(z == 2)
        def _():
            over_far().wait_send()

    for w in sets:
        w.finish()
    wait_all(saving)


def any_spec():
    return pl.BlockSpec(memory_space=pl.ANY)


def vmem():
    return pl.BlockSpec(memory_space=pltpu.VMEM)


def forward(O, tok, cot, vec, hg, meta, freq, wc_hbm, wa_hbm):
    sds = jax.ShapeDtypeStruct
    G = 4 * T
    outs = (
        sds((T, D), BF),
        *(sds((T, D), F32) for _ in range(3)),
        *(sds((4, T, D), BF) for _ in range(4)),
        sds((3, G, QD), F32), sds((G, QD), F32),
        sds((G, WIDE), F32), sds((G, WIDE), F32),
        sds((3, G, 128), F32), sds((O, 4, 2, T, 256), BF), sds((2, G, 128), F32), sds((2, 8, 2 * G), F32),
        sds((2 * O, 2, D // (4 * O), CW), BF), sds((2 * O, 2, D // (4 * O), AW), BF),
        sds((2, 4, 256, 128), BF), sds((8, QD), F32), sds((8, QD), F32),
        sds((G, T), F32), sds((G, T), F32), sds((G, T), jnp.int32), sds((8, G), jnp.int32),
        sds((4, T, D), BF),
    )
    big = (len(outs) - 1, 4, 5, 6, 7, 10, 11, 13, 16, 17)
    dma = pltpu.SemaphoreType.DMA
    return pl.pallas_call(
        functools.partial(forward_kernel, O),
        out_shape=outs,
        in_specs=[vmem()] * 6 + [any_spec()] * 2,
        out_specs=tuple(any_spec() if i in big else vmem() for i in range(len(outs))),
        scratch_shapes=[
            *(pltpu.VMEM(outs[i].shape, outs[i].dtype) for i in big),
            pltpu.VMEM((G, QF), BF), pltpu.VMEM((2, 4, T, D // 2), F32),
            pltpu.VMEM((2, 6, T // 2, D // 2), BF), pltpu.VMEM((2, 6, T // 2, D // 2), BF),
            pltpu.VMEM((8, QD), F32), pltpu.VMEM((4, 256, 128), F32),
            pltpu.VMEM((O, 8, T), jnp.int32), pltpu.VMEM((2, O, 8, T), jnp.int32), pltpu.VMEM((4, 2, O, 8, T), jnp.int32),
            dma((5, 6)), dma((5, 6)), dma((4, 2, 6)), dma((4, 2, 6)), dma((2,)), dma((2,)),
            dma((2 * O + 1,)), dma((2 * O + 1,)),
            dma((2, 6)), dma((2, 6)), dma((2, 6)), dma((2, 6, O)), dma((2, 6, O)), dma((2, 6)), dma((2, 6)), dma((O + 3,)), dma((O + 3,)), dma((10,)),
        ],
        compiler_params=pltpu.CompilerParams(
            collective_id=1, has_side_effects=True, vmem_limit_bytes=61 * 2**20
        ),
        cost_estimate=pl.CostEstimate(flops=10**10, bytes_accessed=6 * 10**7, transcendentals=10**7),
        name="forward",
    )(tok, cot, vec, hg, meta, freq, wc_hbm, wa_hbm)


def tables(segments):
    zero = jnp.sum((segments == 0).astype(jnp.int32))
    two = jnp.sum((segments == 2).astype(jnp.int32))
    row = lax.broadcasted_iota(jnp.int32, (8, T), 0)
    meta = jnp.where(row == 0, segments, jnp.where(row == 1, zero, two))
    inverse_freq = rope_base ** (-(jnp.arange(HEAD_DIM // 2, dtype=F32) * 2.0) / HEAD_DIM)
    sign = jnp.where(jnp.arange(T) % HEAD_DIM < HEAD_DIM // 2, -1.0, 1.0).astype(F32)
    return meta, jnp.stack([jnp.concatenate([inverse_freq] * 4), sign])


def rms_back(x, gain, dh):
    r = rms_scale(x)
    inner = jnp.mean(x * gain * dh, axis=-1, keepdims=True)
    return r * gain * dh - x * (r * r * r) * inner, jnp.sum(dh * x * r, axis=0, keepdims=True)


def ffn_back_tile(DF, W, at, gu, dgu, mx, n):
    d = nn(DF[...].reshape(4 * T, D), cols(W, at + WIDE + n * TILE, TILE))
    two = slice(2 * n * TILE, (2 * n + 1) * TILE), slice((2 * n + 1) * TILE, 2 * (n + 1) * TILE)
    gate, up = gu[:, two[0]], gu[:, two[1]]
    sig = 1.0 / (1.0 + jnp.exp(-gate))
    silu = gate * sig
    dgu[:, two[0]] = (d * up * (sig * (1.0 + gate * (1.0 - sig)))).astype(BF)
    dgu[:, two[1]] = (d * silu).astype(BF)
    mx[:, n * TILE : (n + 1) * TILE] = (silu * up).astype(BF)


class Reduce:
    def __init__(self, here, parts, units, half, own, zb, off, zv, za, plane, out, zs, zr, ld, ps, pr):
        self.here, self.parts, self.units, self.half = here, parts, units, half
        self.own, self.zb, self.off, self.zv, self.za = own, zb, off, zv, za
        self.plane, self.out, self.zs, self.zr, self.ld, self.ps, self.pr = plane, out, zs, zr, ld, ps, pr
        self.few = here.O == 4

    def make(self, u, left, left_other, right, right_other, at):
        h = self.here
        place, width = self.units[u]
        step = TILE if width % TILE == 0 else 256
        rows = self.own.shape[1]

        def body(n, carry):
            o = pl.multiple_of(n * step, 128)
            a = nn(left[:, h.c].reshape(D // 2, 4 * T), right[:, pl.ds(at + o, step)])
            b = nn(left_other[...].reshape(D // 2, 4 * T), right_other[:, pl.ds(at + o, step)])
            self.own[:, :, pl.ds(place + o, step)] = (a + b).astype(BF).reshape(2 * h.O, rows, step)
            return carry

        lax.fori_loop(0, width // step, body, 0)

    def span(self, u):
        place, width = self.units[u]
        return pl.ds(place, width)

    def slot(self, u, dz):
        place, width = self.units[u]
        return self.zb.at[dz, :, :, pl.ds(self.off + place, width)]

    def hop(self, u, dz, plane):
        src = self.own.at[pl.ds(2 * plane, 2), :, self.span(u)]
        return remote(src, self.slot(u, dz), self.zs.at[u, dz], self.zr.at[u, dz], self.here.at(dz=dz))

    def far(self, u):
        h = self.here
        src = self.own.at[pl.ds(2 * (3 - h.z), 2), :, self.span(u)]
        to = h.at(dz=jnp.where(h.z == 0, 1, 3))
        return remote(src, self.slot(u, 0), self.zs.at[u, 0], self.zr.at[u, 0], to)

    def ends(self):
        return (self.here.z == 0) | (self.here.z == 3)

    def middle(self):
        return (self.here.z == 1) | (self.here.z == 2)

    def send(self, u):
        h = self.here
        if not self.few:

            def along(dz, carry):
                self.hop(u, dz, lax.rem(h.z + dz, h.O)).start()
                return carry

            lax.fori_loop(1, h.O, along, 0)
            return

        @pl.when(self.ends())
        def _():
            self.far(u).start()
            self.hop(u, 2, lax.rem(h.z + 2, 4)).start()

        @pl.when(h.z < 3)
        def _():
            self.hop(u, 1, h.z + 1).start()

        @pl.when(h.z > 0)
        def _():
            self.hop(u, 3, h.z - 1).start()

    def load(self, u, dz):
        _, width = self.units[u]
        return pltpu.make_async_copy(self.slot(u, dz), self.zv.at[dz, :, :, pl.ds(0, width)], self.ld.at[dz])

    def relay(self, u):
        if not self.few:
            return
        h = self.here
        _, width = self.units[u]

        @pl.when(self.middle())
        def _():
            self.far(u).wait_recv()
            self.load(u, 0).start()
            self.load(u, 0).wait()
            rows = pl.ds(2 * jnp.where(h.z == 1, 3, 0), 2)
            both = self.own[rows, :, self.span(u)].astype(F32) + self.zv[0, :, :, 0:width].astype(F32)
            self.own[rows, :, self.span(u)] = both.astype(BF)
            self.hop(u, 2, jnp.where(h.z == 1, 3, 0)).start()

    def total(self, u):
        h = self.here
        _, width = self.units[u]
        za = self.za.at[:, :, pl.ds(0, width)]
        za[...] = self.own[pl.ds(2 * h.z, 2), :, self.span(u)].astype(F32)

        def add(dz):
            za[...] += self.zv[dz, :, :, 0:width].astype(F32)

        if self.few:
            came = ((1, h.z > 0), (3, h.z < 3))
            self.hop(u, 2, 0).wait_recv()
            self.load(u, 2).start()
            for dz, there in came:

                @pl.when(there)
                def _():
                    self.hop(u, dz, 0).wait_recv()
                    self.load(u, dz).start()

            self.load(u, 2).wait()
            add(2)
            for dz, there in came:

                @pl.when(there)
                def _():
                    self.load(u, dz).wait()
                    add(dz)

        else:

            def along(dz, carry):
                self.hop(u, dz, 0).wait_recv()
                self.load(u, dz).start()
                self.load(u, dz).wait()
                add(dz)
                return carry

            lax.fori_loop(1, h.O, along, 0)
        self.plane[:, :, self.span(u)] = za[...].astype(BF)
        self.each(u, lambda cp: cp.start(), True)

    def pieces(self, u):
        r, half = self.here.r, self.half
        begin, size = self.units[u]
        out = []
        for base, stride, width, place, _ in self.parts:
            if not begin <= place < begin + size:
                continue
            first = half - base
            if base + 3 * stride + width <= half:
                out.append((place, width, 0, base + r * stride))
            elif first <= 0:
                out.append((place, width, 1, base + r * stride - half))
            else:
                assert base + stride >= half
                cut = min(first, width)
                out.append((place, cut, jnp.where(r == 0, 0, 1), jnp.where(r == 0, base, base + r * stride - half)))
                if cut < width:
                    out.append((place + cut, width - cut, 1, base + r * stride + cut - half))
        return out

    def each(self, u, act, local):
        h = self.here
        for place, width, owner, at in self.pieces(u):
            dx = lax.rem(owner + h.x, 2)
            dst = self.out.at[:, pl.ds(pl.multiple_of(at, 128), width)]
            for dy in (1, 0):
                src = self.plane.at[lax.rem(h.y + dy, 2), :, pl.ds(place, width)]
                cp = remote(src, dst, self.ps.at[u], self.pr, h.at(dx=dx, dy=dy))
                if dy:
                    act(cp)
                    continue

                @pl.when(dx != 0)
                def _():
                    act(cp)

                if local:

                    @pl.when(dx == 0)
                    def _():
                        pltpu.make_async_copy(src, dst, self.pr).start()

    def sent(self):
        h = self.here
        for u in range(len(self.units)):
            if not self.few:

                def along(dz, carry):
                    self.hop(u, dz, 0).wait_send()
                    return carry

                lax.fori_loop(1, h.O, along, 0)
                continue

            @pl.when(self.ends())
            def _():
                self.far(u).wait_send()

            self.hop(u, 2, 0).wait_send()

            @pl.when(h.z < 3)
            def _():
                self.hop(u, 1, 0).wait_send()

            @pl.when(h.z > 0)
            def _():
                self.hop(u, 3, 0).wait_send()

    def finish(self):
        for u in range(len(self.units)):
            self.each(u, lambda cp: cp.wait_send(), False)
        pltpu.make_async_copy(self.out, self.out, self.pr).wait()


class Slots:
    def __init__(self, ref, room, sem):
        self.ref, self.room, self.sem = ref, room, sem

    def read(self, i, s):
        if self.room is None:
            return self.ref[i, 2 * s : 2 * s + 2]
        cp = pltpu.make_async_copy(self.ref.at[i, pl.ds(2 * s, 2)], self.room, self.sem)
        cp.start()
        cp.wait()
        return self.room[...]


ATTN_UNITS = ((768 + WIDE, QF), (768, QF), (768 + QF, QF), (512, 256), (0, 512))
CONV_UNITS = ((1024 + WIDE, QF), (1024, QF), (1024 + QF, QF), (768, 256), (0, 768))


class Renew:
    def __init__(self, here, g, w, m, v, out, f32_room, bf_room, new, ls, ss, rs):
        self.here, self.g, self.state, self.out = here, g, (w, m, v), out
        self.f32_room, self.bf_room, self.new = f32_room, bf_room, new
        self.ls, self.ss, self.rs = ls, ss, rs
        self.flying = []

    def loads(self, k, at, width):
        rows = self.g.shape[0]
        slot = k % 2
        cols = pl.ds(at, width)
        out = [
            pltpu.make_async_copy(
                a.at[:, cols], self.f32_room.at[pl.ds((3 * slot + i) * rows, rows), pl.ds(0, width)], self.ls.at[slot, i]
            )
            for i, a in enumerate(self.state)
        ]
        out.append(
            pltpu.make_async_copy(
                self.g.at[:, cols], self.bf_room.at[pl.ds(slot * rows, rows), pl.ds(0, width)], self.ls.at[slot, 3]
            )
        )
        return out

    def run(self, spans):
        rows = self.g.shape[0]
        x = self.here.x
        half = self.g.shape[1]
        for cp in self.loads(0, *spans[0][1:]):
            cp.start()
        for k, (n, at, width) in enumerate(spans):
            if k + 1 < len(spans):
                for cp in self.loads(k + 1, *spans[k + 1][1:]):
                    cp.start()
            wait_all(self.loads(k, at, width))
            slot = k % 2
            w, m, v = (self.f32_room[(3 * slot + i) * rows : (3 * slot + i + 1) * rows, 0:width] for i in range(3))
            g = self.bf_room[slot * rows : (slot + 1) * rows, 0:width].astype(F32)
            new, _, _ = adam_update(w, m, v, g, STEP)
            place = self.new.at[n, 0, :, pl.ds(0, width)]
            place[...] = new.astype(BF)
            to = self.out.at[:, pl.ds(pl.multiple_of(x * half + at, 128), width)]
            self.flying.append(pltpu.make_async_copy(place, to, self.ls.at[2 + n, 0]))
            self.flying.append(remote(place, to, self.ss.at[n], self.rs.at[n], self.here.at(dx=1)))
            self.flying[-2].start()
            self.flying[-1].start()


def backward_kernel(
    O, cot, tok, vec, hg, x1, x2, x3, h1, h2, h3, h4, bcx, cz, gu1, gu2, qkr, kv, oab, lse, wc, wa, Q, tail_c, tail_z,
    cosb, sinb, start, start_row, cots,
    w_attn, m_attn, v_attn,
    dtok, total, ga, gc, new_attn, zb, dkc, dkz,
    W, gu, DG, HH, dgu, mx, sm, LT, other_lt, other_mx, other_sm, other_gu, own_a, *rest,
):
    few = O == 4
    own_c, rest = (rest[0], rest[1:]) if few else (own_a, rest)
    (zv, za, plane_a, plane_c, part, S, R, dO, delta, dq, dqab, dkv, dkk, heads, head_c, head_z, dprev, vg, v0, v1, v2,
     room, ags, agr, rss, rsr, hs, hr, kvs, kvr, wls, gls, hls, xs, xr, zs, zr, ld, ps, pr, vs, vr, rl, rls, rss2, rrs) = rest
    here = Place(O)
    x, y, z, c, r = here.x, here.y, here.z, here.c, here.r
    core_keys = Slots(dkc, None if few else room, rl)
    z_keys = Slots(dkz, None if few else room, rl)
    A = Reduce(here, ATTN_PARTS, ATTN_UNITS, (3 * D + 3 * FF) // 2, own_a, zb, 0, zv, za, plane_a, ga,
               zs.at[0], zr.at[0], ld, ps.at[0], pr.at[0])
    C = Reduce(here, CONV_PARTS, CONV_UNITS, (4 * D + 3 * FF) // 2, own_c, zb, AW, zv, za, plane_c, gc,
               zs.at[1], zr.at[1], ld, ps.at[1], pr.at[1])
    loads = [pltpu.make_async_copy(h, HH, hls.at[i]) for i, h in enumerate((h4, h3, h2, h1))]
    load_w = pltpu.make_async_copy(wa, W.at[:, :, :, pl.ds(0, AW)], wls.at[0])
    load_g = pltpu.make_async_copy(gu2, gu, gls.at[0])
    load_kv = pltpu.make_async_copy(kv, dkv, gls.at[2])
    load_d = pltpu.make_async_copy(cots, DG.at[0], gls.at[3])
    for cp in (load_d, load_w, load_g, loads[0], load_kv):
        cp.start()
    greet(here)
    vg[...] = jnp.zeros_like(vg)

    done = []

    def at(point):
        for step in REDUCTIONS[point]:
            red = A if step[1] == "a" else C
            {"s": red.send, "r": red.relay, "t": red.total}[step[0]](int(step[2]))

    def flat(H):
        return H[...].reshape(4 * T, D)

    def swap(i, src, dst):
        cp = remote(src, dst, xs.at[i], xr.at[i], here.at(dc=1))
        cp.start()
        return cp

    def turned(e, H):
        if done:
            done.pop().wait_send()
        LT[...] = jnp.transpose(flat(H)).reshape(LT.shape)
        cp = swap(e, LT.at[:, 1 - c], other_lt.at[e % 4])
        done.append(cp)
        return cp

    def turned_saved(i, e):
        loads[i].wait()
        cp = turned(e, HH)
        if i < 3:
            loads[i + 1].start()
        return cp

    def ffn_back(i, e, DF, base, x_in, gain_row, red, dy, name):
        lt = turned(e, DF)
        for n in range(3):
            ffn_back_tile(DF, W, base, gu, dgu, mx, n)
        mixed = swap(8 + e, mx, other_mx)
        grads = swap(9 + e, dgu, other_gu)
        sums = Sums(here, part, S, R, rss.at[i], rsr.at[i])
        sums.begin(lambda n: nt(dgu[...], rows_of(W, n, base, WIDE)))
        lt.wait_recv()
        mixed.wait()
        at(name + " down")
        if i and not few:
            A.sent()
        red.make(0, LT, other_lt.at[e % 4], mx, other_mx, 0)
        red.send(0)
        sums.relay()
        dx, dgain = rms_back(x_in[...], vec[gain_row : gain_row + 1, :], sums.wait())
        vg[gain_row : gain_row + 1, :] = dgain
        dprev[...] = dy + dx
        H2 = DG.at[(i + 1) % 2]
        H2[r] = dprev[...].astype(BF)
        blocks = Gather(here, H2, ags.at[i + 1], agr.at[i + 1])
        lt = turned_saved(i, e + 1)
        blocks.relay()
        lt.wait_recv()
        grads.wait()
        red.make(1, LT, other_lt.at[(e + 1) % 4], dgu, other_gu, 0)
        at(name + " wide")
        red.make(2, LT, other_lt.at[(e + 1) % 4], dgu, other_gu, QF)
        blocks.wait()
        at(name + " end")

    DF = DG.at[0]
    load_d.wait()
    load_w.wait()
    load_g.wait()
    ffn_back(0, 0, DF, 3 * QD, x3, 3, A, cot[...].astype(F32), "ffn2")
    load_g = pltpu.make_async_copy(gu1, gu, gls.at[1])
    load_g.start()

    DA = DG.at[1]
    d_out = nn(flat(DA), cols(W, 2 * QD, QD)).astype(BF).astype(F32)
    left, right = to_pairs(oab[0], oab[1])
    sm[:, 0:QD] = jnp.concatenate([left, right], axis=1).astype(BF)
    attended = swap(10, sm.at[:, 0:QD], other_sm.at[:, 0:QD])
    lt = turned(2, DA)
    da, db = to_pairs(d_out[:, 0:128], d_out[:, 128:256])
    for s in (0, 1):
        rows = slice(s * 256, (s + 1) * 256)
        four = stacked(da[rows], db[rows])
        o_of = (oab[0, rows, :], oab[1, rows, :])
        for g in range(4):
            dO[s, g] = four[g].astype(BF)
            dl = jnp.sum(four[g] * o_of[g % 2], axis=-1, keepdims=True)
            delta[s, :, g * 256 : (g + 1) * 256] = jnp.transpose(jnp.broadcast_to(dl, (256, 128)))[0:8, :]
    load_kv.wait()
    low = lane_low((256, 128))

    def pair_keys(s):
        two = pl.ds(2 * s, 2)
        return remote(dkv.at[:, two, 1 - c], dkc.at[:, two], kvs.at[s, 0], kvr.at[s, 0], here.at(dc=1))

    def down(s, d, owner):
        two = pl.ds(2 * s, 2)
        return remote(dkv.at[owner, two, c], dkz.at[z, two], kvs.at[s, d], kvr.at[s, d], here.at(dz=O - d))

    def send_keys(s):
        two = pl.ds(2 * s, 2)
        pair_keys(s).wait()

        def send_down(zz, carry):
            dkv[zz, two, c] = (dkv[zz, two, c].astype(F32) + core_keys.read(zz, s).astype(F32)).astype(BF)
            down(s, z - zz, zz).start()
            return carry

        lax.fori_loop(0, z, send_down, 0)
        dkk[s * 256 : (s + 1) * 256, :] = (
            dkv[z, two, c].astype(F32) + core_keys.read(z, s).astype(F32)
        ).reshape(256, 256)

    for s in (0, 1):
        at("attention %d" % s)
        dq[...] = jnp.zeros_like(dq)
        first_of = start_row[0:1, s * 256 : (s + 1) * 256]
        col = lax.broadcasted_iota(jnp.int32, (1, 256), 1)
        t = z * 512 + lax.div(col, T) * 256 + c * T + lax.rem(col, T)

        def chunk(j, carry):
            block = dkv[lax.div(j, 2), 2 * s + lax.rem(j, 2)].reshape(256, 256)
            k, v = block[:, 0:128], block[:, 128:256]
            key = j * 256 + lax.broadcasted_iota(jnp.int32, (256, 256), 0)
            allowed = (key >= first_of) & (key <= t)
            dk = jnp.zeros((256, 128), F32)
            dv = jnp.zeros((256, 128), F32)
            for g in range(4):
                span = slice(g * 256, (g + 1) * 256)
                p = jnp.where(allowed, jnp.exp(nt(k, Q[s, g]) - lse[s, 0:1, span]), 0.0)
                ds = (p * (nt(v, dO[s, g]) - delta[s, 0:1, span])).astype(BF)
                dv = dv + nn(p.astype(BF), dO[s, g])
                dk = dk + nn(ds, Q[s, g])
                dq[g] += tn(ds, k)
            dkv[lax.div(j, 2), 2 * s + lax.rem(j, 2)] = (
                jnp.concatenate([dk, dv], axis=1).astype(BF).reshape(2, T, 256)
            )
            return carry

        if s:
            lax.fori_loop(0, z + 1, chunk, 0)
            send_keys(0)
            lax.fori_loop(z + 1, 2 * z + 2, chunk, 0)
        else:
            lax.fori_loop(0, 2 * z + 2, chunk, 0)
        pair_keys(s).start()
        rows = slice(s * 256, (s + 1) * 256)
        dqab[0, rows, :] = jnp.where(low, dq[0], dq[2]) * (HEAD_DIM ** -0.5)
        dqab[1, rows, :] = jnp.where(low, dq[1], dq[3]) * (HEAD_DIM ** -0.5)
    lt.wait_recv()
    attended.wait()
    A.make(3, LT, other_lt.at[2], sm, other_sm, 0)
    send_keys(1)
    at("keys sent")

    def take(d, carry):
        @pl.when(z + d < O)
        def _():
            for s in (0, 1):
                down(s, d, z).wait_recv()
                dkk[s * 256 : (s + 1) * 256, :] += z_keys.read(z + d, s).astype(F32).reshape(256, 256)

        return carry

    lax.fori_loop(1, O, take, 0)
    at("keys")

    for i in range(3):
        up = dqab[i] if i < 2 else dkk[:, 0:128]
        raw = qkr[i]
        gain = hg[0:1, :] if i < 2 else hg[1:2, :]
        dw = up * cosb[...] + turn(up * sinb[...])
        rr = lax.rsqrt(head_mean(raw * raw) + norm_eps)
        dgain = jnp.sum(dw * raw * rr, axis=0, keepdims=True)
        row = 8 if i < 2 else 9
        vg[row : row + 1, 0:128] += dgain
        draw = rr * gain * dw - raw * (rr * rr * rr) * head_mean(raw * gain * dw)
        if i < 2:
            dqab[i] = draw
        else:
            sm[:, 512:640] = draw.astype(BF)
    left, right = to_pairs(dqab[0], dqab[1])
    sm[:, 256:384] = left.astype(BF)
    sm[:, 384:512] = right.astype(BF)
    sm[:, 640:768] = dkk[:, 128:256].astype(BF)
    grads = swap(11, sm.at[:, 256:768], other_sm.at[:, 256:768])
    sums = Sums(here, part, S, R, rss.at[1], rsr.at[1])
    sums.begin(lambda n: nt(sm[:, 256:768], rows_of(W, n, 0, 512)))
    load_w = pltpu.make_async_copy(wc, W, wls.at[1])
    load_w.start()
    lt = turned_saved(1, 3)
    sums.relay()
    lt.wait_recv()
    grads.wait()
    A.make(4, LT, other_lt.at[3], sm, other_sm, 256)
    at("qkv")
    dx, dgain = rms_back(x2[...], vec[2:3, :], sums.wait())
    vg[2:3, :] = dgain
    dprev[...] += dx
    D2 = DG.at[0]
    D2[r] = dprev[...].astype(BF)
    blocks = Gather(here, D2, ags.at[2], agr.at[2])
    blocks.relay()
    at("d2 relayed")
    load_w.wait()
    load_g.wait()
    blocks.wait()
    ffn_back(2, 4, D2, 4 * QD, x1, 1, C, dprev[...], "ffn1")

    DD = DG.at[1]
    tap0, tap1, tap2 = taps(here, vec)
    from_c, from_z = tail_c[...], jnp.where(z > 0, tail_z[...], 0.0)
    dyc = nn(flat(DD), cols(W, 3 * QD, QD))
    sm[:, 0:QD] = (bcx[1] * cz[...]).astype(BF)
    mixed = swap(14, sm.at[:, 0:QD], other_sm.at[:, 0:QD])
    sm[:, 2 * QD : 3 * QD] = (dyc * cz[...]).astype(BF)
    dzs = dyc * bcx[1]
    bx = bcx[0] * bcx[2]
    row = lax.broadcasted_iota(jnp.int32, (T, QD), 0)
    g0, g1, g2 = (jnp.zeros((1, QD), F32) for _ in range(3))
    for b in range(4):
        mine = bx[b * T : (b + 1) * T, :]
        dzb = dzs[b * T : (b + 1) * T, :]
        one, two, m1, m2 = behind(here, b, mine, from_c, from_z, start)
        g0 = g0 + jnp.sum(dzb * mine, axis=0, keepdims=True)
        g1 = g1 + jnp.sum(dzb * one * m1, axis=0, keepdims=True)
        g2 = g2 + jnp.sum(dzb * two * m2, axis=0, keepdims=True)
        b1 = tap1 * dzb * m1
        b2 = tap2 * dzb * m2
        heads[2 * b : 2 * b + 1, :] = b2[0:1]
        heads[2 * b + 1 : 2 * b + 2, :] = b1[0:1] + b2[1:2]
        dkk[b * T : (b + 1) * T, :] = (
            tap0 * dzb
            + jnp.where(row < T - 1, pltpu.roll(b1, T - 1, 0), 0.0)
            + jnp.where(row < T - 2, pltpu.roll(b2, T - 2, 0), 0.0)
        )
    over = remote(heads, head_c, hs.at[0], hr.at[0], here.at(dc=1))
    over.start()
    back = remote(heads, head_z, hs.at[1], hr.at[1], here.at(dz=O - 1, dc=1))

    @pl.when((c == 0) & (z > 0))
    def _():
        back.start()

    at("halo")
    lt = turned(6, DD)
    tap_at = pl.ds(pl.multiple_of(r * QD, 128), QD)
    vg[4:5, tap_at] = g0
    vg[5:6, tap_at] = g1
    vg[6:7, tap_at] = g2
    over.wait()

    @pl.when((c == 1) & (z < O - 1))
    def _():
        back.wait_recv()

    to_c, to_z = head_c[...], jnp.where(z < O - 1, head_z[...], 0.0)
    for b in range(4):
        rows = slice(b * T, (b + 1) * T)
        if b % 2:
            e = jnp.where(c == 0, to_c[2 * b : 2 * b + 2], to_z[2 * b - 2 : 2 * b])
        else:
            e = jnp.where(c == 0, to_c[2 * b : 2 * b + 2], to_c[2 * b + 2 : 2 * b + 4])
        dbx = dkk[rows, :] + jnp.where(row == T - 2, e[0:1], jnp.where(row == T - 1, e[1:2], 0.0))
        sm[rows, QD : 2 * QD] = (dbx * bcx[2, rows, :]).astype(BF)
        sm[rows, 3 * QD : 4 * QD] = (dbx * bcx[0, rows, :]).astype(BF)
    grads = swap(15, sm.at[:, QD : 4 * QD], other_sm.at[:, QD : 4 * QD])
    sums = Sums(here, part, S, R, rss.at[3], rsr.at[3])
    sums.begin(lambda n: nt(sm[:, QD : 4 * QD], rows_of(W, n, 0, 768)))
    lt.wait_recv()
    mixed.wait()
    C.make(3, LT, other_lt.at[2], sm, other_sm, 0)
    C.send(3)
    sums.relay()
    lt = turned_saved(3, 7)
    lt.wait_recv()
    grads.wait()
    C.make(4, LT, other_lt.at[3], sm, other_sm, QD)
    C.send(4)
    dx, dgain = rms_back(tok[...].astype(F32), vec[0:1, :], sums.wait())
    vg[0:1, :] = dgain
    dtok[...] = dprev[...] + dx

    v0[c] = vg[...]
    cp = remote(v0.at[c], v0.at[c], vs.at[0], vr.at[0], here.at(dc=1))
    cp.start()
    at("end")
    A.finish()
    renew = Renew(here, ga, w_attn, m_attn, v_attn, new_attn, gu, dgu, W, rls, rss2, rrs)
    step = 2 * AW // 6
    renew.run([(k, k * step, step) for k in range(6)])
    at("end 0")
    cp.wait()
    v1[r] = v0[0] + v0[1]
    copies = [
        remote(v1.at[r], v1.at[r], vs.at[1 + k], vr.at[1 + k], here.at(dx=dx, dy=dy)) for k, (dx, dy) in enumerate(PLANE)
    ]
    for cp in copies:
        cp.start()
    at("end 1")
    wait_all(copies)
    v2[z] = v1[0] + v1[1] + v1[2] + v1[3]

    def start_z(dz, carry):
        remote(v2.at[z], v2.at[z], vs.at[3 + dz], vr.at[3 + dz], here.at(dz=dz)).start()
        return carry

    lax.fori_loop(1, O, start_z, 0)
    at("end 2")

    def wait_z(dz, carry):
        remote(v2.at[z], v2.at[z], vs.at[3 + dz], vr.at[3 + dz], here.at(dz=dz)).wait()
        return carry

    lax.fori_loop(1, O, wait_z, 0)
    t = v2[0]
    for i in range(1, O):
        t = t + v2[i]
    total[...] = t

    def keys_sent(zz, carry):
        for s in (0, 1):
            down(s, z - zz, zz).wait_send()
        return carry

    lax.fori_loop(0, z, keys_sent, 0)
    @pl.when((c == 0) & (z > 0))
    def _():
        back.wait_send()

    for cp in done:
        cp.wait_send()
    if few:
        A.sent()
    C.sent()
    C.finish()
    wait_all(renew.flying)


def backward(O, cot, tok, vec, hg, saved, state):
    (x1, x2, x3, h1, h2, h3, h4, bcx, cz, gu1, gu2, qkr, kv, oab, lse, wc, wa, Q, tail_c, tail_z, cosb, sinb, start,
     start_row, cots) = saved
    sds = jax.ShapeDtypeStruct
    G = 4 * T
    rows = D // (4 * O)
    few = O == 4
    dma = pltpu.SemaphoreType.DMA
    V = pltpu.VMEM
    keys = sds((O, 4, T, 256), BF)
    outs = (
        sds((T, D), F32), sds((16, D), F32), sds((rows, 2 * AW), BF), sds((rows, 2 * CW), BF),
        sds((rows, 4 * AW), BF), sds((O, 2, rows, AW + CW), BF), keys, keys,
    )
    args = (cot, tok, vec, hg, *saved, *state)
    hbm = {id(a) for a in (*state, gu1, gu2, wc, wa, kv, h1, h2, h3, h4, cots)}
    keys_at = vmem() if few else any_spec()
    return pl.pallas_call(
        functools.partial(backward_kernel, O),
        out_shape=outs,
        in_specs=[any_spec() if id(a) in hbm else vmem() for a in args],
        out_specs=(vmem(), vmem(), *[any_spec()] * 4, keys_at, keys_at),
        scratch_shapes=[
            V((2 * O, 2, rows, CW), BF), V((G, WIDE), F32), V((2, 4, T, D), BF), V((4, T, D), BF),
            V((G, WIDE), BF), V((G, QF), BF), V((G, D), BF), V((2 * O, 2, rows, G), BF),
            V((4, 2 * O, rows, G), BF), V((G, QF), BF), V((G, D), BF), V((G, WIDE), BF),
            V((2 * O, rows, CW), BF), *([V((2 * O, rows, CW), BF)] if few else []),
            V((O, 2, rows, QF), BF), V((2, rows, QF), F32), V((2, rows, AW), BF), V((2, rows, CW), BF),
            V((2, 4, T, D // 2), F32), V((2, 6, T // 2, D // 2), BF), V((2, 6, T // 2, D // 2), BF),
            V((2, 4, 256, 128), BF), V((2, 8, 2 * G), F32), V((4, 256, 128), F32), V((2, G, 128), F32),
            V((O, 4, 2, T, 256), BF), V((G, 256), F32),
            V((8, QD), F32), V((8, QD), F32), V((8, QD), F32), V((T, D), F32), V((16, D), F32),
            V((2, 16, D), F32), V((4, 16, D), F32), V((O, 16, D), F32), V((2, T, 256), BF),
            dma((4, 6)), dma((4, 6)), dma((4, 2, 6)), dma((4, 2, 6)), dma((2,)), dma((2,)),
            dma((2, O)), dma((2, O)), dma((2,)), dma((4,)), dma((4,)), dma((16,)), dma((16,)),
            dma((2, 5, O)), dma((2, 5, O)), dma((O,)), dma((2, 5)), dma((2,)), dma((O + 3,)), dma((O + 3,)), dma,
            dma((8, 4)), dma((6,)), dma((6,)),
        ],
        compiler_params=pltpu.CompilerParams(
            collective_id=2, has_side_effects=True, vmem_limit_bytes=int(63.5 * 2**20)
        ),
        cost_estimate=pl.CostEstimate(flops=2 * 10**10, bytes_accessed=10**8, transcendentals=10**7),
        name="backward",
    )(*args)[:5]


REDUCTIONS = {
    "ffn2 down": (),
    "ffn2 wide": ("sa1",),
    "ffn2 end": (),
    "attention 0": (),
    "attention 1": ("ra0",),
    "keys sent": ("ta0", "ra1"),
    "keys": (),
    "qkv": ("sa2", "sa3", "sa4", "ta1"),
    "d2 relayed": ("ra2", "ra3", "ra4"),
    "ffn1 down": ("ta2", "ta3", "ta4"),
    "ffn1 wide": (),
    "ffn1 end": ("rc0",),
    "halo": ("sc1", "sc2"),
    "end": ("rc1", "rc2"),
    "end 0": ("tc0",),
    "end 1": ("tc1",),
    "end 2": ("rc3", "rc4", "tc2", "tc3", "tc4"),
}


def adam_update(master, first_moment, second, gradient, step_value):
    first_new = beta_one * first_moment + (1.0 - beta_one) * gradient
    second_new = beta_two * second + (1.0 - beta_two) * gradient * gradient
    first_hat = first_new / (1.0 - beta_one**step_value)
    second_hat = second_new / (1.0 - beta_two**step_value)
    master_new = master - learn_rate * (
        first_hat / (jnp.sqrt(second_hat) + adam_eps) + decay_rate * master
    )
    return (master_new, first_new, second_new)


def halves_kernel(half, whole, ls, ss, rs):
    x = lax.axis_index("dp")
    other = {"dp": 1 - x}
    barrier = pltpu.get_barrier_semaphore()
    pl.semaphore_signal(barrier, inc=1, device_id=other, device_id_type=MESH)
    pl.semaphore_wait(barrier, 1)
    width = half.shape[1]
    at = whole.at[:, pl.ds(pl.multiple_of(x * width, 128), width)]
    flying = [remote(half, at, ss, rs, other), pltpu.make_async_copy(half, at, ls)]
    for cp in flying:
        cp.start()
    wait_all(flying)


def halves(half):
    dma = pltpu.SemaphoreType.DMA
    return pl.pallas_call(
        halves_kernel,
        out_shape=jax.ShapeDtypeStruct((half.shape[0], 2 * half.shape[1]), half.dtype),
        in_specs=[any_spec()],
        out_specs=any_spec(),
        scratch_shapes=[dma, dma, dma],
        compiler_params=pltpu.CompilerParams(collective_id=3, has_side_effects=True),
        cost_estimate=pl.CostEstimate(flops=0, bytes_accessed=10**7, transcendentals=0),
        name="halves",
    )(half)


def shards(
    tokens, segments, cotangent, conv_weights, attn_weights, vectors, head_gains,
    master_conv, first_conv, second_conv, master_attn, first_attn, second_attn,
):
    O = lax.axis_size("z")
    hg = jnp.concatenate([head_gains, head_gains], axis=1)
    tok = tokens[0]
    out_tok, *saved = forward(O, tok, cotangent[0], vectors, hg, *tables(segments), conv_weights, attn_weights)
    dtok, total, ga, gc, attn_all = backward(
        O, cotangent[0], tok, vectors, hg, saved, (master_attn, first_attn, second_attn)
    )
    grad_attn, grad_conv = ga.astype(F32), gc.astype(F32)
    grad_vectors = total[0:7]
    grad_gains = total[8:10, 0:64] + total[8:10, 64:128]
    step_value = jnp.float32(STEP)
    new_conv = adam_update(master_conv, first_conv, second_conv, grad_conv, step_value)
    new_attn = adam_update(master_attn, first_attn, second_attn, grad_attn, step_value)
    conv_all = halves(new_conv[0].astype(BF))
    return (
        out_tok[None], dtok[None], grad_conv, grad_attn, grad_vectors, grad_gains, *new_conv, *new_attn,
        conv_all, attn_all,
    )


def solution(mesh):
    outer = mesh.shape["ctx"] // 4
    split = Mesh(mesh.devices.reshape(mesh.shape["dp"], outer, 2, 2), ("dp", "z", "y", "c"))
    ctx = ("z", "y", "c")
    seq, rows, state = P("dp", ctx, None), P(ctx, None), P(ctx, "dp")
    return jax.shard_map(
        shards,
        mesh=split,
        in_specs=(seq, P("dp", ctx), seq, rows, rows, P(), P(), *([state] * 6)),
        out_specs=(seq, seq, state, state, P(), P(), *([state] * 6), rows, rows),
        check_vma=False,
    )
```

```python
import functools
import jax
import jax.numpy as jnp
import numpy as np
from jax import lax
from jax.sharding import Mesh, PartitionSpec as P
import jax.experimental.pallas as pl
import jax.experimental.pallas.tpu as pltpu

D = 1024
FF = 4608
HEADS = 16
KV_HEADS = 8
HEAD_DIM = 64
STEP = 5
KVW = 512
T = 128
QF = FF // 4
QD = D // 4
CW = 4 * QD + 3 * QF
AW = 3 * QD + 3 * QF

norm_eps = 1e-05
rope_base = 1000000.0
learn_rate = 0.01
decay_rate = 0.1
beta_one = 0.9
beta_two = 0.95
adam_eps = 1e-08

MESH = pl.DeviceIdType.MESH

SCHEDULE = {
    "in": ("f0", "f1",),
    "start": ("p0", "p1", "f2",),
    "h1 sent": ("f3", "p2",),
    "h1 relayed": ("f4", "b0", "p3",),
    "h1": ("f5", "l0", "p4", "l1", "r0",),
    "conv": ("r1", "p5",),
    "x1 sent": (),
    "x1 relayed": ("b2", "f6", "f7",),
    "h2 sent": (),
    "h2 relayed": ("b3", "f8",),
    "gate1 0": ("l2", "r2",),
    "gate1 1": ("l3", "r3",),
    "gate1 2": ("l4", "r4",),
    "down1": ("p6", "l5", "p7", "r5", "p8",),
    "x2 sent": (),
    "x2 relayed": ("f9", "b6",),
    "h3 sent": ("p9", "f10", "b7",),
    "h3 relayed": ("f11", "l6", "l7",),
    "qkv": ("r6",),
    "kv sent": ("b8",),
    "kv": ("p10",),
    "half": ("p11", "b9",),
    "attended": ("l8", "r7",),
    "x3 sent": ("b10",),
    "x3 relayed": ("l9",),
    "h4 sent": ("b11",),
    "h4 relayed": (),
    "gate2 0": ("l10", "r8",),
    "gate2 1": ("l11", "r9",),
    "gate2 2": ("r10",),
    "down2": ("r11",),
    "x4 sent": (),
    "x4 relayed": (),
}
BF = jnp.bfloat16
F32 = jnp.float32
PLANE = ((1, 1), (1, 0), (0, 1))

TILE = 384
WIDE = 2 * QF


def packed(lead, base, place):
    parts, spans = list(lead), []
    for n in range(3):
        for k in (0, 1):
            parts.append((base + k * FF + n * TILE, QF, TILE, place + (2 * n + k) * TILE, 2 + n))
    parts.append((base + 2 * FF, QF, QF, place + WIDE, 5))
    for g in range(6):
        mine = [p for p in parts if p[4] == g]
        spans.append((mine[0][3], sum(p[2] for p in mine)))
    return tuple(parts), tuple(spans)


CONV_PARTS, CONV_SPANS = packed(
    ((0, QD, QD, 0, 0), (D, QD, QD, QD, 0), (2 * D, QD, QD, 2 * QD, 0), (3 * D, QD, QD, 3 * QD, 1)), 4 * D, 4 * QD
)
KQ = KVW // 4
ATTN_PARTS, ATTN_SPANS = packed(
    ((0, QD, QD, 0, 0), (D, KQ, KQ, QD, 0), (D + KVW, KQ, KQ, QD + KQ, 0), (2 * D, QD, QD, 2 * QD, 1)), 3 * D, 3 * QD
)


def nn(a, b):
    return jnp.dot(a, b, preferred_element_type=F32)


def nt(a, b):
    return lax.dot_general(a, b, (((1,), (1,)), ((), ())), preferred_element_type=F32)


def tn(a, b):
    return lax.dot_general(a, b, (((0,), (0,)), ((), ())), preferred_element_type=F32)


def rms_scale(v):
    return lax.rsqrt(jnp.mean(v * v, axis=-1, keepdims=True) + norm_eps)


class Place:
    def __init__(self, O):
        self.O = O
        self.x, self.z = lax.axis_index("dp"), lax.axis_index("z")
        self.y, self.c = lax.axis_index("y"), lax.axis_index("c")
        self.r = self.x * 2 + self.y

    def at(self, dx=0, dz=0, dy=0, dc=0):
        out = {}
        if not (isinstance(dx, int) and dx == 0):
            out["dp"] = lax.rem(self.x + dx, 2)
        if not (isinstance(dz, int) and dz == 0):
            out["z"] = lax.rem(self.z + dz, self.O)
        if not (isinstance(dy, int) and dy == 0):
            out["y"] = lax.rem(self.y + dy, 2)
        if not (isinstance(dc, int) and dc == 0):
            out["c"] = lax.rem(self.c + dc, 2)
        return out

    def block(self, dx, dy):
        return lax.rem(self.x + dx, 2) * 2 + lax.rem(self.y + dy, 2)


def greet(here):
    O = here.O
    barrier = pltpu.get_barrier_semaphore()

    def hello(**k):
        pl.semaphore_signal(barrier, inc=1, device_id=here.at(**k), device_id_type=MESH)

    hello(dx=1, dy=1)
    hello(dx=1)
    hello(dy=1)
    hello(dc=1)
    hello(dz=1, dc=1)
    hello(dz=O - 1, dc=1)

    def along(dz, carry):
        for dy in (0, 1):
            hello(dz=dz, dy=dy)
        return carry

    lax.fori_loop(1, O, along, 0)
    pl.semaphore_wait(barrier, 6 + 2 * (O - 1))


def remote(src, dst, ss, rs, dev):
    return pltpu.make_async_remote_copy(
        src_ref=src, dst_ref=dst, send_sem=ss, recv_sem=rs, device_id=dev, device_id_type=MESH
    )


HALF = (slice(0, T // 2), slice(T // 2, T))


class Gather:
    def __init__(self, here, H, ss, rs):
        self.here = here
        r, rx, ry = here.r, here.block(1, 0), here.block(0, 1)
        to_x, to_y = here.at(dx=1), here.at(dy=1)

        def cp(i, block, half, dev):
            rows = pl.ds(half * (T // 2), T // 2)
            return remote(H.at[block, rows], H.at[block, rows], ss.at[i], rs.at[i], dev)

        self.first = (cp(0, r, 0, to_x), cp(1, r, 1, to_y), cp(2, r, 1, to_x), cp(3, r, 0, to_y))
        self.then = (cp(4, rx, 0, to_y), cp(5, ry, 1, to_x))
        for c in self.first:
            c.start()

    def relay(self):
        for i in (0, 1):
            self.first[i].wait_recv()
            self.then[i].start()

    def wait(self):
        for c in self.first[2:]:
            c.wait_recv()
        for c in self.then:
            c.wait_recv()
        for c in self.first + self.then:
            c.wait_send()


class Sums:
    def __init__(self, here, part, S, R, ss, rs):
        self.here, self.part, self.S, self.R, self.ss, self.rs = here, part, S, R, ss, rs

    def cp(self, n, i):
        h = self.here
        dev = h.at(dx=1) if i % 2 == 0 else h.at(dy=1)
        return remote(self.S.at[n, i], self.R.at[n, i], self.ss.at[n, i], self.rs.at[n, i], dev)

    def put(self, n, i, block, half):
        self.S[n, i] = self.part[n, block, HALF[half], :].astype(BF)
        self.cp(n, i).start()

    def begin(self, tile_fn):
        h = self.here
        rx, ry, rd = h.block(1, 0), h.block(0, 1), h.block(1, 1)
        for n in (0, 1):
            self.part[n] = tile_fn(n).reshape(4, T, D // 2)
            self.put(n, 0, rd, 0)
            self.put(n, 1, rd, 1)
            self.put(n, 2, rx, 0)
            self.put(n, 3, ry, 1)

    def relay(self):
        h = self.here
        rx, ry = h.block(1, 0), h.block(0, 1)
        for n in (0, 1):
            for i, block, half in ((0, ry, 0), (1, rx, 1)):
                self.cp(n, i).wait_recv()
                at = 5 - i
                both = self.part[n, block, HALF[half], :] + self.R[n, i].astype(F32)
                self.S[n, at] = both.astype(BF)
                self.cp(n, at).start()

    def wait(self):
        out = []
        for n in (0, 1):
            for i in (2, 3, 4, 5):
                self.cp(n, i).wait_recv()
            for i in range(6):
                self.cp(n, i).wait_send()
            mine = self.part[n, self.here.r]
            R = self.R
            low = mine[HALF[0]] + R[n, 2].astype(F32) + R[n, 5].astype(F32)
            high = mine[HALF[1]] + R[n, 4].astype(F32) + R[n, 3].astype(F32)
            out.append(jnp.concatenate([low, high], axis=0))
        return jnp.concatenate(out, axis=1)


def wait_all(copies):
    for cp in copies:
        cp.wait()


class Weights:
    def __init__(self, here, hbm, W, parts, spans, ls, ys, yr, zs, zr, cs, cr):
        self.here, self.hbm, self.W = here, hbm, W
        self.parts, self.spans = parts, spans
        self.ls, self.ys, self.yr, self.zs, self.zr, self.cs, self.cr = ls, ys, yr, zs, zr, cs, cr
        self.relayed = here.O == 4
        self.passed = set()

    def source(self, part, dy):
        base, stride, width, _, _ = part
        chip = self.here.x * 2 + lax.rem(self.here.y + dy, 2)
        return self.hbm.at[:, pl.ds(pl.multiple_of(base + chip * stride, 128), width)]

    def target(self, part):
        _, _, width, place, _ = part
        h = self.here
        return self.W.at[h.z * 2 + h.y, h.c, :, pl.ds(place, width)]

    def fetch(self, g):
        h = self.here
        for part in self.parts:
            if part[4] != g:
                continue
            pltpu.make_async_copy(self.source(part, 0), self.target(part), self.ls.at[g]).start()
            remote(self.source(part, 1), self.target(part), self.ys.at[g], self.yr.at[g], h.at(dy=1)).start()

    def shards(self, g, first, count):
        place, width = self.spans[g]
        return self.W.at[pl.ds(first, count), self.here.c, :, pl.ds(place, width)]

    def hop(self, g, dz, owner):
        src = self.shards(g, 2 * owner, 2)
        return remote(src, src, self.zs.at[g, dz], self.zr.at[g, dz], self.here.at(dz=dz))

    def near(self, dz):
        z = self.here.z
        return z < 3 if dz == 1 else z > 0 if dz == 3 else z >= 0

    def came(self, dz):
        z = self.here.z
        return z > 0 if dz == 1 else z < 3 if dz == 3 else z >= 0

    def bridge(self, g, owner, dz):
        src = self.shards(g, 2 * owner, 2)
        return remote(src, src, self.zs.at[g, 0], self.zr.at[g, 0], self.here.at(dz=dz))

    def push(self, g):
        h = self.here
        one = self.shards(g, 0, 1)
        pltpu.make_async_copy(one, one, self.ls.at[g]).wait()
        pltpu.make_async_copy(one, one, self.yr.at[g]).wait()
        self.core_copy(g, h.z).start()
        if self.relayed:
            for dz in (2, 1, 3):

                @pl.when(self.near(dz))
                def _():
                    self.hop(g, dz, h.z).start()
        else:

            def along(dz, carry):
                self.hop(g, dz, h.z).start()
                return carry

            lax.fori_loop(1, h.O, along, 0)

    def core_copy(self, g, owner):
        mine = self.shards(g, 2 * owner, 2)
        return remote(mine, mine, self.cs.at[g], self.cr.at[g], self.here.at(dc=1))

    def behind(self, dz):
        return lax.rem(self.here.z + self.here.O - dz, self.here.O)

    def pass_far(self, g):
        h = self.here
        if not self.relayed:
            return
        self.passed.add(g)
        self.hop(g, 2, h.z).wait_recv()

        @pl.when(h.z == 2)
        def _():
            self.bridge(g, 0, 1).start()

        @pl.when(h.z == 1)
        def _():
            self.bridge(g, 3, 3).start()

        self.core_copy(g, self.behind(2)).start()

    def land(self, g):
        h = self.here
        if self.relayed:
            if g not in self.passed:
                self.pass_far(g)
            for dz in (1, 3):

                @pl.when(self.came(dz))
                def _():
                    self.hop(g, dz, h.z).wait_recv()
                    self.core_copy(g, self.behind(dz)).start()

            @pl.when((h.z == 0) | (h.z == 3))
            def _():
                self.bridge(g, 0, 1).wait_recv()
                self.core_copy(g, 3 - h.z).start()

        else:

            def along(dz, carry):
                self.hop(g, dz, h.z).wait_recv()
                self.core_copy(g, self.behind(dz)).start()
                return carry

            lax.fori_loop(1, h.O, along, 0)

    def ready(self, g):
        place, width = self.spans[g]
        half = self.W.at[:, 0, :, pl.ds(place, width)]
        pltpu.make_async_copy(half, half, self.cs.at[g]).wait()
        pltpu.make_async_copy(half, half, self.cr.at[g]).wait()

    def finish(self):
        h = self.here
        for g in range(6):
            one = self.shards(g, 0, 1)
            pltpu.make_async_copy(one, one, self.ys.at[g]).wait()
            if self.relayed:
                for dz in (1, 2, 3):

                    @pl.when(self.near(dz))
                    def _():
                        self.hop(g, dz, h.z).wait_send()

                @pl.when((h.z == 1) | (h.z == 2))
                def _():
                    self.bridge(g, 0, 1).wait_send()

            else:

                def along(dz, carry):
                    self.hop(g, dz, h.z).wait_send()
                    return carry

                lax.fori_loop(1, h.O, along, 0)


def cols(W, place, width):
    v = W[:, :, :, pl.ds(place, width)]
    return v.reshape(D, width)


def rows_of(W, n, place, width):
    h = W.shape[0] // 2
    v = W[n * h : (n + 1) * h, :, :, pl.ds(place, width)]
    return v.reshape(D // 2, width)


def lane_low(shape):
    return lax.broadcasted_iota(jnp.int32, shape, len(shape) - 1) < 64


def lane_first(shape):
    return lax.rem(lax.broadcasted_iota(jnp.int32, shape, len(shape) - 1), 64) < 32


def head_mean(v):
    low = lane_low(v.shape)
    a = jnp.sum(jnp.where(low, v, 0.0), axis=-1, keepdims=True)
    b = jnp.sum(jnp.where(low, 0.0, v), axis=-1, keepdims=True)
    return jnp.where(low, a, b) * (1.0 / HEAD_DIM)


def turn(v):
    return jnp.where(lane_first(v.shape), pltpu.roll(v, 96, 1), pltpu.roll(v, 32, 1))


def to_pairs(left, right):
    low = lane_low(left.shape)
    a = jnp.where(low, left, pltpu.roll(right, 64, 1))
    b = jnp.where(low, pltpu.roll(left, 64, 1), right)
    return a, b


def stacked(a, b):
    low = lane_low(a.shape)
    zero = jnp.zeros_like(a)
    return (jnp.where(low, a, zero), jnp.where(low, b, zero), jnp.where(low, zero, a), jnp.where(low, zero, b))


def ffn_forward_tile(H, W, at, gu, u, n):
    both = nn(H[...].reshape(4 * T, D), cols(W, at + 2 * n * TILE, 2 * TILE))
    gu[:, 2 * n * TILE : 2 * (n + 1) * TILE] = both
    gate, up = both[:, 0:TILE], both[:, TILE:]
    u[:, n * TILE : (n + 1) * TILE] = (gate / (1.0 + jnp.exp(-gate)) * up).astype(BF)


def taps(here, vec):
    at = pl.ds(pl.multiple_of(here.r * QD, 128), QD)
    return tuple(vec[4 + i : 5 + i, at] for i in range(3))


def behind(here, b, mine, from_c, from_z, start):
    z, c, yb = here.z, here.c, b % 2
    if yb:
        before = jnp.where(c == 1, from_c[2 * b : 2 * b + 2], from_c[2 * b - 2 : 2 * b])
    else:
        before = jnp.where(c == 1, from_c[2 * b : 2 * b + 2], from_z[2 * b + 2 : 2 * b + 4])
    row = lax.broadcasted_iota(jnp.int32, (T, QD), 0)
    one = jnp.where(row == 0, before[1:2], pltpu.roll(mine, 1, 0))
    two = jnp.where(row == 0, before[0:1], jnp.where(row == 1, before[1:2], pltpu.roll(mine, 2, 0)))
    t = z * 512 + yb * 256 + c * T + lax.broadcasted_iota(jnp.int32, (T, 1), 0)
    pos = t - start[b * T : (b + 1) * T, 0:1]
    return one, two, jnp.where(pos >= 1, 1.0, 0.0), jnp.where(pos >= 2, 1.0, 0.0)


def meta_copies(here, M1, M2, M3, ms, mr):
    def along(act):
        def body(dz, carry):
            act(remote(M1.at[here.z], M1.at[here.z], ms.at[dz], mr.at[dz], here.at(dz=dz)))
            return carry

        lax.fori_loop(1, here.O, body, 0)

    core = remote(M2.at[here.c], M2.at[here.c], ms.at[0], mr.at[0], here.at(dc=1))
    plane = [
        remote(M3.at[here.r], M3.at[here.r], ms.at[here.O + k], mr.at[here.O + k], here.at(dx=dx, dy=dy))
        for k, (dx, dy) in enumerate(PLANE)
    ]
    return along, core, plane


def write_starts(here, M3, start, start_row):
    counts = jnp.sum(M3[...].reshape(4, 2 * here.O, 8, T), axis=1)
    for b in range(4):
        xb = b // 2
        pair = counts[2 * xb] + counts[2 * xb + 1]
        begin, end = pair[1:2, :], here.O * 4 * T - pair[2:3, :]
        seg = M3[b, here.c, here.z, 0:1, :]
        start_row[:, b * T : (b + 1) * T] = jnp.broadcast_to(
            jnp.where(seg == 0, 0, jnp.where(seg == 1, begin, end)), (8, T)
        )
        ids = jnp.transpose(jnp.broadcast_to(seg.astype(F32), (T, T)))
        first = jnp.where(ids < 0.5, 0, jnp.where(ids < 1.5, begin, end))
        start[b * T : (b + 1) * T, :] = first


def write_rotary(here, start, freq, cosb, sinb):
    for b in range(4):
        rows = slice(b * T, (b + 1) * T)
        t = here.z * 512 + (b % 2) * 256 + here.c * T + lax.broadcasted_iota(jnp.int32, (T, T), 0)
        angle = (t - start[rows, :]).astype(F32) * freq[0:1, :]
        cosb[rows, :] = jnp.cos(angle)
        sinb[rows, :] = jnp.sin(angle) * freq[1:2, :]


def forward_kernel(
    O, tok, cot, vec, head_gains, segments, freq, wc_hbm, wa_hbm,
    out_tok, hg, x1, x2, x3, h1_out, h2_out, h3_out, h4_out, bcx, cz, gu1_out, gu2_out, qkr, kv_out, oab, lse, wc_out, wa_out, Q,
    tail_c, tail_z, cosb, sinb, start, start_row, cots_out,
    cots, h1, h2, h3, h4, gu1, gu2, kv, wc, wa,
    u, part, S, R, tails, acc, M1, M2, M3,
    ags, agr, rss, rsr, hs, hr, kvs, kvr, wls, wys, wyr, wzs, wzr, wcs, wcr, ms, mr, outs,
):
    here = Place(O)
    x, y, z, c, r = here.x, here.y, here.z, here.c, here.r
    greet(here)
    sets = []
    for i, (hbm, W, parts, spans) in enumerate(
        ((wc_hbm, wc, CONV_PARTS, CONV_SPANS), (wa_hbm, wa, ATTN_PARTS, ATTN_SPANS))
    ):
        sets.append(
            Weights(here, hbm, W, parts, spans, *(a.at[i] for a in (wls, wys, wyr, wzs, wzr, wcs, wcr)))
        )
    queue = [(w, g) for w in sets for g in range(6)]

    def at(point):
        for step in SCHEDULE[point]:
            w, g = queue[int(step[1:])]
            {"f": w.fetch, "p": w.push, "b": w.pass_far, "l": w.land, "r": w.ready}[step[0]](g)

    z_meta, core_meta, plane_meta = meta_copies(here, M1, M2, M3, ms, mr)
    row = lax.broadcasted_iota(jnp.int32, (8, T), 0)
    seg = segments[...]
    count = [jnp.sum(jnp.where(seg == i, 1.0, 0.0), axis=1, keepdims=True).astype(jnp.int32) for i in (0, 2)]
    M1[z] = jnp.where(row == 0, seg, jnp.where(row == 1, count[0], count[1]))
    hg[:, 0:64] = head_gains[...]
    hg[:, 64:128] = head_gains[...]
    z_meta(lambda cp: cp.start())
    saving = []

    def save(i, src, dst):
        cp = pltpu.make_async_copy(src, dst, outs.at[i])
        cp.start()
        saving.append(cp)

    at("in")
    x0 = tok[...].astype(F32)
    h1[r] = (x0 * rms_scale(x0) * vec[0:1, :]).astype(BF)
    blocks = Gather(here, h1, ags.at[0], agr.at[0])
    at("start")
    z_meta(lambda cp: cp.wait())
    M2[c] = M1[...]
    core_meta.start()
    at("h1 sent")
    blocks.relay()
    core_meta.wait()
    M3[r] = M2[...]
    for cp in plane_meta:
        cp.start()
    at("h1 relayed")
    blocks.wait()
    wait_all(plane_meta)
    write_starts(here, M3, start, start_row)
    at("h1")

    save(0, h1, h1_out)
    h = h1[...].reshape(4 * T, D)
    for i in range(3):
        bcx[i] = nn(h, cols(wc, i * QD, QD))
    bx = bcx[0] * bcx[2]
    for b in range(4):
        tails[2 * b : 2 * b + 2, :] = bx[b * T + T - 2 : b * T + T, :]
    over = remote(tails, tail_c, hs.at[0], hr.at[0], here.at(dc=1))
    over.start()
    ahead = remote(tails, tail_z, hs.at[1], hr.at[1], here.at(dz=1, dc=1))

    @pl.when((c == 1) & (z < O - 1))
    def _():
        ahead.start()

    over.wait()

    @pl.when((c == 0) & (z > 0))
    def _():
        ahead.wait_recv()

    @pl.when((c == 1) & (z < O - 1))
    def _():
        ahead.wait_send()

    tap0, tap1, tap2 = taps(here, vec)
    from_c, from_z = tail_c[...], jnp.where(z > 0, tail_z[...], 0.0)
    for b in range(4):
        mine = bx[b * T : (b + 1) * T, :]
        one, two, m1, m2 = behind(here, b, mine, from_c, from_z, start)
        cz[b * T : (b + 1) * T, :] = tap0 * mine + tap1 * one * m1 + tap2 * two * m2
    yc = (bcx[1] * cz[...]).astype(BF)
    at("conv")
    sums = Sums(here, part, S, R, rss.at[0], rsr.at[0])
    sums.begin(lambda n: nt(yc, rows_of(wc, n, 3 * QD, QD)))
    at("x1 sent")
    sums.relay()
    at("x1 relayed")
    xn = tok[...].astype(F32) + sums.wait()
    x1[...] = xn
    h2[r] = (xn * rms_scale(xn) * vec[1:2, :]).astype(BF)
    blocks = Gather(here, h2, ags.at[1], agr.at[1])
    at("h2 sent")
    blocks.relay()
    at("h2 relayed")
    write_rotary(here, start, freq, cosb, sinb)
    blocks.wait()
    cots[r] = cot[...]
    cot_blocks = Gather(here, cots, ags.at[4], agr.at[4])
    for n in range(3):
        at("gate1 %d" % n)
        if n == 1:
            cot_blocks.relay()
        ffn_forward_tile(h2, wc, 4 * QD, gu1, u, n)
    cot_blocks.wait()
    save(9, cots, cots_out)
    save(1, h2, h2_out)
    save(2, gu1, gu1_out)
    at("down1")
    sums = Sums(here, part, S, R, rss.at[1], rsr.at[1])
    sums.begin(lambda n: nt(u[...], rows_of(wc, n, 4 * QD + WIDE, QF)))
    save(3, wc, wc_out)
    at("x2 sent")
    sums.relay()
    at("x2 relayed")
    xn = x1[...] + sums.wait()
    x2[...] = xn
    h3[r] = (xn * rms_scale(xn) * vec[2:3, :]).astype(BF)
    blocks = Gather(here, h3, ags.at[2], agr.at[2])
    at("h3 sent")
    blocks.relay()
    at("h3 relayed")
    blocks.wait()
    at("qkv")

    qkv = nn(h3[...].reshape(4 * T, D), cols(wa, 0, 512))
    qa, qb = to_pairs(qkv[:, 0:128], qkv[:, 128:256])
    raw = (qa, qb, qkv[:, 256:384])
    turned = []
    for i in range(3):
        qkr[i] = raw[i]
        gain = hg[0:1, :] if i < 2 else hg[1:2, :]
        w = raw[i] * lax.rsqrt(head_mean(raw[i] * raw[i]) + norm_eps) * gain
        turned.append(w * cosb[...] + turn(w) * sinb[...])
    keys = turned[2].astype(BF)
    values = qkv[:, 384:512].astype(BF)
    for b in range(4):
        kv[z, b, c, :, 0:128] = keys[b * T : (b + 1) * T]
        kv[z, b, c, :, 128:256] = values[b * T : (b + 1) * T]
    mine = kv.at[z, :, c]

    bridged = O == 4

    def far(dz):
        return bridged and dz == 3

    def up(dz):
        return remote(mine, mine, kvs.at[dz], kvr.at[dz], here.at(dz=dz))

    def over_far():
        got = kv.at[0, :, c]
        return remote(got, got, kvs.at[2 * O], kvr.at[2 * O], here.at(dz=1))

    def along_z(act):
        if bridged:
            for dz in range(1, O):
                act(dz)
        else:

            def body(dz, carry):
                act(dz)
                return carry

            lax.fori_loop(1, O, body, 0)

    def send_up(dz):
        if not far(dz):

            @pl.when(z + dz < O)
            def _():
                up(dz).start()

    along_z(send_up)
    at("kv sent")
    pair0 = remote(mine, mine, kvs.at[0], kvr.at[0], here.at(dc=1))
    pair0.start()
    for s in (0, 1):
        low4 = stacked(*(
            (turned[i][s * 256 : (s + 1) * 256] * (HEAD_DIM ** -0.5)).astype(BF) for i in (0, 1)
        ))
        for g in range(4):
            Q[s, g] = low4[g]

    def passed(dz):
        got = kv.at[z - dz, :, c]
        return remote(got, got, kvs.at[O + dz], kvr.at[O + dz], here.at(dc=1))

    if bridged:

        @pl.when(z == 2)
        def _():
            up(2).wait_recv()
            over_far().start()

    def pass_on(dz):
        @pl.when(z - dz >= 0)
        def _():
            if far(dz):
                over_far().wait_recv()
            elif bridged and dz == 2:

                @pl.when(z != 2)
                def _():
                    up(dz).wait_recv()

            else:
                up(dz).wait_recv()
            passed(dz).start()

    along_z(pass_on)
    pair0.wait()

    def pass_wait(dz):
        @pl.when(z - dz >= 0)
        def _():
            passed(dz).wait()

    along_z(pass_wait)
    at("kv")
    save(4, h3, h3_out)
    save(5, kv, kv_out)

    low = lane_low((256, 128))
    for s in (0, 1):
        if s:
            at("half")
        acc[...] = jnp.zeros_like(acc)
        first_of = start[s * 256 : (s + 1) * 256, 0:1]
        row = lax.broadcasted_iota(jnp.int32, (256, 1), 0)
        t = z * 512 + lax.div(row, T) * 256 + c * T + lax.rem(row, T)

        def chunk(j, carry):
            block = kv[lax.div(j, 2), 2 * s + lax.rem(j, 2)].reshape(256, 256)
            k, v = block[:, 0:128], block[:, 128:256]
            one = jnp.ones_like(v)
            v_low = jnp.where(low, v, one)
            v_high = jnp.where(low, one, v)
            at = j * 256 + lax.broadcasted_iota(jnp.int32, (256, 256), 1)
            allowed = (at >= first_of) & (at <= t)
            for g in range(4):
                sc = nt(Q[s, g], k)
                p = jnp.where(allowed, jnp.exp(sc), 0.0).astype(BF)
                acc[g] += nn(p, v_low if g < 2 else v_high)
            return carry

        lax.fori_loop(0, 2 * z + 2, chunk, 0)
        heads = []
        for g in range(4):
            a = acc[g]
            other = pltpu.roll(a, 64, 1)
            heads.append(a / other)
            total = jnp.where(low, other, a) if g < 2 else jnp.where(low, a, other)
            lse[s, :, g * 256 : (g + 1) * 256] = jnp.transpose(jnp.log(total))[0:8, :]
        oab[0, s * 256 : (s + 1) * 256, :] = jnp.where(low, heads[0], heads[2])
        oab[1, s * 256 : (s + 1) * 256, :] = jnp.where(low, heads[1], heads[3])
    at("attended")
    left, right = to_pairs(oab[0], oab[1])
    ao = jnp.concatenate([left, right], axis=1).astype(BF)
    sums = Sums(here, part, S, R, rss.at[2], rsr.at[2])
    sums.begin(lambda n: nt(ao, rows_of(wa, n, 2 * QD, QD)))
    at("x3 sent")
    sums.relay()
    at("x3 relayed")
    xn = x2[...] + sums.wait()
    x3[...] = xn
    h4[r] = (xn * rms_scale(xn) * vec[3:4, :]).astype(BF)
    blocks = Gather(here, h4, ags.at[3], agr.at[3])
    at("h4 sent")
    blocks.relay()
    at("h4 relayed")
    blocks.wait()
    for n in range(3):
        at("gate2 %d" % n)
        ffn_forward_tile(h4, wa, 3 * QD, gu2, u, n)
    save(6, h4, h4_out)
    save(7, gu2, gu2_out)
    at("down2")
    sums = Sums(here, part, S, R, rss.at[3], rsr.at[3])
    sums.begin(lambda n: nt(u[...], rows_of(wa, n, 3 * QD + WIDE, QF)))
    save(8, wa, wa_out)
    at("x4 sent")
    sums.relay()
    at("x4 relayed")
    out_tok[...] = (x3[...] + sums.wait()).astype(BF)

    def up_sent(dz):
        if not far(dz):

            @pl.when(z + dz < O)
            def _():
                up(dz).wait_send()

    along_z(up_sent)
    if bridged:

        @pl.when(z == 2)
        def _():
            over_far().wait_send()

    for w in sets:
        w.finish()
    wait_all(saving)


def any_spec():
    return pl.BlockSpec(memory_space=pl.ANY)


def vmem():
    return pl.BlockSpec(memory_space=pltpu.VMEM)


def forward(O, tok, cot, vec, hg, segments, freq, wc_hbm, wa_hbm):
    sds = jax.ShapeDtypeStruct
    G = 4 * T
    outs = (
        sds((T, D), BF), sds((2, 128), F32),
        *(sds((T, D), F32) for _ in range(3)),
        *(sds((4, T, D), BF) for _ in range(4)),
        sds((3, G, QD), F32), sds((G, QD), F32),
        sds((G, WIDE), F32), sds((G, WIDE), F32),
        sds((3, G, 128), F32), sds((O, 4, 2, T, 256), BF), sds((2, G, 128), F32), sds((2, 8, 2 * G), F32),
        sds((2 * O, 2, D // (4 * O), CW), BF), sds((2 * O, 2, D // (4 * O), AW), BF),
        sds((2, 4, 256, 128), BF), sds((8, QD), F32), sds((8, QD), F32),
        sds((G, T), F32), sds((G, T), F32), sds((G, T), jnp.int32), sds((8, G), jnp.int32),
        sds((4, T, D), BF),
    )
    big = (len(outs) - 1, 5, 6, 7, 8, 11, 12, 14, 17, 18)
    dma = pltpu.SemaphoreType.DMA
    return pl.pallas_call(
        functools.partial(forward_kernel, O),
        out_shape=outs,
        in_specs=[vmem()] * 6 + [any_spec()] * 2,
        out_specs=tuple(any_spec() if i in big else vmem() for i in range(len(outs))),
        scratch_shapes=[
            *(pltpu.VMEM(outs[i].shape, outs[i].dtype) for i in big),
            pltpu.VMEM((G, QF), BF), pltpu.VMEM((2, 4, T, D // 2), F32),
            pltpu.VMEM((2, 6, T // 2, D // 2), BF), pltpu.VMEM((2, 6, T // 2, D // 2), BF),
            pltpu.VMEM((8, QD), F32), pltpu.VMEM((4, 256, 128), F32),
            pltpu.VMEM((O, 8, T), jnp.int32), pltpu.VMEM((2, O, 8, T), jnp.int32), pltpu.VMEM((4, 2, O, 8, T), jnp.int32),
            dma((5, 6)), dma((5, 6)), dma((4, 2, 6)), dma((4, 2, 6)), dma((2,)), dma((2,)),
            dma((2 * O + 1,)), dma((2 * O + 1,)),
            dma((2, 6)), dma((2, 6)), dma((2, 6)), dma((2, 6, O)), dma((2, 6, O)), dma((2, 6)), dma((2, 6)), dma((O + 3,)), dma((O + 3,)), dma((10,)),
        ],
        compiler_params=pltpu.CompilerParams(
            collective_id=1, has_side_effects=True, vmem_limit_bytes=61 * 2**20
        ),
        cost_estimate=pl.CostEstimate(flops=10**10, bytes_accessed=6 * 10**7, transcendentals=10**7),
        name="forward",
    )(tok, cot, vec, hg, segments, freq, wc_hbm, wa_hbm)


def rotary_rows():
    lane = np.arange(T)
    freq = rope_base ** (-((lane % (HEAD_DIM // 2)).astype(np.float32) * 2.0) / HEAD_DIM)
    sign = np.where(lane % HEAD_DIM < HEAD_DIM // 2, -1.0, 1.0)
    return jnp.asarray(np.stack([freq, sign]), F32)


def rms_back(x, gain, dh):
    r = rms_scale(x)
    inner = jnp.mean(x * gain * dh, axis=-1, keepdims=True)
    return r * gain * dh - x * (r * r * r) * inner, jnp.sum(dh * x * r, axis=0, keepdims=True)


def ffn_back_tile(DF, W, at, gu, dgu, mx, n):
    d = nn(DF[...].reshape(4 * T, D), cols(W, at + WIDE + n * TILE, TILE))
    two = slice(2 * n * TILE, (2 * n + 1) * TILE), slice((2 * n + 1) * TILE, 2 * (n + 1) * TILE)
    gate, up = gu[:, two[0]], gu[:, two[1]]
    sig = 1.0 / (1.0 + jnp.exp(-gate))
    silu = gate * sig
    dgu[:, two[0]] = (d * up * (sig * (1.0 + gate * (1.0 - sig)))).astype(BF)
    dgu[:, two[1]] = (d * silu).astype(BF)
    mx[:, n * TILE : (n + 1) * TILE] = (silu * up).astype(BF)


class Reduce:
    def __init__(self, here, parts, units, half, own, zb, off, zv, za, plane, out, zs, zr, ld, ps, pr):
        self.here, self.parts, self.units, self.half = here, parts, units, half
        self.own, self.zb, self.off, self.zv, self.za = own, zb, off, zv, za
        self.plane, self.out, self.zs, self.zr, self.ld, self.ps, self.pr = plane, out, zs, zr, ld, ps, pr
        self.few = here.O == 4

    def make(self, u, left, left_other, right, right_other, at):
        h = self.here
        place, width = self.units[u]
        step = TILE if width % TILE == 0 else 256
        rows = self.own.shape[1]

        def body(n, carry):
            o = pl.multiple_of(n * step, 128)
            a = nn(left[:, h.c].reshape(D // 2, 4 * T), right[:, pl.ds(at + o, step)])
            b = nn(left_other[...].reshape(D // 2, 4 * T), right_other[:, pl.ds(at + o, step)])
            self.own[:, :, pl.ds(place + o, step)] = (a + b).astype(BF).reshape(2 * h.O, rows, step)
            return carry

        lax.fori_loop(0, width // step, body, 0)

    def span(self, u):
        place, width = self.units[u]
        return pl.ds(place, width)

    def slot(self, u, dz):
        place, width = self.units[u]
        return self.zb.at[dz, :, :, pl.ds(self.off + place, width)]

    def hop(self, u, dz, plane):
        src = self.own.at[pl.ds(2 * plane, 2), :, self.span(u)]
        return remote(src, self.slot(u, dz), self.zs.at[u, dz], self.zr.at[u, dz], self.here.at(dz=dz))

    def far(self, u):
        h = self.here
        src = self.own.at[pl.ds(2 * (3 - h.z), 2), :, self.span(u)]
        to = h.at(dz=jnp.where(h.z == 0, 1, 3))
        return remote(src, self.slot(u, 0), self.zs.at[u, 0], self.zr.at[u, 0], to)

    def ends(self):
        return (self.here.z == 0) | (self.here.z == 3)

    def middle(self):
        return (self.here.z == 1) | (self.here.z == 2)

    def send(self, u):
        h = self.here
        if not self.few:

            def along(dz, carry):
                self.hop(u, dz, lax.rem(h.z + dz, h.O)).start()
                return carry

            lax.fori_loop(1, h.O, along, 0)
            return

        @pl.when(self.ends())
        def _():
            self.far(u).start()
            self.hop(u, 2, lax.rem(h.z + 2, 4)).start()

        @pl.when(h.z < 3)
        def _():
            self.hop(u, 1, h.z + 1).start()

        @pl.when(h.z > 0)
        def _():
            self.hop(u, 3, h.z - 1).start()

    def load(self, u, dz):
        _, width = self.units[u]
        return pltpu.make_async_copy(self.slot(u, dz), self.zv.at[dz, :, :, pl.ds(0, width)], self.ld.at[dz])

    def relay(self, u):
        if not self.few:
            return
        h = self.here
        _, width = self.units[u]

        @pl.when(self.middle())
        def _():
            self.far(u).wait_recv()
            self.load(u, 0).start()
            self.load(u, 0).wait()
            rows = pl.ds(2 * jnp.where(h.z == 1, 3, 0), 2)
            both = self.own[rows, :, self.span(u)].astype(F32) + self.zv[0, :, :, 0:width].astype(F32)
            self.own[rows, :, self.span(u)] = both.astype(BF)
            self.hop(u, 2, jnp.where(h.z == 1, 3, 0)).start()

    def total(self, u):
        h = self.here
        _, width = self.units[u]
        za = self.za.at[:, :, pl.ds(0, width)]
        za[...] = self.own[pl.ds(2 * h.z, 2), :, self.span(u)].astype(F32)

        def add(dz):
            za[...] += self.zv[dz, :, :, 0:width].astype(F32)

        if self.few:
            came = ((1, h.z > 0), (3, h.z < 3))
            self.hop(u, 2, 0).wait_recv()
            self.load(u, 2).start()
            for dz, there in came:

                @pl.when(there)
                def _():
                    self.hop(u, dz, 0).wait_recv()
                    self.load(u, dz).start()

            self.load(u, 2).wait()
            add(2)
            for dz, there in came:

                @pl.when(there)
                def _():
                    self.load(u, dz).wait()
                    add(dz)

        else:

            def along(dz, carry):
                self.hop(u, dz, 0).wait_recv()
                self.load(u, dz).start()
                self.load(u, dz).wait()
                add(dz)
                return carry

            lax.fori_loop(1, h.O, along, 0)
        self.plane[:, :, self.span(u)] = za[...].astype(BF)
        self.each(u, lambda cp: cp.start(), True)

    def pieces(self, u):
        r, half = self.here.r, self.half
        begin, size = self.units[u]
        out = []
        for base, stride, width, place, _ in self.parts:
            if not begin <= place < begin + size:
                continue
            first = half - base
            if base + 3 * stride + width <= half:
                out.append((place, width, 0, base + r * stride))
            elif first <= 0:
                out.append((place, width, 1, base + r * stride - half))
            else:
                assert base + stride >= half
                cut = min(first, width)
                out.append((place, cut, jnp.where(r == 0, 0, 1), jnp.where(r == 0, base, base + r * stride - half)))
                if cut < width:
                    out.append((place + cut, width - cut, 1, base + r * stride + cut - half))
        return out

    def each(self, u, act, local):
        h = self.here
        for place, width, owner, at in self.pieces(u):
            dx = lax.rem(owner + h.x, 2)
            dst = self.out.at[:, pl.ds(pl.multiple_of(at, 128), width)]
            for dy in (1, 0):
                src = self.plane.at[lax.rem(h.y + dy, 2), :, pl.ds(place, width)]
                cp = remote(src, dst, self.ps.at[u], self.pr.at[u], h.at(dx=dx, dy=dy))
                if dy:
                    act(cp)
                    continue

                @pl.when(dx != 0)
                def _():
                    act(cp)

                if local:

                    @pl.when(dx == 0)
                    def _():
                        pltpu.make_async_copy(src, dst, self.pr.at[u]).start()

    def sent(self):
        h = self.here
        for u in range(len(self.units)):
            if not self.few:

                def along(dz, carry):
                    self.hop(u, dz, 0).wait_send()
                    return carry

                lax.fori_loop(1, h.O, along, 0)
                continue

            @pl.when(self.ends())
            def _():
                self.far(u).wait_send()

            self.hop(u, 2, 0).wait_send()

            @pl.when(h.z < 3)
            def _():
                self.hop(u, 1, 0).wait_send()

            @pl.when(h.z > 0)
            def _():
                self.hop(u, 3, 0).wait_send()

    def spans_at(self, u, x):
        half = self.half
        begin, size = self.units[u]
        out = []
        for base, stride, width, place, _ in self.parts:
            if begin <= place < begin + size:
                for chip in range(4):
                    lo = max(base + chip * stride, x * half)
                    hi = min(base + chip * stride + width, (x + 1) * half)
                    if lo < hi:
                        out.append((lo - x * half, hi - lo))
        joined = []
        for at, width in sorted(out):
            if joined and joined[-1][0] + joined[-1][1] == at:
                joined[-1] = (joined[-1][0], joined[-1][1] + width)
            else:
                joined.append((at, width))
        return joined

    def owned(self, u):
        for x in (0, 1):
            width = sum(w for _, w in self.spans_at(u, x))
            if width:

                @pl.when(self.here.x == x)
                def _():
                    all_of = self.out.at[:, pl.ds(0, width)]
                    pltpu.make_async_copy(all_of, all_of, self.pr.at[u]).wait()

    def finish(self):
        for u in range(len(self.units)):
            self.each(u, lambda cp: cp.wait_send(), False)


class Slots:
    def __init__(self, ref, room, sem):
        self.ref, self.room, self.sem = ref, room, sem

    def read(self, i, s):
        if self.room is None:
            return self.ref[i, 2 * s : 2 * s + 2]
        cp = pltpu.make_async_copy(self.ref.at[i, pl.ds(2 * s, 2)], self.room, self.sem)
        cp.start()
        cp.wait()
        return self.room[...]


ATTN_UNITS = ((768 + WIDE, QF), (768, QF), (768 + QF, QF), (512, 256), (0, 512))
CONV_UNITS = ((1024 + WIDE, QF), (1024, QF), (1024 + QF, QF), (768, 256), (0, 768))


class Renew:
    def __init__(self, here, g, w, m, v, out, f32_room, bf_room, new, ls, ss, rs):
        self.here, self.g, self.state, self.out = here, g, (w, m, v), out
        self.f32_room, self.bf_room, self.new = f32_room, bf_room, new
        self.ls, self.ss, self.rs = ls, ss, rs
        self.next = [0, 0]
        self.flying = ([], [])

    def loads(self, k, at, width):
        rows = self.g.shape[0]
        slot = k % 2
        cols = pl.ds(at, width)
        out = [
            pltpu.make_async_copy(
                a.at[:, cols], self.f32_room.at[pl.ds((3 * slot + i) * rows, rows), pl.ds(0, width)], self.ls.at[slot, i]
            )
            for i, a in enumerate(self.state)
        ]
        out.append(
            pltpu.make_async_copy(
                self.g.at[:, cols], self.bf_room.at[pl.ds(slot * rows, rows), pl.ds(0, width)], self.ls.at[slot, 3]
            )
        )
        return out

    def steps(self, x, spans):
        out = []
        for at, width in spans:
            parts = -(-width // WIDE)
            while width % (128 * parts):
                parts += 1
            for p in range(parts):
                n = self.next[x]
                self.next[x] += 1
                w, to = width // parts, at + p * (width // parts)
                place = self.new(n, w)
                dst = self.out.at[:, pl.ds(x * self.g.shape[1] + to, w)]
                out.append((
                    to, w, place, pltpu.make_async_copy(place, dst, self.ls.at[2 + n, 0]),
                    remote(place, dst, self.ss.at[n], self.rs.at[n], self.here.at(dx=1)),
                ))
        self.flying[x].extend(out)
        return out

    def run(self, x, spans):
        steps = self.steps(x, spans)
        if not steps:
            return

        @pl.when(self.here.x == x)
        def _():
            rows = self.g.shape[0]
            for cp in self.loads(0, *steps[0][:2]):
                cp.start()
            for k, (at, width, place, keep, give) in enumerate(steps):
                if k + 1 < len(steps):
                    for cp in self.loads(k + 1, *steps[k + 1][:2]):
                        cp.start()
                wait_all(self.loads(k, at, width))
                slot = k % 2
                w, m, v = (self.f32_room[(3 * slot + i) * rows : (3 * slot + i + 1) * rows, 0:width] for i in range(3))
                g = self.bf_room[slot * rows : (slot + 1) * rows, 0:width].astype(F32)
                place[...] = adam_update(w, m, v, g, STEP)[0].astype(BF)
                keep.start()
                give.start()

    def wait(self):
        for x in (0, 1):

            @pl.when(self.here.x == x)
            def _():
                for _, _, _, keep, give in self.flying[x]:
                    keep.wait()
                    give.wait_send()
                for _, _, _, _, give in self.flying[1 - x]:
                    give.wait_recv()


def backward_kernel(
    O, cot, tok, vec, hg, x1, x2, x3, h1, h2, h3, h4, bcx, cz, gu1, gu2, qkr, kv, oab, lse, wc, wa, Q, tail_c, tail_z,
    cosb, sinb, start, start_row, cots,
    w_attn, m_attn, v_attn, w_conv, m_conv, v_conv,
    dtok, vectors, gains, ga, gc, new_attn, new_conv, zb, dkc, dkz,
    W, gu, DG, HH, dgu, mx, sm, LT, other_lt, other_mx, other_sm, other_gu, own_a, *rest,
):
    few = O == 4
    own_c, rest = (rest[0], rest[1:]) if few else (own_a, rest)
    (zv, za, plane_a, plane_c, part, S, R, dO, delta, dq, dqab, dkv, dkk, heads, head_c, head_z, dprev, vg, v0, v1, v2,
     room, ags, agr, rss, rsr, hs, hr, kvs, kvr, wls, gls, hls, xs, xr, zs, zr, ld, ps, pr, vs, vr, rl, rls, rss2, rrs) = rest
    here = Place(O)
    x, y, z, c, r = here.x, here.y, here.z, here.c, here.r
    core_keys = Slots(dkc, None if few else room, rl)
    z_keys = Slots(dkz, None if few else room, rl)
    A = Reduce(here, ATTN_PARTS, ATTN_UNITS, (3 * D + 3 * FF) // 2, own_a, zb, 0, zv, za, plane_a, ga,
               zs.at[0], zr.at[0], ld, ps.at[0], pr.at[0])
    C = Reduce(here, CONV_PARTS, CONV_UNITS, (4 * D + 3 * FF) // 2, own_c, zb, AW, zv, za, plane_c, gc,
               zs.at[1], zr.at[1], ld, ps.at[1], pr.at[1])
    loads = [pltpu.make_async_copy(h, HH, hls.at[i]) for i, h in enumerate((h4, h3, h2, h1))]
    load_w = pltpu.make_async_copy(wa, W.at[:, :, :, pl.ds(0, AW)], wls.at[0])
    load_g = pltpu.make_async_copy(gu2, gu, gls.at[0])
    load_kv = pltpu.make_async_copy(kv, dkv, gls.at[2])
    load_d = pltpu.make_async_copy(cots, DG.at[0], gls.at[3])
    for cp in (load_d, load_w, load_g, loads[0], load_kv):
        cp.start()
    greet(here)
    vg[...] = jnp.zeros_like(vg)

    done = []

    def move(kind, red, u):
        if kind == "n":
            red.owned(u)
            for x_ in (0, 1):
                renew_c.run(x_, red.spans_at(u, x_))
        else:
            {"s": red.send, "r": red.relay, "t": red.total}[kind](u)

    def at(point):
        for step in REDUCTIONS[point]:
            move(step[0], A if step[1] == "a" else C, int(step[2]))

    def flat(H):
        return H[...].reshape(4 * T, D)

    def swap(i, src, dst):
        cp = remote(src, dst, xs.at[i], xr.at[i], here.at(dc=1))
        cp.start()
        return cp

    def turned(e, H):
        if done:
            done.pop().wait_send()
        LT[...] = jnp.transpose(flat(H)).reshape(LT.shape)
        cp = swap(e, LT.at[:, 1 - c], other_lt.at[e % 4])
        done.append(cp)
        return cp

    def turned_saved(i, e):
        loads[i].wait()
        cp = turned(e, HH)
        if i < 3:
            loads[i + 1].start()
        return cp

    def ffn_back(i, e, DF, base, x_in, gain_row, red, dy, name):
        lt = turned(e, DF)
        for n in range(3):
            ffn_back_tile(DF, W, base, gu, dgu, mx, n)
        mixed = swap(8 + e, mx, other_mx)
        grads = swap(9 + e, dgu, other_gu)
        sums = Sums(here, part, S, R, rss.at[i], rsr.at[i])
        sums.begin(lambda n: nt(dgu[...], rows_of(W, n, base, WIDE)))
        lt.wait_recv()
        mixed.wait()
        at(name + " down")
        if i and not few:
            A.sent()
        red.make(0, LT, other_lt.at[e % 4], mx, other_mx, 0)
        red.send(0)
        sums.relay()
        dx, dgain = rms_back(x_in[...], vec[gain_row : gain_row + 1, :], sums.wait())
        vg[gain_row : gain_row + 1, :] = dgain
        dprev[...] = dy + dx
        H2 = DG.at[(i + 1) % 2]
        H2[r] = dprev[...].astype(BF)
        blocks = Gather(here, H2, ags.at[i + 1], agr.at[i + 1])
        lt = turned_saved(i, e + 1)
        blocks.relay()
        lt.wait_recv()
        grads.wait()
        red.make(1, LT, other_lt.at[(e + 1) % 4], dgu, other_gu, 0)
        at(name + " wide")
        red.make(2, LT, other_lt.at[(e + 1) % 4], dgu, other_gu, QF)
        blocks.wait()
        at(name + " end")

    DF = DG.at[0]
    load_d.wait()
    load_w.wait()
    load_g.wait()
    ffn_back(0, 0, DF, 3 * QD, x3, 3, A, cot[...].astype(F32), "ffn2")
    load_g = pltpu.make_async_copy(gu1, gu, gls.at[1])
    load_g.start()

    DA = DG.at[1]
    d_out = nn(flat(DA), cols(W, 2 * QD, QD)).astype(BF).astype(F32)
    left, right = to_pairs(oab[0], oab[1])
    sm[:, 0:QD] = jnp.concatenate([left, right], axis=1).astype(BF)
    attended = swap(10, sm.at[:, 0:QD], other_sm.at[:, 0:QD])
    lt = turned(2, DA)
    da, db = to_pairs(d_out[:, 0:128], d_out[:, 128:256])
    for s in (0, 1):
        rows = slice(s * 256, (s + 1) * 256)
        four = stacked(da[rows], db[rows])
        o_of = (oab[0, rows, :], oab[1, rows, :])
        for g in range(4):
            dO[s, g] = four[g].astype(BF)
            dl = jnp.sum(four[g] * o_of[g % 2], axis=-1, keepdims=True)
            delta[s, :, g * 256 : (g + 1) * 256] = jnp.transpose(jnp.broadcast_to(dl, (256, 128)))[0:8, :]
    load_kv.wait()
    low = lane_low((256, 128))

    def pair_keys(s):
        two = pl.ds(2 * s, 2)
        return remote(dkv.at[:, two, 1 - c], dkc.at[:, two], kvs.at[s, 0], kvr.at[s, 0], here.at(dc=1))

    def down(s, d, owner):
        two = pl.ds(2 * s, 2)
        return remote(dkv.at[owner, two, c], dkz.at[z, two], kvs.at[s, d], kvr.at[s, d], here.at(dz=O - d))

    def send_keys(s):
        two = pl.ds(2 * s, 2)
        pair_keys(s).wait()

        def send_down(zz, carry):
            dkv[zz, two, c] = (dkv[zz, two, c].astype(F32) + core_keys.read(zz, s).astype(F32)).astype(BF)
            down(s, z - zz, zz).start()
            return carry

        lax.fori_loop(0, z, send_down, 0)
        dkk[s * 256 : (s + 1) * 256, :] = (
            dkv[z, two, c].astype(F32) + core_keys.read(z, s).astype(F32)
        ).reshape(256, 256)

    for s in (0, 1):
        at("attention %d" % s)
        dq[...] = jnp.zeros_like(dq)
        first_of = start_row[0:1, s * 256 : (s + 1) * 256]
        col = lax.broadcasted_iota(jnp.int32, (1, 256), 1)
        t = z * 512 + lax.div(col, T) * 256 + c * T + lax.rem(col, T)

        def chunk(j, carry):
            block = dkv[lax.div(j, 2), 2 * s + lax.rem(j, 2)].reshape(256, 256)
            k, v = block[:, 0:128], block[:, 128:256]
            key = j * 256 + lax.broadcasted_iota(jnp.int32, (256, 256), 0)
            allowed = (key >= first_of) & (key <= t)
            dk = jnp.zeros((256, 128), F32)
            dv = jnp.zeros((256, 128), F32)
            for g in range(4):
                span = slice(g * 256, (g + 1) * 256)
                p = jnp.where(allowed, jnp.exp(nt(k, Q[s, g]) - lse[s, 0:1, span]), 0.0)
                ds = (p * (nt(v, dO[s, g]) - delta[s, 0:1, span])).astype(BF)
                dv = dv + nn(p.astype(BF), dO[s, g])
                dk = dk + nn(ds, Q[s, g])
                dq[g] += tn(ds, k)
            dkv[lax.div(j, 2), 2 * s + lax.rem(j, 2)] = (
                jnp.concatenate([dk, dv], axis=1).astype(BF).reshape(2, T, 256)
            )
            return carry

        if s:
            lax.fori_loop(0, z + 1, chunk, 0)
            send_keys(0)
            lax.fori_loop(z + 1, 2 * z + 2, chunk, 0)
        else:
            lax.fori_loop(0, 2 * z + 2, chunk, 0)
        pair_keys(s).start()
        rows = slice(s * 256, (s + 1) * 256)
        dqab[0, rows, :] = jnp.where(low, dq[0], dq[2]) * (HEAD_DIM ** -0.5)
        dqab[1, rows, :] = jnp.where(low, dq[1], dq[3]) * (HEAD_DIM ** -0.5)
    lt.wait_recv()
    attended.wait()
    A.make(3, LT, other_lt.at[2], sm, other_sm, 0)
    send_keys(1)
    at("keys sent")

    def take(d, carry):
        @pl.when(z + d < O)
        def _():
            for s in (0, 1):
                down(s, d, z).wait_recv()
                dkk[s * 256 : (s + 1) * 256, :] += z_keys.read(z + d, s).astype(F32).reshape(256, 256)

        return carry

    lax.fori_loop(1, O, take, 0)
    at("keys")

    for i in range(3):
        up = dqab[i] if i < 2 else dkk[:, 0:128]
        raw = qkr[i]
        gain = hg[0:1, :] if i < 2 else hg[1:2, :]
        dw = up * cosb[...] + turn(up * sinb[...])
        rr = lax.rsqrt(head_mean(raw * raw) + norm_eps)
        dgain = jnp.sum(dw * raw * rr, axis=0, keepdims=True)
        row = 8 if i < 2 else 9
        vg[row : row + 1, 0:128] += dgain
        draw = rr * gain * dw - raw * (rr * rr * rr) * head_mean(raw * gain * dw)
        if i < 2:
            dqab[i] = draw
        else:
            sm[:, 512:640] = draw.astype(BF)
    left, right = to_pairs(dqab[0], dqab[1])
    sm[:, 256:384] = left.astype(BF)
    sm[:, 384:512] = right.astype(BF)
    sm[:, 640:768] = dkk[:, 128:256].astype(BF)
    grads = swap(11, sm.at[:, 256:768], other_sm.at[:, 256:768])
    sums = Sums(here, part, S, R, rss.at[1], rsr.at[1])
    sums.begin(lambda n: nt(sm[:, 256:768], rows_of(W, n, 0, 512)))
    load_w = pltpu.make_async_copy(wc, W, wls.at[1])
    load_w.start()
    lt = turned_saved(1, 3)
    sums.relay()
    lt.wait_recv()
    grads.wait()
    A.make(4, LT, other_lt.at[3], sm, other_sm, 256)
    at("qkv")
    dx, dgain = rms_back(x2[...], vec[2:3, :], sums.wait())
    vg[2:3, :] = dgain
    dprev[...] += dx
    D2 = DG.at[0]
    D2[r] = dprev[...].astype(BF)
    blocks = Gather(here, D2, ags.at[2], agr.at[2])
    blocks.relay()
    at("d2 relayed")
    load_w.wait()
    load_g.wait()
    blocks.wait()
    ffn_back(2, 4, D2, 4 * QD, x1, 1, C, dprev[...], "ffn1")

    DD = DG.at[1]
    tap0, tap1, tap2 = taps(here, vec)
    from_c, from_z = tail_c[...], jnp.where(z > 0, tail_z[...], 0.0)
    dyc = nn(flat(DD), cols(W, 3 * QD, QD))
    sm[:, 0:QD] = (bcx[1] * cz[...]).astype(BF)
    mixed = swap(14, sm.at[:, 0:QD], other_sm.at[:, 0:QD])
    sm[:, 2 * QD : 3 * QD] = (dyc * cz[...]).astype(BF)
    dzs = dyc * bcx[1]
    bx = bcx[0] * bcx[2]
    row = lax.broadcasted_iota(jnp.int32, (T, QD), 0)
    g0, g1, g2 = (jnp.zeros((1, QD), F32) for _ in range(3))
    for b in range(4):
        mine = bx[b * T : (b + 1) * T, :]
        dzb = dzs[b * T : (b + 1) * T, :]
        one, two, m1, m2 = behind(here, b, mine, from_c, from_z, start)
        g0 = g0 + jnp.sum(dzb * mine, axis=0, keepdims=True)
        g1 = g1 + jnp.sum(dzb * one * m1, axis=0, keepdims=True)
        g2 = g2 + jnp.sum(dzb * two * m2, axis=0, keepdims=True)
        b1 = tap1 * dzb * m1
        b2 = tap2 * dzb * m2
        heads[2 * b : 2 * b + 1, :] = b2[0:1]
        heads[2 * b + 1 : 2 * b + 2, :] = b1[0:1] + b2[1:2]
        dkk[b * T : (b + 1) * T, :] = (
            tap0 * dzb
            + jnp.where(row < T - 1, pltpu.roll(b1, T - 1, 0), 0.0)
            + jnp.where(row < T - 2, pltpu.roll(b2, T - 2, 0), 0.0)
        )
    over = remote(heads, head_c, hs.at[0], hr.at[0], here.at(dc=1))
    over.start()
    back = remote(heads, head_z, hs.at[1], hr.at[1], here.at(dz=O - 1, dc=1))

    @pl.when((c == 0) & (z > 0))
    def _():
        back.start()

    at("halo")
    rows = ga.shape[0]
    renew_a = Renew(here, ga, w_attn, m_attn, v_attn, new_attn, gu, dgu,
                    lambda n, w: other_gu.at[pl.ds(n * rows, rows), pl.ds(0, w)], rls.at[0], rss2.at[0], rrs.at[0])
    renew_c = Renew(here, gc, w_conv, m_conv, v_conv, new_conv, gu, dgu,
                    lambda n, w: W.at[n // 2, n % 2, :, pl.ds(0, w)], rls.at[1], rss2.at[1], rrs.at[1])
    for u in range(5):
        A.owned(u)
    for x_ in (0, 1):
        renew_a.run(x_, [(0, 2 * AW)])
    lt = turned(6, DD)
    tap_at = pl.ds(pl.multiple_of(r * QD, 128), QD)
    vg[4:5, tap_at] = g0
    vg[5:6, tap_at] = g1
    vg[6:7, tap_at] = g2
    over.wait()

    @pl.when((c == 1) & (z < O - 1))
    def _():
        back.wait_recv()

    to_c, to_z = head_c[...], jnp.where(z < O - 1, head_z[...], 0.0)
    for b in range(4):
        rows = slice(b * T, (b + 1) * T)
        if b % 2:
            e = jnp.where(c == 0, to_c[2 * b : 2 * b + 2], to_z[2 * b - 2 : 2 * b])
        else:
            e = jnp.where(c == 0, to_c[2 * b : 2 * b + 2], to_c[2 * b + 2 : 2 * b + 4])
        dbx = dkk[rows, :] + jnp.where(row == T - 2, e[0:1], jnp.where(row == T - 1, e[1:2], 0.0))
        sm[rows, QD : 2 * QD] = (dbx * bcx[2, rows, :]).astype(BF)
        sm[rows, 3 * QD : 4 * QD] = (dbx * bcx[0, rows, :]).astype(BF)
    grads = swap(15, sm.at[:, QD : 4 * QD], other_sm.at[:, QD : 4 * QD])
    sums = Sums(here, part, S, R, rss.at[3], rsr.at[3])
    sums.begin(lambda n: nt(sm[:, QD : 4 * QD], rows_of(W, n, 0, 768)))
    lt.wait_recv()
    mixed.wait()
    C.make(3, LT, other_lt.at[2], sm, other_sm, 0)
    lt = turned_saved(3, 7)
    lt.wait_recv()
    grads.wait()
    C.make(4, LT, other_lt.at[3], sm, other_sm, QD)
    at("made")
    sums.relay()
    at("sums relayed")
    dx, dgain = rms_back(tok[...].astype(F32), vec[0:1, :], sums.wait())
    vg[0:1, :] = dgain
    dtok[...] = dprev[...] + dx

    v0[c] = vg[...]
    cp = remote(v0.at[c], v0.at[c], vs.at[0], vr.at[0], here.at(dc=1))
    cp.start()
    at("end")
    cp.wait()
    v1[r] = v0[0] + v0[1]
    copies = [
        remote(v1.at[r], v1.at[r], vs.at[1 + k], vr.at[1 + k], here.at(dx=dx, dy=dy)) for k, (dx, dy) in enumerate(PLANE)
    ]
    for cp in copies:
        cp.start()
    at("end 1")
    wait_all(copies)
    v2[z] = v1[0] + v1[1] + v1[2] + v1[3]

    def start_z(dz, carry):
        remote(v2.at[z], v2.at[z], vs.at[3 + dz], vr.at[3 + dz], here.at(dz=dz)).start()
        return carry

    lax.fori_loop(1, O, start_z, 0)
    at("end 2")

    def wait_z(dz, carry):
        remote(v2.at[z], v2.at[z], vs.at[3 + dz], vr.at[3 + dz], here.at(dz=dz)).wait()
        return carry

    lax.fori_loop(1, O, wait_z, 0)
    t = v2[0]
    for i in range(1, O):
        t = t + v2[i]
    vectors[...] = t[0:7, :]
    gains[...] = t[8:10, 0:64] + pltpu.roll(t[8:10, 0:128], 64, 1)[:, 0:64]
    at("end 3")

    def keys_sent(zz, carry):
        for s in (0, 1):
            down(s, z - zz, zz).wait_send()
        return carry

    lax.fori_loop(0, z, keys_sent, 0)
    @pl.when((c == 0) & (z > 0))
    def _():
        back.wait_send()

    for cp in done:
        cp.wait_send()
    if few:
        A.sent()
    C.sent()
    A.finish()
    C.finish()
    renew_a.wait()
    renew_c.wait()


def backward(O, cot, tok, vec, hg, saved, state):
    (x1, x2, x3, h1, h2, h3, h4, bcx, cz, gu1, gu2, qkr, kv, oab, lse, wc, wa, Q, tail_c, tail_z, cosb, sinb, start,
     start_row, cots) = saved
    sds = jax.ShapeDtypeStruct
    G = 4 * T
    rows = D // (4 * O)
    few = O == 4
    dma = pltpu.SemaphoreType.DMA
    V = pltpu.VMEM
    keys = sds((O, 4, T, 256), BF)
    outs = (
        sds((T, D), F32), sds((7, D), F32), sds((2, HEAD_DIM), F32), sds((rows, 2 * AW), BF), sds((rows, 2 * CW), BF),
        sds((rows, 4 * AW), BF), sds((rows, 4 * CW), BF), sds((O, 2, rows, AW + CW), BF), keys, keys,
    )
    args = (cot, tok, vec, hg, *saved, *state)
    hbm = {id(a) for a in (*state, gu1, gu2, wc, wa, kv, h1, h2, h3, h4, cots)}
    keys_at = vmem() if few else any_spec()
    return pl.pallas_call(
        functools.partial(backward_kernel, O),
        out_shape=outs,
        in_specs=[any_spec() if id(a) in hbm else vmem() for a in args],
        out_specs=(vmem(), vmem(), vmem(), *[any_spec()] * 5, keys_at, keys_at),
        scratch_shapes=[
            V((2 * O, 2, rows, CW), BF), V((G, WIDE), F32), V((2, 4, T, D), BF), V((4, T, D), BF),
            V((G, WIDE), BF), V((G, QF), BF), V((G, D), BF), V((2 * O, 2, rows, G), BF),
            V((4, 2 * O, rows, G), BF), V((G, QF), BF), V((G, D), BF), V((G, WIDE), BF),
            V((2 * O, rows, CW), BF), *([V((2 * O, rows, CW), BF)] if few else []),
            V((O, 2, rows, QF), BF), V((2, rows, QF), F32), V((2, rows, AW), BF), V((2, rows, CW), BF),
            V((2, 4, T, D // 2), F32), V((2, 6, T // 2, D // 2), BF), V((2, 6, T // 2, D // 2), BF),
            V((2, 4, 256, 128), BF), V((2, 8, 2 * G), F32), V((4, 256, 128), F32), V((2, G, 128), F32),
            V((O, 4, 2, T, 256), BF), V((G, 256), F32),
            V((8, QD), F32), V((8, QD), F32), V((8, QD), F32), V((T, D), F32), V((16, D), F32),
            V((2, 16, D), F32), V((4, 16, D), F32), V((O, 16, D), F32), V((2, T, 256), BF),
            dma((4, 6)), dma((4, 6)), dma((4, 2, 6)), dma((4, 2, 6)), dma((2,)), dma((2,)),
            dma((2, O)), dma((2, O)), dma((2,)), dma((4,)), dma((4,)), dma((16,)), dma((16,)),
            dma((2, 5, O)), dma((2, 5, O)), dma((O,)), dma((2, 5)), dma((2, 5)), dma((O + 3,)), dma((O + 3,)), dma,
            dma((2, 20, 4)), dma((2, 20)), dma((2, 20)),
        ],
        compiler_params=pltpu.CompilerParams(
            collective_id=2, has_side_effects=True, vmem_limit_bytes=int(63.5 * 2**20)
        ),
        cost_estimate=pl.CostEstimate(flops=2 * 10**10, bytes_accessed=10**8, transcendentals=10**7),
        name="backward",
    )(*args)[:7]


REDUCTIONS = {
    "ffn2 down": (),
    "ffn2 wide": ("sa1",),
    "ffn2 end": (),
    "attention 0": (),
    "attention 1": ("ra0",),
    "keys sent": ("ta0", "ra1"),
    "keys": (),
    "qkv": ("sa2", "sa3", "sa4", "ta1"),
    "d2 relayed": ("ra2", "ra3", "ra4"),
    "ffn1 down": ("ta2", "ta3", "ta4"),
    "ffn1 wide": (),
    "ffn1 end": ("rc0",),
    "halo": ("sc1",),
    "made": ("sc2", "tc0"),
    "sums relayed": ("rc1", "nc0"),
    "end": ("tc1", "sc3", "sc4"),
    "end 1": ("rc2", "nc1"),
    "end 2": ("tc2", "rc3", "rc4", "nc2", "tc3", "tc4"),
    "end 3": ("nc3", "nc4"),
}


def adam_update(master, first_moment, second, gradient, step_value):
    first_new = beta_one * first_moment + (1.0 - beta_one) * gradient
    second_new = beta_two * second + (1.0 - beta_two) * gradient * gradient
    first_hat = first_new / (1.0 - beta_one**step_value)
    second_hat = second_new / (1.0 - beta_two**step_value)
    master_new = master - learn_rate * (
        first_hat / (jnp.sqrt(second_hat) + adam_eps) + decay_rate * master
    )
    return (master_new, first_new, second_new)


def shards(
    tokens, segments, cotangent, conv_weights, attn_weights, vectors, head_gains,
    master_conv, first_conv, second_conv, master_attn, first_attn, second_attn,
):
    O = lax.axis_size("z")
    tok = tokens[0]
    out_tok, hg, *saved = forward(O, tok, cotangent[0], vectors, head_gains, segments, rotary_rows(), conv_weights, attn_weights)
    state = (master_attn, first_attn, second_attn, master_conv, first_conv, second_conv)
    dtok, grad_vectors, grad_gains, ga, gc, attn_all, conv_all = backward(O, cotangent[0], tok, vectors, hg, saved, state)
    grad_attn, grad_conv = ga.astype(F32), gc.astype(F32)
    step_value = jnp.float32(STEP)
    new_conv = adam_update(master_conv, first_conv, second_conv, grad_conv, step_value)
    new_attn = adam_update(master_attn, first_attn, second_attn, grad_attn, step_value)
    return (
        out_tok[None], dtok[None], grad_conv, grad_attn, grad_vectors, grad_gains, *new_conv, *new_attn,
        conv_all, attn_all,
    )


def solution(mesh):
    outer = mesh.shape["ctx"] // 4
    split = Mesh(mesh.devices.reshape(mesh.shape["dp"], outer, 2, 2), ("dp", "z", "y", "c"))
    ctx = ("z", "y", "c")
    seq, rows, state = P("dp", ctx, None), P(ctx, None), P(ctx, "dp")
    return jax.shard_map(
        shards,
        mesh=split,
        in_specs=(seq, P("dp", ctx), seq, rows, rows, P(), P(), *([state] * 6)),
        out_specs=(seq, seq, state, state, P(), P(), *([state] * 6), rows, rows),
        check_vma=False,
    )
```

```python
import functools
import jax
import jax.numpy as jnp
import numpy as np
from jax import lax
from jax.sharding import Mesh, PartitionSpec as P
import jax.experimental.pallas as pl
import jax.experimental.pallas.tpu as pltpu

D = 1024
FF = 4608
HEADS = 16
KV_HEADS = 8
HEAD_DIM = 64
STEP = 5
KVW = 512
T = 128
QF = FF // 4
QD = D // 4
CW = 4 * QD + 3 * QF
AW = 3 * QD + 3 * QF

norm_eps = 1e-05
rope_base = 1000000.0
learn_rate = 0.01
decay_rate = 0.1
beta_one = 0.9
beta_two = 0.95
adam_eps = 1e-08

MESH = pl.DeviceIdType.MESH

SCHEDULE = {
    "in": ("f0", "f1",),
    "start": ("p0", "p1", "f2",),
    "h1 sent": ("f3", "p2",),
    "h1 relayed": ("f4", "b0",),
    "h1": ("f5", "l0", "l1", "r0",),
    "halo": ("p3", "p4",),
    "conv": ("r1", "p5",),
    "x1 sent": (),
    "x1 relayed": ("b2", "f6", "f7",),
    "h2 sent": (),
    "h2 relayed": ("b3", "f8",),
    "gate1 0": ("l2", "r2",),
    "gate1 1": ("l3", "r3",),
    "gate1 2": ("l4", "r4",),
    "down1": ("p6", "l5", "p7", "r5", "p8",),
    "x2 sent": (),
    "x2 relayed": ("f9", "b6",),
    "h3 sent": ("f10", "b7",),
    "h3 relayed": ("f11", "l6", "l7",),
    "qkv": ("r6",),
    "kv sent": ("p9", "b8",),
    "kv": ("p10",),
    "half": ("p11", "b9",),
    "attended": ("l8", "r7",),
    "x3 sent": ("b10",),
    "x3 relayed": ("l9",),
    "h4 sent": ("b11",),
    "h4 relayed": (),
    "gate2 0": ("l10", "r8",),
    "gate2 1": ("l11", "r9",),
    "gate2 2": ("r10",),
    "down2": ("r11",),
    "x4 sent": (),
    "x4 relayed": (),
}
BF = jnp.bfloat16
F32 = jnp.float32
PLANE = ((1, 1), (1, 0), (0, 1))

TILE = 384
WIDE = 2 * QF


def packed(lead, base, place):
    parts, spans = list(lead), []
    for n in range(3):
        for k in (0, 1):
            parts.append((base + k * FF + n * TILE, QF, TILE, place + (2 * n + k) * TILE, 2 + n))
    parts.append((base + 2 * FF, QF, QF, place + WIDE, 5))
    for g in range(6):
        mine = [p for p in parts if p[4] == g]
        spans.append((mine[0][3], sum(p[2] for p in mine)))
    return tuple(parts), tuple(spans)


CONV_PARTS, CONV_SPANS = packed(
    ((0, QD, QD, 0, 0), (D, QD, QD, QD, 0), (2 * D, QD, QD, 2 * QD, 0), (3 * D, QD, QD, 3 * QD, 1)), 4 * D, 4 * QD
)
KQ = KVW // 4
ATTN_PARTS, ATTN_SPANS = packed(
    ((0, QD, QD, 0, 0), (D, KQ, KQ, QD, 0), (D + KVW, KQ, KQ, QD + KQ, 0), (2 * D, QD, QD, 2 * QD, 1)), 3 * D, 3 * QD
)


def nn(a, b):
    return jnp.dot(a, b, preferred_element_type=F32)


def nt(a, b):
    return lax.dot_general(a, b, (((1,), (1,)), ((), ())), preferred_element_type=F32)


def tn(a, b):
    return lax.dot_general(a, b, (((0,), (0,)), ((), ())), preferred_element_type=F32)


def rms_scale(v):
    return lax.rsqrt(jnp.mean(v * v, axis=-1, keepdims=True) + norm_eps)


class Place:
    def __init__(self, O):
        self.O = O
        self.x, self.z = lax.axis_index("dp"), lax.axis_index("z")
        self.y, self.c = lax.axis_index("y"), lax.axis_index("c")
        self.r = self.x * 2 + self.y

    def at(self, dx=0, dz=0, dy=0, dc=0):
        out = {}
        if not (isinstance(dx, int) and dx == 0):
            out["dp"] = lax.rem(self.x + dx, 2)
        if not (isinstance(dz, int) and dz == 0):
            out["z"] = lax.rem(self.z + dz, self.O)
        if not (isinstance(dy, int) and dy == 0):
            out["y"] = lax.rem(self.y + dy, 2)
        if not (isinstance(dc, int) and dc == 0):
            out["c"] = lax.rem(self.c + dc, 2)
        return out

    def block(self, dx, dy):
        return lax.rem(self.x + dx, 2) * 2 + lax.rem(self.y + dy, 2)


def greet(here):
    O = here.O
    barrier = pltpu.get_barrier_semaphore()

    def hello(**k):
        pl.semaphore_signal(barrier, inc=1, device_id=here.at(**k), device_id_type=MESH)

    hello(dx=1, dy=1)
    hello(dx=1)
    hello(dy=1)
    hello(dc=1)
    hello(dz=1, dc=1)
    hello(dz=O - 1, dc=1)

    def along(dz, carry):
        for dy in (0, 1):
            hello(dz=dz, dy=dy)
        return carry

    lax.fori_loop(1, O, along, 0)
    pl.semaphore_wait(barrier, 6 + 2 * (O - 1))


def remote(src, dst, ss, rs, dev):
    return pltpu.make_async_remote_copy(
        src_ref=src, dst_ref=dst, send_sem=ss, recv_sem=rs, device_id=dev, device_id_type=MESH
    )


HALF = (slice(0, T // 2), slice(T // 2, T))


class Gather:
    def __init__(self, here, H, ss, rs):
        self.here = here
        r, rx, ry = here.r, here.block(1, 0), here.block(0, 1)
        to_x, to_y = here.at(dx=1), here.at(dy=1)

        def cp(i, block, half, dev):
            rows = pl.ds(half * (T // 2), T // 2)
            return remote(H.at[block, rows], H.at[block, rows], ss.at[i], rs.at[i], dev)

        self.first = (cp(0, r, 0, to_x), cp(1, r, 1, to_y), cp(2, r, 1, to_x), cp(3, r, 0, to_y))
        self.then = (cp(4, rx, 0, to_y), cp(5, ry, 1, to_x))
        for c in self.first:
            c.start()

    def relay(self):
        for i in (0, 1):
            self.first[i].wait_recv()
            self.then[i].start()

    def wait(self):
        for c in self.first[2:]:
            c.wait_recv()
        for c in self.then:
            c.wait_recv()
        for c in self.first + self.then:
            c.wait_send()


class Sums:
    def __init__(self, here, part, S, R, ss, rs):
        self.here, self.part, self.S, self.R, self.ss, self.rs = here, part, S, R, ss, rs

    def cp(self, n, i):
        h = self.here
        dev = h.at(dx=1) if i % 2 == 0 else h.at(dy=1)
        return remote(self.S.at[n, i], self.R.at[n, i], self.ss.at[n, i], self.rs.at[n, i], dev)

    def put(self, n, i, block, half):
        self.S[n, i] = self.part[n, block, HALF[half], :].astype(BF)
        self.cp(n, i).start()

    def begin(self, tile_fn):
        h = self.here
        rx, ry, rd = h.block(1, 0), h.block(0, 1), h.block(1, 1)
        for n in (0, 1):
            self.part[n] = tile_fn(n).reshape(4, T, D // 2)
            self.put(n, 0, rd, 0)
            self.put(n, 1, rd, 1)
            self.put(n, 2, rx, 0)
            self.put(n, 3, ry, 1)

    def relay(self):
        h = self.here
        rx, ry = h.block(1, 0), h.block(0, 1)
        for n in (0, 1):
            for i, block, half in ((0, ry, 0), (1, rx, 1)):
                self.cp(n, i).wait_recv()
                at = 5 - i
                both = self.part[n, block, HALF[half], :] + self.R[n, i].astype(F32)
                self.S[n, at] = both.astype(BF)
                self.cp(n, at).start()

    def wait(self):
        out = []
        for n in (0, 1):
            for i in (2, 3, 4, 5):
                self.cp(n, i).wait_recv()
            for i in range(6):
                self.cp(n, i).wait_send()
            mine = self.part[n, self.here.r]
            R = self.R
            low = mine[HALF[0]] + R[n, 2].astype(F32) + R[n, 5].astype(F32)
            high = mine[HALF[1]] + R[n, 4].astype(F32) + R[n, 3].astype(F32)
            out.append(jnp.concatenate([low, high], axis=0))
        return jnp.concatenate(out, axis=1)


def wait_all(copies):
    for cp in copies:
        cp.wait()


class Weights:
    def __init__(self, here, hbm, W, parts, spans, ls, ys, yr, zs, zr, cs, cr):
        self.here, self.hbm, self.W = here, hbm, W
        self.parts, self.spans = parts, spans
        self.ls, self.ys, self.yr, self.zs, self.zr, self.cs, self.cr = ls, ys, yr, zs, zr, cs, cr
        self.relayed = here.O == 4
        self.passed = set()

    def source(self, part, dy):
        base, stride, width, _, _ = part
        chip = self.here.x * 2 + lax.rem(self.here.y + dy, 2)
        return self.hbm.at[:, pl.ds(pl.multiple_of(base + chip * stride, 128), width)]

    def target(self, part):
        _, _, width, place, _ = part
        h = self.here
        return self.W.at[h.z * 2 + h.y, h.c, :, pl.ds(place, width)]

    def fetch(self, g):
        h = self.here
        for part in self.parts:
            if part[4] != g:
                continue
            pltpu.make_async_copy(self.source(part, 0), self.target(part), self.ls.at[g]).start()
            remote(self.source(part, 1), self.target(part), self.ys.at[g], self.yr.at[g], h.at(dy=1)).start()

    def shards(self, g, first, count):
        place, width = self.spans[g]
        return self.W.at[pl.ds(first, count), self.here.c, :, pl.ds(place, width)]

    def hop(self, g, dz, owner):
        src = self.shards(g, 2 * owner, 2)
        return remote(src, src, self.zs.at[g, dz], self.zr.at[g, dz], self.here.at(dz=dz))

    def near(self, dz):
        z = self.here.z
        return z < 3 if dz == 1 else z > 0 if dz == 3 else z >= 0

    def came(self, dz):
        z = self.here.z
        return z > 0 if dz == 1 else z < 3 if dz == 3 else z >= 0

    def bridge(self, g, owner, dz):
        src = self.shards(g, 2 * owner, 2)
        return remote(src, src, self.zs.at[g, 0], self.zr.at[g, 0], self.here.at(dz=dz))

    def push(self, g):
        h = self.here
        one = self.shards(g, 0, 1)
        pltpu.make_async_copy(one, one, self.ls.at[g]).wait()
        pltpu.make_async_copy(one, one, self.yr.at[g]).wait()
        self.core_copy(g, h.z).start()
        if self.relayed:
            for dz in (2, 1, 3):

                @pl.when(self.near(dz))
                def _():
                    self.hop(g, dz, h.z).start()
        else:

            def along(dz, carry):
                self.hop(g, dz, h.z).start()
                return carry

            lax.fori_loop(1, h.O, along, 0)

    def core_copy(self, g, owner):
        mine = self.shards(g, 2 * owner, 2)
        return remote(mine, mine, self.cs.at[g], self.cr.at[g], self.here.at(dc=1))

    def behind(self, dz):
        return lax.rem(self.here.z + self.here.O - dz, self.here.O)

    def pass_far(self, g):
        h = self.here
        if not self.relayed:
            return
        self.passed.add(g)
        self.hop(g, 2, h.z).wait_recv()

        @pl.when(h.z == 2)
        def _():
            self.bridge(g, 0, 1).start()

        @pl.when(h.z == 1)
        def _():
            self.bridge(g, 3, 3).start()

        self.core_copy(g, self.behind(2)).start()

    def land(self, g):
        h = self.here
        if self.relayed:
            if g not in self.passed:
                self.pass_far(g)
            for dz in (1, 3):

                @pl.when(self.came(dz))
                def _():
                    self.hop(g, dz, h.z).wait_recv()
                    self.core_copy(g, self.behind(dz)).start()

            @pl.when((h.z == 0) | (h.z == 3))
            def _():
                self.bridge(g, 0, 1).wait_recv()
                self.core_copy(g, 3 - h.z).start()

        else:

            def along(dz, carry):
                self.hop(g, dz, h.z).wait_recv()
                self.core_copy(g, self.behind(dz)).start()
                return carry

            lax.fori_loop(1, h.O, along, 0)

    def ready(self, g):
        place, width = self.spans[g]
        half = self.W.at[:, 0, :, pl.ds(place, width)]
        pltpu.make_async_copy(half, half, self.cs.at[g]).wait()
        pltpu.make_async_copy(half, half, self.cr.at[g]).wait()

    def finish(self):
        h = self.here
        for g in range(6):
            one = self.shards(g, 0, 1)
            pltpu.make_async_copy(one, one, self.ys.at[g]).wait()
            if self.relayed:
                for dz in (1, 2, 3):

                    @pl.when(self.near(dz))
                    def _():
                        self.hop(g, dz, h.z).wait_send()

                @pl.when((h.z == 1) | (h.z == 2))
                def _():
                    self.bridge(g, 0, 1).wait_send()

            else:

                def along(dz, carry):
                    self.hop(g, dz, h.z).wait_send()
                    return carry

                lax.fori_loop(1, h.O, along, 0)


def cols(W, place, width):
    v = W[:, :, :, pl.ds(place, width)]
    return v.reshape(D, width)


def rows_of(W, n, place, width):
    h = W.shape[0] // 2
    v = W[n * h : (n + 1) * h, :, :, pl.ds(place, width)]
    return v.reshape(D // 2, width)


def lane_low(shape):
    return lax.broadcasted_iota(jnp.int32, shape, len(shape) - 1) < 64


def lane_first(shape):
    return lax.rem(lax.broadcasted_iota(jnp.int32, shape, len(shape) - 1), 64) < 32


def head_mean(v):
    low = lane_low(v.shape)
    a = jnp.sum(jnp.where(low, v, 0.0), axis=-1, keepdims=True)
    b = jnp.sum(jnp.where(low, 0.0, v), axis=-1, keepdims=True)
    return jnp.where(low, a, b) * (1.0 / HEAD_DIM)


def turn(v):
    return jnp.where(lane_first(v.shape), pltpu.roll(v, 96, 1), pltpu.roll(v, 32, 1))


def to_pairs(left, right):
    low = lane_low(left.shape)
    a = jnp.where(low, left, pltpu.roll(right, 64, 1))
    b = jnp.where(low, pltpu.roll(left, 64, 1), right)
    return a, b


def stacked(a, b):
    low = lane_low(a.shape)
    zero = jnp.zeros_like(a)
    return (jnp.where(low, a, zero), jnp.where(low, b, zero), jnp.where(low, zero, a), jnp.where(low, zero, b))


def ffn_forward_tile(H, W, at, gu, u, n):
    both = nn(H[...].reshape(4 * T, D), cols(W, at + 2 * n * TILE, 2 * TILE))
    gu[:, 2 * n * TILE : 2 * (n + 1) * TILE] = both
    gate, up = both[:, 0:TILE], both[:, TILE:]
    u[:, n * TILE : (n + 1) * TILE] = (gate / (1.0 + jnp.exp(-gate)) * up).astype(BF)


def taps(here, vec):
    at = pl.ds(pl.multiple_of(here.r * QD, 128), QD)
    return tuple(vec[4 + i : 5 + i, at] for i in range(3))


def behind(here, b, mine, from_c, from_z, start):
    z, c, yb = here.z, here.c, b % 2
    if yb:
        before = jnp.where(c == 1, from_c[2 * b : 2 * b + 2], from_c[2 * b - 2 : 2 * b])
    else:
        before = jnp.where(c == 1, from_c[2 * b : 2 * b + 2], from_z[2 * b + 2 : 2 * b + 4])
    row = lax.broadcasted_iota(jnp.int32, (T, QD), 0)
    one = jnp.where(row == 0, before[1:2], pltpu.roll(mine, 1, 0))
    two = jnp.where(row == 0, before[0:1], jnp.where(row == 1, before[1:2], pltpu.roll(mine, 2, 0)))
    t = z * 512 + yb * 256 + c * T + lax.broadcasted_iota(jnp.int32, (T, 1), 0)
    pos = t - start[b * T : (b + 1) * T, 0:1]
    return one, two, jnp.where(pos >= 1, 1.0, 0.0), jnp.where(pos >= 2, 1.0, 0.0)


def meta_copies(here, M1, M2, M3, ms, mr):
    def along(act):
        def body(dz, carry):
            act(remote(M1.at[here.z], M1.at[here.z], ms.at[dz], mr.at[dz], here.at(dz=dz)))
            return carry

        lax.fori_loop(1, here.O, body, 0)

    core = remote(M2.at[here.c], M2.at[here.c], ms.at[0], mr.at[0], here.at(dc=1))
    plane = [
        remote(M3.at[here.r], M3.at[here.r], ms.at[here.O + k], mr.at[here.O + k], here.at(dx=dx, dy=dy))
        for k, (dx, dy) in enumerate(PLANE)
    ]
    return along, core, plane


def write_starts(here, M3, start, start_row):
    counts = jnp.sum(M3[...].reshape(4, 2 * here.O, 8, T), axis=1)
    for b in range(4):
        xb = b // 2
        pair = counts[2 * xb] + counts[2 * xb + 1]
        begin, end = pair[1:2, :], here.O * 4 * T - pair[2:3, :]
        seg = M3[b, here.c, here.z, 0:1, :]
        start_row[:, b * T : (b + 1) * T] = jnp.broadcast_to(
            jnp.where(seg == 0, 0, jnp.where(seg == 1, begin, end)), (8, T)
        )
        ids = jnp.transpose(jnp.broadcast_to(seg.astype(F32), (T, T)))
        first = jnp.where(ids < 0.5, 0, jnp.where(ids < 1.5, begin, end))
        start[b * T : (b + 1) * T, :] = first


def write_rotary(here, start, freq, cosb, sinb):
    for b in range(4):
        rows = slice(b * T, (b + 1) * T)
        t = here.z * 512 + (b % 2) * 256 + here.c * T + lax.broadcasted_iota(jnp.int32, (T, T), 0)
        angle = (t - start[rows, :]).astype(F32) * freq[0:1, :]
        cosb[rows, :] = jnp.cos(angle)
        sinb[rows, :] = jnp.sin(angle) * freq[1:2, :]


def forward_kernel(
    O, tok, cot, vec, head_gains, segments, freq, wc_hbm, wa_hbm,
    out_tok, hg, x1, x2, x3, h1_out, h2_out, h3_out, h4_out, bcx, cz, gu1_out, gu2_out, qkr, kv_out, oab, lse, wc_out, wa_out, Q,
    tail_c, tail_z, cosb, sinb, start, start_row, cots_out,
    cots, h1, h2, h3, h4, gu1, gu2, kv, wc, wa,
    u, part, S, R, tails, acc, M1, M2, M3,
    ags, agr, rss, rsr, hs, hr, kvs, kvr, wls, wys, wyr, wzs, wzr, wcs, wcr, ms, mr, outs,
):
    here = Place(O)
    x, y, z, c, r = here.x, here.y, here.z, here.c, here.r
    greet(here)
    sets = []
    for i, (hbm, W, parts, spans) in enumerate(
        ((wc_hbm, wc, CONV_PARTS, CONV_SPANS), (wa_hbm, wa, ATTN_PARTS, ATTN_SPANS))
    ):
        sets.append(
            Weights(here, hbm, W, parts, spans, *(a.at[i] for a in (wls, wys, wyr, wzs, wzr, wcs, wcr)))
        )
    queue = [(w, g) for w in sets for g in range(6)]

    def at(point):
        for step in SCHEDULE[point]:
            w, g = queue[int(step[1:])]
            {"f": w.fetch, "p": w.push, "b": w.pass_far, "l": w.land, "r": w.ready}[step[0]](g)

    z_meta, core_meta, plane_meta = meta_copies(here, M1, M2, M3, ms, mr)
    row = lax.broadcasted_iota(jnp.int32, (8, T), 0)
    seg = segments[...]
    count = [jnp.sum(jnp.where(seg == i, 1.0, 0.0), axis=1, keepdims=True).astype(jnp.int32) for i in (0, 2)]
    M1[z] = jnp.where(row == 0, seg, jnp.where(row == 1, count[0], count[1]))
    hg[:, 0:64] = head_gains[...]
    hg[:, 64:128] = head_gains[...]
    z_meta(lambda cp: cp.start())
    saving = []

    def save(i, src, dst):
        cp = pltpu.make_async_copy(src, dst, outs.at[i])
        cp.start()
        saving.append(cp)

    at("in")
    x0 = tok[...].astype(F32)
    h1[r] = (x0 * rms_scale(x0) * vec[0:1, :]).astype(BF)
    blocks = Gather(here, h1, ags.at[0], agr.at[0])
    at("start")
    z_meta(lambda cp: cp.wait())
    M2[c] = M1[...]
    core_meta.start()
    at("h1 sent")
    blocks.relay()
    core_meta.wait()
    M3[r] = M2[...]
    for cp in plane_meta:
        cp.start()
    at("h1 relayed")
    blocks.wait()
    wait_all(plane_meta)
    write_starts(here, M3, start, start_row)
    at("h1")

    save(0, h1, h1_out)
    h = h1[...].reshape(4 * T, D)
    for i in range(3):
        bcx[i] = nn(h, cols(wc, i * QD, QD))
    bx = bcx[0] * bcx[2]
    for b in range(4):
        tails[2 * b : 2 * b + 2, :] = bx[b * T + T - 2 : b * T + T, :]
    over = remote(tails, tail_c, hs.at[0], hr.at[0], here.at(dc=1))
    over.start()
    ahead = remote(tails, tail_z, hs.at[1], hr.at[1], here.at(dz=1, dc=1))

    @pl.when((c == 1) & (z < O - 1))
    def _():
        ahead.start()

    at("halo")
    over.wait()

    @pl.when((c == 0) & (z > 0))
    def _():
        ahead.wait_recv()

    tap0, tap1, tap2 = taps(here, vec)
    from_c, from_z = tail_c[...], jnp.where(z > 0, tail_z[...], 0.0)
    for b in range(4):
        mine = bx[b * T : (b + 1) * T, :]
        one, two, m1, m2 = behind(here, b, mine, from_c, from_z, start)
        cz[b * T : (b + 1) * T, :] = tap0 * mine + tap1 * one * m1 + tap2 * two * m2
    yc = (bcx[1] * cz[...]).astype(BF)
    at("conv")
    sums = Sums(here, part, S, R, rss.at[0], rsr.at[0])
    sums.begin(lambda n: nt(yc, rows_of(wc, n, 3 * QD, QD)))
    at("x1 sent")
    sums.relay()
    at("x1 relayed")
    xn = tok[...].astype(F32) + sums.wait()
    x1[...] = xn
    h2[r] = (xn * rms_scale(xn) * vec[1:2, :]).astype(BF)
    blocks = Gather(here, h2, ags.at[1], agr.at[1])
    at("h2 sent")
    blocks.relay()
    at("h2 relayed")
    write_rotary(here, start, freq, cosb, sinb)
    blocks.wait()
    cots[r] = cot[...]
    cot_blocks = Gather(here, cots, ags.at[4], agr.at[4])
    for n in range(3):
        at("gate1 %d" % n)
        if n == 1:
            cot_blocks.relay()
        ffn_forward_tile(h2, wc, 4 * QD, gu1, u, n)
    cot_blocks.wait()
    save(9, cots, cots_out)
    save(1, h2, h2_out)
    save(2, gu1, gu1_out)
    at("down1")
    sums = Sums(here, part, S, R, rss.at[1], rsr.at[1])
    sums.begin(lambda n: nt(u[...], rows_of(wc, n, 4 * QD + WIDE, QF)))
    save(3, wc, wc_out)
    at("x2 sent")
    sums.relay()
    at("x2 relayed")
    xn = x1[...] + sums.wait()
    x2[...] = xn
    h3[r] = (xn * rms_scale(xn) * vec[2:3, :]).astype(BF)
    blocks = Gather(here, h3, ags.at[2], agr.at[2])
    at("h3 sent")
    blocks.relay()
    at("h3 relayed")
    blocks.wait()
    at("qkv")

    qkv = nn(h3[...].reshape(4 * T, D), cols(wa, 0, 512))
    qa, qb = to_pairs(qkv[:, 0:128], qkv[:, 128:256])
    raw = (qa, qb, qkv[:, 256:384])
    turned = []
    for i in range(3):
        qkr[i] = raw[i]
        gain = hg[0:1, :] if i < 2 else hg[1:2, :]
        w = raw[i] * lax.rsqrt(head_mean(raw[i] * raw[i]) + norm_eps) * gain
        turned.append(w * cosb[...] + turn(w) * sinb[...])
    keys = turned[2].astype(BF)
    values = qkv[:, 384:512].astype(BF)
    for b in range(4):
        kv[z, b, c, :, 0:128] = keys[b * T : (b + 1) * T]
        kv[z, b, c, :, 128:256] = values[b * T : (b + 1) * T]
    mine = kv.at[z, :, c]

    bridged = False

    def far(dz):
        return bridged and dz == 3

    def up(dz):
        return remote(mine, mine, kvs.at[dz], kvr.at[dz], here.at(dz=dz))

    def over_far():
        got = kv.at[0, :, c]
        return remote(got, got, kvs.at[2 * O], kvr.at[2 * O], here.at(dz=1))

    def along_z(act):
        if bridged:
            for dz in range(1, O):
                act(dz)
        else:

            def body(dz, carry):
                act(dz)
                return carry

            lax.fori_loop(1, O, body, 0)

    def send_up(dz):
        if not far(dz):

            @pl.when(z + dz < O)
            def _():
                up(dz).start()

    along_z(send_up)
    at("kv sent")
    pair0 = remote(mine, mine, kvs.at[0], kvr.at[0], here.at(dc=1))
    pair0.start()
    for s in (0, 1):
        low4 = stacked(*(
            (turned[i][s * 256 : (s + 1) * 256] * (HEAD_DIM ** -0.5)).astype(BF) for i in (0, 1)
        ))
        for g in range(4):
            Q[s, g] = low4[g]

    def passed(dz):
        got = kv.at[z - dz, :, c]
        return remote(got, got, kvs.at[O + dz], kvr.at[O + dz], here.at(dc=1))

    if bridged:

        @pl.when(z == 2)
        def _():
            up(2).wait_recv()
            over_far().start()

    def pass_on(dz):
        @pl.when(z - dz >= 0)
        def _():
            if far(dz):
                over_far().wait_recv()
            elif bridged and dz == 2:

                @pl.when(z != 2)
                def _():
                    up(dz).wait_recv()

            else:
                up(dz).wait_recv()
            passed(dz).start()

    along_z(pass_on)
    pair0.wait()

    def pass_wait(dz):
        @pl.when(z - dz >= 0)
        def _():
            passed(dz).wait()

    along_z(pass_wait)
    at("kv")
    save(4, h3, h3_out)
    save(5, kv, kv_out)

    low = lane_low((256, 128))
    for s in (0, 1):
        if s:
            at("half")
        acc[...] = jnp.zeros_like(acc)
        first_of = start[s * 256 : (s + 1) * 256, 0:1]
        row = lax.broadcasted_iota(jnp.int32, (256, 1), 0)
        t = z * 512 + lax.div(row, T) * 256 + c * T + lax.rem(row, T)

        def chunk(j, carry):
            block = kv[lax.div(j, 2), 2 * s + lax.rem(j, 2)].reshape(256, 256)
            k, v = block[:, 0:128], block[:, 128:256]
            one = jnp.ones_like(v)
            v_low = jnp.where(low, v, one)
            v_high = jnp.where(low, one, v)
            at = j * 256 + lax.broadcasted_iota(jnp.int32, (256, 256), 1)
            allowed = (at >= first_of) & (at <= t)
            for g in range(4):
                sc = nt(Q[s, g], k)
                p = jnp.where(allowed, jnp.exp(sc), 0.0).astype(BF)
                acc[g] += nn(p, v_low if g < 2 else v_high)
            return carry

        lax.fori_loop(0, 2 * z + 2, chunk, 0)
        heads = []
        for g in range(4):
            a = acc[g]
            other = pltpu.roll(a, 64, 1)
            heads.append(a / other)
            total = jnp.where(low, other, a) if g < 2 else jnp.where(low, a, other)
            lse[s, :, g * 256 : (g + 1) * 256] = jnp.transpose(jnp.log(total))[0:8, :]
        oab[0, s * 256 : (s + 1) * 256, :] = jnp.where(low, heads[0], heads[2])
        oab[1, s * 256 : (s + 1) * 256, :] = jnp.where(low, heads[1], heads[3])
    at("attended")
    left, right = to_pairs(oab[0], oab[1])
    ao = jnp.concatenate([left, right], axis=1).astype(BF)
    sums = Sums(here, part, S, R, rss.at[2], rsr.at[2])
    sums.begin(lambda n: nt(ao, rows_of(wa, n, 2 * QD, QD)))
    at("x3 sent")
    sums.relay()
    at("x3 relayed")
    xn = x2[...] + sums.wait()
    x3[...] = xn
    h4[r] = (xn * rms_scale(xn) * vec[3:4, :]).astype(BF)
    blocks = Gather(here, h4, ags.at[3], agr.at[3])
    at("h4 sent")
    blocks.relay()
    at("h4 relayed")
    blocks.wait()
    for n in range(3):
        at("gate2 %d" % n)
        ffn_forward_tile(h4, wa, 3 * QD, gu2, u, n)
    save(6, h4, h4_out)
    save(7, gu2, gu2_out)
    at("down2")
    sums = Sums(here, part, S, R, rss.at[3], rsr.at[3])
    sums.begin(lambda n: nt(u[...], rows_of(wa, n, 3 * QD + WIDE, QF)))
    save(8, wa, wa_out)
    at("x4 sent")
    sums.relay()
    at("x4 relayed")
    out_tok[...] = (x3[...] + sums.wait()).astype(BF)

    @pl.when((c == 1) & (z < O - 1))
    def _():
        ahead.wait_send()

    def up_sent(dz):
        if not far(dz):

            @pl.when(z + dz < O)
            def _():
                up(dz).wait_send()

    along_z(up_sent)
    if bridged:

        @pl.when(z == 2)
        def _():
            over_far().wait_send()

    for w in sets:
        w.finish()
    wait_all(saving)


def any_spec():
    return pl.BlockSpec(memory_space=pl.ANY)


def vmem():
    return pl.BlockSpec(memory_space=pltpu.VMEM)


def forward(O, tok, cot, vec, hg, segments, freq, wc_hbm, wa_hbm):
    sds = jax.ShapeDtypeStruct
    G = 4 * T
    outs = (
        sds((T, D), BF), sds((2, 128), F32),
        *(sds((T, D), F32) for _ in range(3)),
        *(sds((4, T, D), BF) for _ in range(4)),
        sds((3, G, QD), F32), sds((G, QD), F32),
        sds((G, WIDE), F32), sds((G, WIDE), F32),
        sds((3, G, 128), F32), sds((O, 4, 2, T, 256), BF), sds((2, G, 128), F32), sds((2, 8, 2 * G), F32),
        sds((2 * O, 2, D // (4 * O), CW), BF), sds((2 * O, 2, D // (4 * O), AW), BF),
        sds((2, 4, 256, 128), BF), sds((8, QD), F32), sds((8, QD), F32),
        sds((G, T), F32), sds((G, T), F32), sds((G, T), jnp.int32), sds((8, G), jnp.int32),
        sds((4, T, D), BF),
    )
    big = (len(outs) - 1, 5, 6, 7, 8, 11, 12, 14, 17, 18)
    dma = pltpu.SemaphoreType.DMA
    return pl.pallas_call(
        functools.partial(forward_kernel, O),
        out_shape=outs,
        in_specs=[vmem()] * 6 + [any_spec()] * 2,
        out_specs=tuple(any_spec() if i in big else vmem() for i in range(len(outs))),
        scratch_shapes=[
            *(pltpu.VMEM(outs[i].shape, outs[i].dtype) for i in big),
            pltpu.VMEM((G, QF), BF), pltpu.VMEM((2, 4, T, D // 2), F32),
            pltpu.VMEM((2, 6, T // 2, D // 2), BF), pltpu.VMEM((2, 6, T // 2, D // 2), BF),
            pltpu.VMEM((8, QD), F32), pltpu.VMEM((4, 256, 128), F32),
            pltpu.VMEM((O, 8, T), jnp.int32), pltpu.VMEM((2, O, 8, T), jnp.int32), pltpu.VMEM((4, 2, O, 8, T), jnp.int32),
            dma((5, 6)), dma((5, 6)), dma((4, 2, 6)), dma((4, 2, 6)), dma((2,)), dma((2,)),
            dma((2 * O + 1,)), dma((2 * O + 1,)),
            dma((2, 6)), dma((2, 6)), dma((2, 6)), dma((2, 6, O)), dma((2, 6, O)), dma((2, 6)), dma((2, 6)), dma((O + 3,)), dma((O + 3,)), dma((10,)),
        ],
        compiler_params=pltpu.CompilerParams(
            collective_id=1, has_side_effects=True, vmem_limit_bytes=61 * 2**20
        ),
        cost_estimate=pl.CostEstimate(flops=10**10, bytes_accessed=6 * 10**7, transcendentals=10**7),
        name="forward",
    )(tok, cot, vec, hg, segments, freq, wc_hbm, wa_hbm)


def rotary_rows():
    lane = np.arange(T)
    freq = rope_base ** (-((lane % (HEAD_DIM // 2)).astype(np.float32) * 2.0) / HEAD_DIM)
    sign = np.where(lane % HEAD_DIM < HEAD_DIM // 2, -1.0, 1.0)
    return jnp.asarray(np.stack([freq, sign]), F32)


def rms_back(x, gain, dh):
    r = rms_scale(x)
    inner = jnp.mean(x * gain * dh, axis=-1, keepdims=True)
    return r * gain * dh - x * (r * r * r) * inner, jnp.sum(dh * x * r, axis=0, keepdims=True)


def ffn_back_tile(DF, W, at, gu, dgu, mx, n):
    d = nn(DF[...].reshape(4 * T, D), cols(W, at + WIDE + n * TILE, TILE))
    two = slice(2 * n * TILE, (2 * n + 1) * TILE), slice((2 * n + 1) * TILE, 2 * (n + 1) * TILE)
    gate, up = gu[:, two[0]], gu[:, two[1]]
    sig = 1.0 / (1.0 + jnp.exp(-gate))
    silu = gate * sig
    dgu[:, two[0]] = (d * up * (sig * (1.0 + gate * (1.0 - sig)))).astype(BF)
    dgu[:, two[1]] = (d * silu).astype(BF)
    mx[:, n * TILE : (n + 1) * TILE] = (silu * up).astype(BF)


class Reduce:
    def __init__(self, here, parts, units, half, own, zb, off, zv, za, plane, out, zs, zr, ld, ps, pr):
        self.here, self.parts, self.units, self.half = here, parts, units, half
        self.own, self.zb, self.off, self.zv, self.za = own, zb, off, zv, za
        self.plane, self.out, self.zs, self.zr, self.ld, self.ps, self.pr = plane, out, zs, zr, ld, ps, pr
        self.few = here.O == 4

    def make(self, u, left, left_other, right, right_other, at):
        h = self.here
        place, width = self.units[u]
        step = TILE if width % TILE == 0 else 256
        rows = self.own.shape[1]

        def body(n, carry):
            o = pl.multiple_of(n * step, 128)
            a = nn(left[:, h.c].reshape(D // 2, 4 * T), right[:, pl.ds(at + o, step)])
            b = nn(left_other[...].reshape(D // 2, 4 * T), right_other[:, pl.ds(at + o, step)])
            self.own[:, :, pl.ds(place + o, step)] = (a + b).astype(BF).reshape(2 * h.O, rows, step)
            return carry

        lax.fori_loop(0, width // step, body, 0)

    def span(self, u):
        place, width = self.units[u]
        return pl.ds(place, width)

    def slot(self, u, dz):
        place, width = self.units[u]
        return self.zb.at[dz, :, :, pl.ds(self.off + place, width)]

    def hop(self, u, dz, plane):
        src = self.own.at[pl.ds(2 * plane, 2), :, self.span(u)]
        return remote(src, self.slot(u, dz), self.zs.at[u, dz], self.zr.at[u, dz], self.here.at(dz=dz))

    def far(self, u):
        h = self.here
        src = self.own.at[pl.ds(2 * (3 - h.z), 2), :, self.span(u)]
        to = h.at(dz=jnp.where(h.z == 0, 1, 3))
        return remote(src, self.slot(u, 0), self.zs.at[u, 0], self.zr.at[u, 0], to)

    def ends(self):
        return (self.here.z == 0) | (self.here.z == 3)

    def middle(self):
        return (self.here.z == 1) | (self.here.z == 2)

    def send(self, u):
        h = self.here
        if not self.few:

            def along(dz, carry):
                self.hop(u, dz, lax.rem(h.z + dz, h.O)).start()
                return carry

            lax.fori_loop(1, h.O, along, 0)
            return

        @pl.when(self.ends())
        def _():
            self.far(u).start()
            self.hop(u, 2, lax.rem(h.z + 2, 4)).start()

        @pl.when(h.z < 3)
        def _():
            self.hop(u, 1, h.z + 1).start()

        @pl.when(h.z > 0)
        def _():
            self.hop(u, 3, h.z - 1).start()

    def load(self, u, dz):
        _, width = self.units[u]
        return pltpu.make_async_copy(self.slot(u, dz), self.zv.at[dz, :, :, pl.ds(0, width)], self.ld.at[dz])

    def relay(self, u):
        if not self.few:
            return
        h = self.here
        _, width = self.units[u]

        @pl.when(self.middle())
        def _():
            self.far(u).wait_recv()
            self.load(u, 0).start()
            self.load(u, 0).wait()
            rows = pl.ds(2 * jnp.where(h.z == 1, 3, 0), 2)
            both = self.own[rows, :, self.span(u)].astype(F32) + self.zv[0, :, :, 0:width].astype(F32)
            self.own[rows, :, self.span(u)] = both.astype(BF)
            self.hop(u, 2, jnp.where(h.z == 1, 3, 0)).start()

    def total(self, u):
        h = self.here
        _, width = self.units[u]
        za = self.za.at[:, :, pl.ds(0, width)]
        za[...] = self.own[pl.ds(2 * h.z, 2), :, self.span(u)].astype(F32)

        def add(dz):
            za[...] += self.zv[dz, :, :, 0:width].astype(F32)

        if self.few:
            came = ((1, h.z > 0), (3, h.z < 3))
            self.hop(u, 2, 0).wait_recv()
            self.load(u, 2).start()
            for dz, there in came:

                @pl.when(there)
                def _():
                    self.hop(u, dz, 0).wait_recv()
                    self.load(u, dz).start()

            self.load(u, 2).wait()
            add(2)
            for dz, there in came:

                @pl.when(there)
                def _():
                    self.load(u, dz).wait()
                    add(dz)

        else:

            def along(dz, carry):
                self.hop(u, dz, 0).wait_recv()
                self.load(u, dz).start()
                self.load(u, dz).wait()
                add(dz)
                return carry

            lax.fori_loop(1, h.O, along, 0)
        self.plane[:, :, self.span(u)] = za[...].astype(BF)
        self.each(u, lambda cp: cp.start(), True)

    def pieces(self, u):
        r, half = self.here.r, self.half
        begin, size = self.units[u]
        out = []
        for base, stride, width, place, _ in self.parts:
            if not begin <= place < begin + size:
                continue
            first = half - base
            if base + 3 * stride + width <= half:
                out.append((place, width, 0, base + r * stride))
            elif first <= 0:
                out.append((place, width, 1, base + r * stride - half))
            else:
                assert base + stride >= half
                cut = min(first, width)
                out.append((place, cut, jnp.where(r == 0, 0, 1), jnp.where(r == 0, base, base + r * stride - half)))
                if cut < width:
                    out.append((place + cut, width - cut, 1, base + r * stride + cut - half))
        return out

    def each(self, u, act, local):
        h = self.here
        for place, width, owner, at in self.pieces(u):
            dx = lax.rem(owner + h.x, 2)
            dst = self.out.at[:, pl.ds(pl.multiple_of(at, 128), width)]
            for dy in (1, 0):
                src = self.plane.at[lax.rem(h.y + dy, 2), :, pl.ds(place, width)]
                cp = remote(src, dst, self.ps.at[u], self.pr.at[u], h.at(dx=dx, dy=dy))
                if dy:
                    act(cp)
                    continue

                @pl.when(dx != 0)
                def _():
                    act(cp)

                if local:

                    @pl.when(dx == 0)
                    def _():
                        pltpu.make_async_copy(src, dst, self.pr.at[u]).start()

    def sent(self):
        h = self.here
        for u in range(len(self.units)):
            if not self.few:

                def along(dz, carry):
                    self.hop(u, dz, 0).wait_send()
                    return carry

                lax.fori_loop(1, h.O, along, 0)
                continue

            @pl.when(self.ends())
            def _():
                self.far(u).wait_send()

            self.hop(u, 2, 0).wait_send()

            @pl.when(h.z < 3)
            def _():
                self.hop(u, 1, 0).wait_send()

            @pl.when(h.z > 0)
            def _():
                self.hop(u, 3, 0).wait_send()

    def spans_at(self, u, x):
        half = self.half
        begin, size = self.units[u]
        out = []
        for base, stride, width, place, _ in self.parts:
            if begin <= place < begin + size:
                for chip in range(4):
                    lo = max(base + chip * stride, x * half)
                    hi = min(base + chip * stride + width, (x + 1) * half)
                    if lo < hi:
                        out.append((lo - x * half, hi - lo))
        joined = []
        for at, width in sorted(out):
            if joined and joined[-1][0] + joined[-1][1] == at:
                joined[-1] = (joined[-1][0], joined[-1][1] + width)
            else:
                joined.append((at, width))
        return joined

    def owned(self, u):
        for x in (0, 1):
            width = sum(w for _, w in self.spans_at(u, x))
            if width:

                @pl.when(self.here.x == x)
                def _():
                    all_of = self.out.at[:, pl.ds(0, width)]
                    pltpu.make_async_copy(all_of, all_of, self.pr.at[u]).wait()

    def finish(self):
        for u in range(len(self.units)):
            self.each(u, lambda cp: cp.wait_send(), False)


class Slots:
    def __init__(self, ref, room, sem):
        self.ref, self.room, self.sem = ref, room, sem

    def read(self, i, s):
        if self.room is None:
            return self.ref[i, 2 * s : 2 * s + 2]
        cp = pltpu.make_async_copy(self.ref.at[i, pl.ds(2 * s, 2)], self.room, self.sem)
        cp.start()
        cp.wait()
        return self.room[...]


ATTN_UNITS = ((768 + WIDE, QF), (768, QF), (768 + QF, QF), (512, 256), (0, 512))
CONV_UNITS = ((1024 + WIDE, QF), (1024, QF), (1024 + QF, QF), (768, 256), (0, 768))


class Renew:
    def __init__(self, here, g, w, m, v, out, f32_room, bf_room, new, ls, ss, rs):
        self.here, self.g, self.state, self.out = here, g, (w, m, v), out
        self.f32_room, self.bf_room, self.new = f32_room, bf_room, new
        self.ls, self.ss, self.rs = ls, ss, rs
        self.next = [0, 0]
        self.flying = ([], [])

    def loads(self, k, at, width):
        rows = self.g.shape[0]
        slot = k % 2
        cols = pl.ds(at, width)
        out = [
            pltpu.make_async_copy(
                a.at[:, cols], self.f32_room.at[pl.ds((3 * slot + i) * rows, rows), pl.ds(0, width)], self.ls.at[slot, i]
            )
            for i, a in enumerate(self.state)
        ]
        out.append(
            pltpu.make_async_copy(
                self.g.at[:, cols], self.bf_room.at[pl.ds(slot * rows, rows), pl.ds(0, width)], self.ls.at[slot, 3]
            )
        )
        return out

    def steps(self, x, spans):
        out = []
        for at, width in spans:
            parts = -(-width // WIDE)
            while width % (128 * parts):
                parts += 1
            for p in range(parts):
                n = self.next[x]
                self.next[x] += 1
                w, to = width // parts, at + p * (width // parts)
                place = self.new(n, w)
                dst = self.out.at[:, pl.ds(x * self.g.shape[1] + to, w)]
                out.append((
                    to, w, place, pltpu.make_async_copy(place, dst, self.ls.at[2 + n, 0]),
                    remote(place, dst, self.ss.at[n], self.rs.at[n], self.here.at(dx=1)),
                ))
        self.flying[x].extend(out)
        return out

    def run(self, x, spans):
        steps = self.steps(x, spans)
        if not steps:
            return

        @pl.when(self.here.x == x)
        def _():
            rows = self.g.shape[0]
            for cp in self.loads(0, *steps[0][:2]):
                cp.start()
            for k, (at, width, place, keep, give) in enumerate(steps):
                if k + 1 < len(steps):
                    for cp in self.loads(k + 1, *steps[k + 1][:2]):
                        cp.start()
                wait_all(self.loads(k, at, width))
                slot = k % 2
                w, m, v = (self.f32_room[(3 * slot + i) * rows : (3 * slot + i + 1) * rows, 0:width] for i in range(3))
                g = self.bf_room[slot * rows : (slot + 1) * rows, 0:width].astype(F32)
                place[...] = adam_update(w, m, v, g, STEP)[0].astype(BF)
                keep.start()
                give.start()

    def wait(self):
        for x in (0, 1):

            @pl.when(self.here.x == x)
            def _():
                for _, _, _, keep, give in self.flying[x]:
                    keep.wait()
                    give.wait_send()
                for _, _, _, _, give in self.flying[1 - x]:
                    give.wait_recv()


def backward_kernel(
    O, cot, tok, vec, hg, x1, x2, x3, h1, h2, h3, h4, bcx, cz, gu1, gu2, qkr, kv, oab, lse, wc, wa, Q, tail_c, tail_z,
    cosb, sinb, start, start_row, cots,
    w_attn, m_attn, v_attn, w_conv, m_conv, v_conv,
    dtok, vectors, gains, ga, gc, new_attn, new_conv, zb, dkc, dkz,
    W, gu, DG, HH, dgu, mx, sm, LT, other_lt, other_mx, other_sm, other_gu, own_a, *rest,
):
    few = O == 4
    own_c, rest = (rest[0], rest[1:]) if few else (own_a, rest)
    (zv, za, plane_a, plane_c, part, S, R, dO, delta, dq, dqab, dkv, dkk, heads, head_c, head_z, dprev, vg, v0, v1, v2,
     room, ags, agr, rss, rsr, hs, hr, kvs, kvr, wls, gls, hls, xs, xr, zs, zr, ld, ps, pr, vs, vr, rl, rls, rss2, rrs) = rest
    here = Place(O)
    x, y, z, c, r = here.x, here.y, here.z, here.c, here.r
    core_keys = Slots(dkc, None if few else room, rl)
    z_keys = Slots(dkz, None if few else room, rl)
    A = Reduce(here, ATTN_PARTS, ATTN_UNITS, (3 * D + 3 * FF) // 2, own_a, zb, 0, zv, za, plane_a, ga,
               zs.at[0], zr.at[0], ld, ps.at[0], pr.at[0])
    C = Reduce(here, CONV_PARTS, CONV_UNITS, (4 * D + 3 * FF) // 2, own_c, zb, AW, zv, za, plane_c, gc,
               zs.at[1], zr.at[1], ld, ps.at[1], pr.at[1])
    loads = [pltpu.make_async_copy(h, HH, hls.at[i]) for i, h in enumerate((h4, h3, h2, h1))]
    load_w = pltpu.make_async_copy(wa, W.at[:, :, :, pl.ds(0, AW)], wls.at[0])
    load_g = pltpu.make_async_copy(gu2, gu, gls.at[0])
    load_kv = pltpu.make_async_copy(kv, dkv, gls.at[2])
    load_d = pltpu.make_async_copy(cots, DG.at[0], gls.at[3])
    for cp in (load_d, load_w, load_g, loads[0], load_kv):
        cp.start()
    greet(here)
    vg[...] = jnp.zeros_like(vg)

    done = []

    def move(kind, red, u):
        if kind == "n":
            red.owned(u)
            for x_ in (0, 1):
                renew_c.run(x_, red.spans_at(u, x_))
        else:
            {"s": red.send, "r": red.relay, "t": red.total}[kind](u)

    def at(point):
        for step in REDUCTIONS[point]:
            move(step[0], A if step[1] == "a" else C, int(step[2]))

    def flat(H):
        return H[...].reshape(4 * T, D)

    def swap(i, src, dst):
        cp = remote(src, dst, xs.at[i], xr.at[i], here.at(dc=1))
        cp.start()
        return cp

    def turned(e, H):
        if done:
            done.pop().wait_send()
        LT[...] = jnp.transpose(flat(H)).reshape(LT.shape)
        cp = swap(e, LT.at[:, 1 - c], other_lt.at[e % 4])
        done.append(cp)
        return cp

    def turned_saved(i, e):
        loads[i].wait()
        cp = turned(e, HH)
        if i < 3:
            loads[i + 1].start()
        return cp

    def ffn_back(i, e, DF, base, x_in, gain_row, red, dy, name):
        lt = turned(e, DF)
        for n in range(3):
            ffn_back_tile(DF, W, base, gu, dgu, mx, n)
        mixed = swap(8 + e, mx, other_mx)
        grads = swap(9 + e, dgu, other_gu)
        sums = Sums(here, part, S, R, rss.at[i], rsr.at[i])
        sums.begin(lambda n: nt(dgu[...], rows_of(W, n, base, WIDE)))
        lt.wait_recv()
        mixed.wait()
        at(name + " down")
        if i and not few:
            A.sent()
        red.make(0, LT, other_lt.at[e % 4], mx, other_mx, 0)
        red.send(0)
        sums.relay()
        dx, dgain = rms_back(x_in[...], vec[gain_row : gain_row + 1, :], sums.wait())
        vg[gain_row : gain_row + 1, :] = dgain
        dprev[...] = dy + dx
        H2 = DG.at[(i + 1) % 2]
        H2[r] = dprev[...].astype(BF)
        blocks = Gather(here, H2, ags.at[i + 1], agr.at[i + 1])
        lt = turned_saved(i, e + 1)
        blocks.relay()
        lt.wait_recv()
        grads.wait()
        red.make(1, LT, other_lt.at[(e + 1) % 4], dgu, other_gu, 0)
        at(name + " wide")
        red.make(2, LT, other_lt.at[(e + 1) % 4], dgu, other_gu, QF)
        blocks.wait()
        at(name + " end")

    DF = DG.at[0]
    load_d.wait()
    load_w.wait()
    load_g.wait()
    ffn_back(0, 0, DF, 3 * QD, x3, 3, A, cot[...].astype(F32), "ffn2")
    load_g = pltpu.make_async_copy(gu1, gu, gls.at[1])
    load_g.start()

    DA = DG.at[1]
    d_out = nn(flat(DA), cols(W, 2 * QD, QD)).astype(BF).astype(F32)
    left, right = to_pairs(oab[0], oab[1])
    sm[:, 0:QD] = jnp.concatenate([left, right], axis=1).astype(BF)
    attended = swap(10, sm.at[:, 0:QD], other_sm.at[:, 0:QD])
    lt = turned(2, DA)
    da, db = to_pairs(d_out[:, 0:128], d_out[:, 128:256])
    for s in (0, 1):
        rows = slice(s * 256, (s + 1) * 256)
        four = stacked(da[rows], db[rows])
        o_of = (oab[0, rows, :], oab[1, rows, :])
        for g in range(4):
            dO[s, g] = four[g].astype(BF)
            dl = jnp.sum(four[g] * o_of[g % 2], axis=-1, keepdims=True)
            delta[s, :, g * 256 : (g + 1) * 256] = jnp.transpose(jnp.broadcast_to(dl, (256, 128)))[0:8, :]
    load_kv.wait()
    low = lane_low((256, 128))

    def pair_keys(s):
        two = pl.ds(2 * s, 2)
        return remote(dkv.at[:, two, 1 - c], dkc.at[:, two], kvs.at[s, 0], kvr.at[s, 0], here.at(dc=1))

    def down(s, d, owner):
        two = pl.ds(2 * s, 2)
        return remote(dkv.at[owner, two, c], dkz.at[z, two], kvs.at[s, d], kvr.at[s, d], here.at(dz=O - d))

    def send_keys(s):
        two = pl.ds(2 * s, 2)
        pair_keys(s).wait()

        def send_down(zz, carry):
            dkv[zz, two, c] = (dkv[zz, two, c].astype(F32) + core_keys.read(zz, s).astype(F32)).astype(BF)
            down(s, z - zz, zz).start()
            return carry

        lax.fori_loop(0, z, send_down, 0)
        dkk[s * 256 : (s + 1) * 256, :] = (
            dkv[z, two, c].astype(F32) + core_keys.read(z, s).astype(F32)
        ).reshape(256, 256)

    for s in (0, 1):
        at("attention %d" % s)
        dq[...] = jnp.zeros_like(dq)
        first_of = start_row[0:1, s * 256 : (s + 1) * 256]
        col = lax.broadcasted_iota(jnp.int32, (1, 256), 1)
        t = z * 512 + lax.div(col, T) * 256 + c * T + lax.rem(col, T)

        def chunk(j, carry):
            block = dkv[lax.div(j, 2), 2 * s + lax.rem(j, 2)].reshape(256, 256)
            k, v = block[:, 0:128], block[:, 128:256]
            key = j * 256 + lax.broadcasted_iota(jnp.int32, (256, 256), 0)
            allowed = (key >= first_of) & (key <= t)
            dk = jnp.zeros((256, 128), F32)
            dv = jnp.zeros((256, 128), F32)
            for g in range(4):
                span = slice(g * 256, (g + 1) * 256)
                p = jnp.where(allowed, jnp.exp(nt(k, Q[s, g]) - lse[s, 0:1, span]), 0.0)
                ds = (p * (nt(v, dO[s, g]) - delta[s, 0:1, span])).astype(BF)
                dv = dv + nn(p.astype(BF), dO[s, g])
                dk = dk + nn(ds, Q[s, g])
                dq[g] += tn(ds, k)
            dkv[lax.div(j, 2), 2 * s + lax.rem(j, 2)] = (
                jnp.concatenate([dk, dv], axis=1).astype(BF).reshape(2, T, 256)
            )
            return carry

        if s:
            lax.fori_loop(0, z + 1, chunk, 0)
            send_keys(0)
            lax.fori_loop(z + 1, 2 * z + 2, chunk, 0)
        else:
            lax.fori_loop(0, 2 * z + 2, chunk, 0)
        pair_keys(s).start()
        rows = slice(s * 256, (s + 1) * 256)
        dqab[0, rows, :] = jnp.where(low, dq[0], dq[2]) * (HEAD_DIM ** -0.5)
        dqab[1, rows, :] = jnp.where(low, dq[1], dq[3]) * (HEAD_DIM ** -0.5)
    lt.wait_recv()
    attended.wait()
    A.make(3, LT, other_lt.at[2], sm, other_sm, 0)
    send_keys(1)
    at("keys sent")

    def take(d, carry):
        @pl.when(z + d < O)
        def _():
            for s in (0, 1):
                down(s, d, z).wait_recv()
                dkk[s * 256 : (s + 1) * 256, :] += z_keys.read(z + d, s).astype(F32).reshape(256, 256)

        return carry

    lax.fori_loop(1, O, take, 0)
    at("keys")

    for i in range(3):
        up = dqab[i] if i < 2 else dkk[:, 0:128]
        raw = qkr[i]
        gain = hg[0:1, :] if i < 2 else hg[1:2, :]
        dw = up * cosb[...] + turn(up * sinb[...])
        rr = lax.rsqrt(head_mean(raw * raw) + norm_eps)
        dgain = jnp.sum(dw * raw * rr, axis=0, keepdims=True)
        row = 8 if i < 2 else 9
        vg[row : row + 1, 0:128] += dgain
        draw = rr * gain * dw - raw * (rr * rr * rr) * head_mean(raw * gain * dw)
        if i < 2:
            dqab[i] = draw
        else:
            sm[:, 512:640] = draw.astype(BF)
    left, right = to_pairs(dqab[0], dqab[1])
    sm[:, 256:384] = left.astype(BF)
    sm[:, 384:512] = right.astype(BF)
    sm[:, 640:768] = dkk[:, 128:256].astype(BF)
    grads = swap(11, sm.at[:, 256:768], other_sm.at[:, 256:768])
    sums = Sums(here, part, S, R, rss.at[1], rsr.at[1])
    sums.begin(lambda n: nt(sm[:, 256:768], rows_of(W, n, 0, 512)))
    load_w = pltpu.make_async_copy(wc, W, wls.at[1])
    load_w.start()
    lt = turned_saved(1, 3)
    sums.relay()
    lt.wait_recv()
    grads.wait()
    A.make(4, LT, other_lt.at[3], sm, other_sm, 256)
    at("qkv")
    dx, dgain = rms_back(x2[...], vec[2:3, :], sums.wait())
    vg[2:3, :] = dgain
    dprev[...] += dx
    D2 = DG.at[0]
    D2[r] = dprev[...].astype(BF)
    blocks = Gather(here, D2, ags.at[2], agr.at[2])
    blocks.relay()
    at("d2 relayed")
    load_w.wait()
    load_g.wait()
    blocks.wait()
    ffn_back(2, 4, D2, 4 * QD, x1, 1, C, dprev[...], "ffn1")

    DD = DG.at[1]
    tap0, tap1, tap2 = taps(here, vec)
    from_c, from_z = tail_c[...], jnp.where(z > 0, tail_z[...], 0.0)
    dyc = nn(flat(DD), cols(W, 3 * QD, QD))
    sm[:, 0:QD] = (bcx[1] * cz[...]).astype(BF)
    mixed = swap(14, sm.at[:, 0:QD], other_sm.at[:, 0:QD])
    sm[:, 2 * QD : 3 * QD] = (dyc * cz[...]).astype(BF)
    dzs = dyc * bcx[1]
    bx = bcx[0] * bcx[2]
    row = lax.broadcasted_iota(jnp.int32, (T, QD), 0)
    g0, g1, g2 = (jnp.zeros((1, QD), F32) for _ in range(3))
    for b in range(4):
        mine = bx[b * T : (b + 1) * T, :]
        dzb = dzs[b * T : (b + 1) * T, :]
        one, two, m1, m2 = behind(here, b, mine, from_c, from_z, start)
        g0 = g0 + jnp.sum(dzb * mine, axis=0, keepdims=True)
        g1 = g1 + jnp.sum(dzb * one * m1, axis=0, keepdims=True)
        g2 = g2 + jnp.sum(dzb * two * m2, axis=0, keepdims=True)
        b1 = tap1 * dzb * m1
        b2 = tap2 * dzb * m2
        heads[2 * b : 2 * b + 1, :] = b2[0:1]
        heads[2 * b + 1 : 2 * b + 2, :] = b1[0:1] + b2[1:2]
        dkk[b * T : (b + 1) * T, :] = (
            tap0 * dzb
            + jnp.where(row < T - 1, pltpu.roll(b1, T - 1, 0), 0.0)
            + jnp.where(row < T - 2, pltpu.roll(b2, T - 2, 0), 0.0)
        )
    over = remote(heads, head_c, hs.at[0], hr.at[0], here.at(dc=1))
    over.start()
    back = remote(heads, head_z, hs.at[1], hr.at[1], here.at(dz=O - 1, dc=1))

    @pl.when((c == 0) & (z > 0))
    def _():
        back.start()

    at("halo")
    rows = ga.shape[0]
    renew_a = Renew(here, ga, w_attn, m_attn, v_attn, new_attn, gu, dgu,
                    lambda n, w: other_gu.at[pl.ds(n * rows, rows), pl.ds(0, w)], rls.at[0], rss2.at[0], rrs.at[0])
    renew_c = Renew(here, gc, w_conv, m_conv, v_conv, new_conv, gu, dgu,
                    lambda n, w: W.at[n // 2, n % 2, :, pl.ds(0, w)], rls.at[1], rss2.at[1], rrs.at[1])
    for u in range(5):
        A.owned(u)
    for x_ in (0, 1):
        renew_a.run(x_, [(0, 2 * AW)])
    lt = turned(6, DD)
    tap_at = pl.ds(pl.multiple_of(r * QD, 128), QD)
    vg[4:5, tap_at] = g0
    vg[5:6, tap_at] = g1
    vg[6:7, tap_at] = g2
    over.wait()

    @pl.when((c == 1) & (z < O - 1))
    def _():
        back.wait_recv()

    to_c, to_z = head_c[...], jnp.where(z < O - 1, head_z[...], 0.0)
    for b in range(4):
        rows = slice(b * T, (b + 1) * T)
        if b % 2:
            e = jnp.where(c == 0, to_c[2 * b : 2 * b + 2], to_z[2 * b - 2 : 2 * b])
        else:
            e = jnp.where(c == 0, to_c[2 * b : 2 * b + 2], to_c[2 * b + 2 : 2 * b + 4])
        dbx = dkk[rows, :] + jnp.where(row == T - 2, e[0:1], jnp.where(row == T - 1, e[1:2], 0.0))
        sm[rows, QD : 2 * QD] = (dbx * bcx[2, rows, :]).astype(BF)
        sm[rows, 3 * QD : 4 * QD] = (dbx * bcx[0, rows, :]).astype(BF)
    grads = swap(15, sm.at[:, QD : 4 * QD], other_sm.at[:, QD : 4 * QD])
    sums = Sums(here, part, S, R, rss.at[3], rsr.at[3])
    sums.begin(lambda n: nt(sm[:, QD : 4 * QD], rows_of(W, n, 0, 768)))
    lt.wait_recv()
    mixed.wait()
    C.make(3, LT, other_lt.at[2], sm, other_sm, 0)
    lt = turned_saved(3, 7)
    lt.wait_recv()
    grads.wait()
    C.make(4, LT, other_lt.at[3], sm, other_sm, QD)
    at("made")
    sums.relay()
    at("sums relayed")
    dx, dgain = rms_back(tok[...].astype(F32), vec[0:1, :], sums.wait())
    vg[0:1, :] = dgain
    dtok[...] = dprev[...] + dx

    v0[c] = vg[...]
    cp = remote(v0.at[c], v0.at[c], vs.at[0], vr.at[0], here.at(dc=1))
    cp.start()
    at("end")
    cp.wait()
    v1[r] = v0[0] + v0[1]
    copies = [
        remote(v1.at[r], v1.at[r], vs.at[1 + k], vr.at[1 + k], here.at(dx=dx, dy=dy)) for k, (dx, dy) in enumerate(PLANE)
    ]
    for cp in copies:
        cp.start()
    at("end 1")
    wait_all(copies)
    v2[z] = v1[0] + v1[1] + v1[2] + v1[3]

    def start_z(dz, carry):
        remote(v2.at[z], v2.at[z], vs.at[3 + dz], vr.at[3 + dz], here.at(dz=dz)).start()
        return carry

    lax.fori_loop(1, O, start_z, 0)
    at("end 2")

    def wait_z(dz, carry):
        remote(v2.at[z], v2.at[z], vs.at[3 + dz], vr.at[3 + dz], here.at(dz=dz)).wait()
        return carry

    lax.fori_loop(1, O, wait_z, 0)
    t = v2[0]
    for i in range(1, O):
        t = t + v2[i]
    vectors[...] = t[0:7, :]
    gains[...] = t[8:10, 0:64] + pltpu.roll(t[8:10, 0:128], 64, 1)[:, 0:64]
    at("end 3")

    def keys_sent(zz, carry):
        for s in (0, 1):
            down(s, z - zz, zz).wait_send()
        return carry

    lax.fori_loop(0, z, keys_sent, 0)
    @pl.when((c == 0) & (z > 0))
    def _():
        back.wait_send()

    for cp in done:
        cp.wait_send()
    if few:
        A.sent()
    C.sent()
    A.finish()
    C.finish()
    renew_a.wait()
    renew_c.wait()


def backward(O, cot, tok, vec, hg, saved, state):
    (x1, x2, x3, h1, h2, h3, h4, bcx, cz, gu1, gu2, qkr, kv, oab, lse, wc, wa, Q, tail_c, tail_z, cosb, sinb, start,
     start_row, cots) = saved
    sds = jax.ShapeDtypeStruct
    G = 4 * T
    rows = D // (4 * O)
    few = O == 4
    dma = pltpu.SemaphoreType.DMA
    V = pltpu.VMEM
    keys = sds((O, 4, T, 256), BF)
    outs = (
        sds((T, D), F32), sds((7, D), F32), sds((2, HEAD_DIM), F32), sds((rows, 2 * AW), BF), sds((rows, 2 * CW), BF),
        sds((rows, 4 * AW), BF), sds((rows, 4 * CW), BF), sds((O, 2, rows, AW + CW), BF), keys, keys,
    )
    args = (cot, tok, vec, hg, *saved, *state)
    hbm = {id(a) for a in (*state, gu1, gu2, wc, wa, kv, h1, h2, h3, h4, cots)}
    keys_at = vmem() if few else any_spec()
    return pl.pallas_call(
        functools.partial(backward_kernel, O),
        out_shape=outs,
        in_specs=[any_spec() if id(a) in hbm else vmem() for a in args],
        out_specs=(vmem(), vmem(), vmem(), *[any_spec()] * 5, keys_at, keys_at),
        scratch_shapes=[
            V((2 * O, 2, rows, CW), BF), V((G, WIDE), F32), V((2, 4, T, D), BF), V((4, T, D), BF),
            V((G, WIDE), BF), V((G, QF), BF), V((G, D), BF), V((2 * O, 2, rows, G), BF),
            V((4, 2 * O, rows, G), BF), V((G, QF), BF), V((G, D), BF), V((G, WIDE), BF),
            V((2 * O, rows, CW), BF), *([V((2 * O, rows, CW), BF)] if few else []),
            V((O, 2, rows, QF), BF), V((2, rows, QF), F32), V((2, rows, AW), BF), V((2, rows, CW), BF),
            V((2, 4, T, D // 2), F32), V((2, 6, T // 2, D // 2), BF), V((2, 6, T // 2, D // 2), BF),
            V((2, 4, 256, 128), BF), V((2, 8, 2 * G), F32), V((4, 256, 128), F32), V((2, G, 128), F32),
            V((O, 4, 2, T, 256), BF), V((G, 256), F32),
            V((8, QD), F32), V((8, QD), F32), V((8, QD), F32), V((T, D), F32), V((16, D), F32),
            V((2, 16, D), F32), V((4, 16, D), F32), V((O, 16, D), F32), V((2, T, 256), BF),
            dma((4, 6)), dma((4, 6)), dma((4, 2, 6)), dma((4, 2, 6)), dma((2,)), dma((2,)),
            dma((2, O)), dma((2, O)), dma((2,)), dma((4,)), dma((4,)), dma((16,)), dma((16,)),
            dma((2, 5, O)), dma((2, 5, O)), dma((O,)), dma((2, 5)), dma((2, 5)), dma((O + 3,)), dma((O + 3,)), dma,
            dma((2, 20, 4)), dma((2, 20)), dma((2, 20)),
        ],
        compiler_params=pltpu.CompilerParams(
            collective_id=2, has_side_effects=True, vmem_limit_bytes=int(63.5 * 2**20)
        ),
        cost_estimate=pl.CostEstimate(flops=2 * 10**10, bytes_accessed=10**8, transcendentals=10**7),
        name="backward",
    )(*args)[:7]


REDUCTIONS = {
    "ffn2 down": (),
    "ffn2 wide": ("sa1",),
    "ffn2 end": (),
    "attention 0": (),
    "attention 1": ("ra0",),
    "keys sent": ("ta0", "ra1"),
    "keys": (),
    "qkv": ("sa2", "sa3", "sa4", "ta1"),
    "d2 relayed": ("ra2", "ra3", "ra4"),
    "ffn1 down": ("ta2", "ta3", "ta4"),
    "ffn1 wide": (),
    "ffn1 end": ("rc0",),
    "halo": ("sc1",),
    "made": ("sc2", "tc0"),
    "sums relayed": ("rc1", "nc0"),
    "end": ("tc1", "sc3", "sc4"),
    "end 1": ("rc2", "nc1"),
    "end 2": ("tc2", "rc3", "rc4", "nc2", "tc3", "tc4"),
    "end 3": ("nc3", "nc4"),
}


def adam_update(master, first_moment, second, gradient, step_value):
    first_new = beta_one * first_moment + (1.0 - beta_one) * gradient
    second_new = beta_two * second + (1.0 - beta_two) * gradient * gradient
    first_hat = first_new / (1.0 - beta_one**step_value)
    second_hat = second_new / (1.0 - beta_two**step_value)
    master_new = master - learn_rate * (
        first_hat / (jnp.sqrt(second_hat) + adam_eps) + decay_rate * master
    )
    return (master_new, first_new, second_new)


def shards(
    tokens, segments, cotangent, conv_weights, attn_weights, vectors, head_gains,
    master_conv, first_conv, second_conv, master_attn, first_attn, second_attn,
):
    O = lax.axis_size("z")
    tok = tokens[0]
    out_tok, hg, *saved = forward(O, tok, cotangent[0], vectors, head_gains, segments, rotary_rows(), conv_weights, attn_weights)
    state = (master_attn, first_attn, second_attn, master_conv, first_conv, second_conv)
    dtok, grad_vectors, grad_gains, ga, gc, attn_all, conv_all = backward(O, cotangent[0], tok, vectors, hg, saved, state)
    grad_attn, grad_conv = ga.astype(F32), gc.astype(F32)
    step_value = jnp.float32(STEP)
    new_conv = adam_update(master_conv, first_conv, second_conv, grad_conv, step_value)
    new_attn = adam_update(master_attn, first_attn, second_attn, grad_attn, step_value)
    return (
        out_tok[None], dtok[None], grad_conv, grad_attn, grad_vectors, grad_gains, *new_conv, *new_attn,
        conv_all, attn_all,
    )


def solution(mesh):
    outer = mesh.shape["ctx"] // 4
    split = Mesh(mesh.devices.reshape(mesh.shape["dp"], outer, 2, 2), ("dp", "z", "y", "c"))
    ctx = ("z", "y", "c")
    seq, rows, state = P("dp", ctx, None), P(ctx, None), P(ctx, "dp")
    return jax.shard_map(
        shards,
        mesh=split,
        in_specs=(seq, P("dp", ctx), seq, rows, rows, P(), P(), *([state] * 6)),
        out_specs=(seq, seq, state, state, P(), P(), *([state] * 6), rows, rows),
        check_vma=False,
    )
```
